32 devices in a mesh: ta: 4 (over y, core), ha: 8 (over z, x).
Axes of the slice: x: 2, y: 2, z: 4, core: 2. Of those that a mesh axis runs over, the one named last changes fastest.
Arguments:
- query_states: bfloat16 [8, 16, 56, 768], P('ta', 'ha'), may hold values from -51 to 51
- key_states: bfloat16 [8, 16, 56, 768], P('ta', 'ha'), may hold values from -6 to 6
- value_states: bfloat16 [8, 16, 56, 768], P('ta', 'ha'), may hold values from -6 to 6
- conv_weight: bfloat16 [27, 768], replicated, may hold values from -1.1953125 to 1.1953125
- out_grad: bfloat16 [8, 16, 56, 768], P('ta', 'ha'), may hold values from -6 to 6
- tile_mask: int32 [4, 8, 9], replicated, may hold values from 0 to 1, as said below
- clip_lengths: int32 [8], replicated, may hold values from 2 to 56
Outputs:
- layer_out: bfloat16 [8, 16, 56, 768], P('ta', 'ha')
- query_grad: bfloat16 [8, 16, 56, 768], P('ta', 'ha')
- key_grad: bfloat16 [8, 16, 56, 768], P('ta', 'ha')
- value_grad: bfloat16 [8, 16, 56, 768], P('ta', 'ha')
The draws below stay inside these ranges and needn't reach their ends.
Inputs may be any that keep to these rules, and one draw needn't show every extreme that they name: `tile_mask`: entries are 0 or 1; entry 4, a tile's own keys, is always 1.
All inputs are finite; a program needn't handle non-finite values.
Results may differ from the reference program's by a relative error of at most 0.0095.
Values may be sent and summed in bfloat16 or wider, within the bound.
No kernel may reach another device: no remote copies, remote signals or barrier semaphores. Data moves between devices by JAX's collectives and lax.ppermute only.
A program may use at most 128 MiB of HBM per device.

```python
import jax
import jax.numpy as jnp
from jax import lax

HEAD_COUNT = 6
HEAD_DIM = 128
CHANNELS = 768
TILE_SIDE = 2
WIDTH_CELLS = 56
TIME_TILES = 4
HEIGHT_TILES = 8
FRAMES = 8
LATENT_ROWS = 16
N_TA = 4
N_HA = 8


def shared_states(key):
    shape = (FRAMES, LATENT_ROWS, WIDTH_CELLS, CHANNELS)
    key_query = jax.random.fold_in(key, 11)
    key_keys = jax.random.fold_in(key, 12)
    query_f = jnp.clip(jax.random.normal(key_query, shape, jnp.float32), -6.0, 6.0)
    keys_f = jnp.clip(jax.random.normal(key_keys, shape, jnp.float32), -6.0, 6.0)
    return (query_f, keys_f)


def draw_query_states(key, part):
    return shared_states(key)[0].astype(jnp.bfloat16)


def draw_key_states(key, part):
    return shared_states(key)[1].astype(jnp.bfloat16)


def draw_tile_mask(key, part):
    level = jax.random.randint(jax.random.fold_in(key, 21), (TIME_TILES, HEIGHT_TILES, 1), 0, 3)
    picked = jax.random.randint(jax.random.fold_in(key, 22), (TIME_TILES, HEIGHT_TILES, 9), 0, 9)
    kept_tiles = (picked < 2 + 3 * level).astype(jnp.int32)
    centre = jnp.arange(9) == 4
    return jnp.where(centre[None, None, :], 1, kept_tiles).astype(jnp.int32)


def draw_clip_lengths(key, part):
    lengths = jax.random.randint(jax.random.fold_in(key, 31), (FRAMES,), 2, WIDTH_CELLS + 1)
    order = jax.random.permutation(jax.random.fold_in(key, 32), FRAMES)
    lengths = lengths.at[order[0]].set(WIDTH_CELLS)
    lengths = lengths.at[order[1]].set(2)
    return lengths.astype(jnp.int32)


def steps_of(own_key, extent, shards, smallest, high):
    def one(position, parts):
        steps = jax.random.uniform(jax.random.fold_in(jax.random.fold_in(own_key, 6), position), (parts,), jnp.float32, smallest / len(shards), high / len(shards))
        return jnp.repeat(jnp.exp(steps), extent[position] // parts).reshape((-1,) + (1,) * (len(extent) - position - 1))

    factor_of = one(*shards[0])
    for cut in shards[1:]:
        factor_of = factor_of * one(*cut)
    return factor_of


def centred(key, extent, deviation, limit, shards=(), kind=jnp.bfloat16):
    values = deviation * jax.random.normal(key, extent, jnp.float32)
    if shards:
        values = values * steps_of(key, extent, shards, -0.22, 0.18)
    return jnp.clip(values, -limit, limit).astype(kind)


def setup_inputs(seed: int = 0) -> dict:
    seeds = jax.random.split(jax.random.key(seed), 8)
    query_states = draw_query_states(jax.random.fold_in(seeds[7], 71), 0)
    key_states = draw_key_states(jax.random.fold_in(seeds[7], 71), 0)
    value_states = centred(seeds[2], (FRAMES, LATENT_ROWS, WIDTH_CELLS, CHANNELS), 1.0, 6.0, ((0, 4), (1, 8)))
    conv_weight = centred(seeds[3], (27, CHANNELS), 0.2, 1.1953125)
    out_grad = centred(seeds[4], (FRAMES, LATENT_ROWS, WIDTH_CELLS, CHANNELS), 1.0, 6.0, ((0, 4), (1, 8)))
    tile_mask = draw_tile_mask(jax.random.fold_in(seeds[7], 71), 0)
    clip_lengths = draw_clip_lengths(jax.random.fold_in(seeds[7], 71), 0)
    return dict(query_states=query_states, key_states=key_states, value_states=value_states, conv_weight=conv_weight, out_grad=out_grad, tile_mask=tile_mask, clip_lengths=clip_lengths)


def starts(*values):
    return tuple(jnp.asarray(value).astype(jnp.int32) for value in values)


def depthwise(source, weight, size_t, size_h, width_len):
    result = jnp.zeros((size_t, size_h, width_len, source.shape[3]), jnp.float32)
    for offset_id in range(27):
        step_t, step_h, step_w = offset_id // 9, (offset_id // 3) % 3, offset_id % 3
        piece = source[step_t:step_t + size_t, step_h:step_h + size_h, step_w:step_w + width_len].astype(jnp.float32)
        result = result + weight[offset_id].astype(jnp.float32) * piece
    return result


def source_conv(grad_window, weight, tile_side, width_len):
    slab = grad_window[tile_side - 1:2 * tile_side + 1, tile_side - 1:2 * tile_side + 1].astype(jnp.float32)
    slab = jnp.pad(slab, ((0, 0), (0, 0), (1, 1), (0, 0)))
    result = jnp.zeros((3, 3, tile_side, tile_side, width_len, slab.shape[3]), jnp.float32)
    three = jnp.arange(3)
    for offset_id in range(27):
        step_t, step_h, step_w = offset_id // 9, (offset_id // 3) % 3, offset_id % 3
        piece = slab[step_t:step_t + tile_side, step_h:step_h + tile_side, step_w:step_w + width_len]
        piece = weight[26 - offset_id].astype(jnp.float32) * piece
        tiles_t = (tile_side - 1 + step_t + jnp.arange(tile_side)) // tile_side
        tiles_h = (tile_side - 1 + step_h + jnp.arange(tile_side)) // tile_side
        pick_t = (tiles_t[None, :] == three[:, None]).astype(jnp.float32)
        pick_h = (tiles_h[None, :] == three[:, None]).astype(jnp.float32)
        result = result + pick_t[:, None, :, None, None, None] * pick_h[None, :, None, :, None, None] * piece[None, None]
    return result


def combine_tiles(terms):
    three = jnp.arange(3)
    centre = (three[:, None] == 1) & (three[None, :] == 1)
    rounded = lax.optimization_barrier(terms.astype(jnp.bfloat16)).astype(jnp.float32)
    return jnp.sum(jnp.where(centre[:, :, None, None, None, None], terms, rounded), axis=(0, 1))


def to_grid(stacked):
    last_dim = stacked.shape[-1]
    shaped = stacked.reshape(N_TA, N_HA, TILE_SIDE, TILE_SIDE, WIDTH_CELLS, last_dim)
    return shaped.transpose(0, 2, 1, 3, 4, 5).reshape(TILE_SIDE * N_TA, TILE_SIDE * N_HA, WIDTH_CELLS, last_dim)


def reference(query_states, key_states, value_states, conv_weight, out_grad, tile_mask, clip_lengths):
    score_scale = HEAD_DIM ** -0.5
    window_len = 3 * TILE_SIDE
    channels = HEAD_COUNT * HEAD_DIM
    queries = TILE_SIDE * TILE_SIDE * WIDTH_CELLS
    pad_grid = ((TILE_SIDE, TILE_SIDE), (TILE_SIDE, TILE_SIDE), (0, 0), (0, 0))
    query_pad = jnp.pad(query_states, pad_grid)
    key_pad = jnp.pad(key_states, pad_grid)
    value_pad = jnp.pad(value_states, pad_grid)
    grad_pad = jnp.pad(out_grad, pad_grid)
    lens_pad = jnp.pad(clip_lengths, (TILE_SIDE, TILE_SIDE))
    mask_pad = jnp.pad(tile_mask, ((1, 1), (1, 1), (0, 0)))
    tile_offset = jnp.arange(window_len) // TILE_SIDE
    columns = jnp.arange(WIDTH_CELLS)

    def query_pass(tile_id):
        tile_t = tile_id // N_HA
        tile_h = tile_id % N_HA
        own_start = starts(tile_t * TILE_SIDE + TILE_SIDE, tile_h * TILE_SIDE + TILE_SIDE, 0, 0)
        win_start = starts(tile_t * TILE_SIDE, tile_h * TILE_SIDE, 0, 0)
        own_size = (TILE_SIDE, TILE_SIDE, WIDTH_CELLS, channels)
        win_size = (window_len, window_len, WIDTH_CELLS, channels)
        query_f = lax.dynamic_slice(query_pad, own_start, own_size).reshape(queries, HEAD_COUNT, HEAD_DIM).astype(jnp.float32)
        grad_f = lax.dynamic_slice(grad_pad, own_start, own_size).reshape(queries, HEAD_COUNT, HEAD_DIM).astype(jnp.float32)
        key_f = lax.dynamic_slice(key_pad, win_start, win_size).reshape(-1, HEAD_COUNT, HEAD_DIM).astype(jnp.float32)
        value_f = lax.dynamic_slice(value_pad, win_start, win_size).reshape(-1, HEAD_COUNT, HEAD_DIM).astype(jnp.float32)
        frame_lens = lax.dynamic_slice(lens_pad, starts(tile_t * TILE_SIDE), (window_len,))
        entries = mask_pad[tile_t + 1, tile_h + 1].reshape(3, 3)
        kept_tiles = entries[tile_offset][:, tile_offset] == 1
        height_ids = tile_h + tile_offset - 1
        in_height = (height_ids >= 0) & (height_ids < N_HA)
        key_valid = kept_tiles[:, :, None] & in_height[None, :, None] & (columns[None, None, :] < frame_lens[:, None, None])
        key_valid = key_valid.reshape(-1)
        scores = jnp.einsum("qhd,khd->hqk", query_f, key_f) * score_scale
        scores = jnp.where(key_valid[None, None, :], scores, -jnp.inf)
        row_max = jnp.max(scores, axis=-1, keepdims=True)
        exponent = jnp.exp(scores - row_max)
        row_total = jnp.sum(exponent, axis=-1, keepdims=True)
        softmax_p = exponent / row_total
        probs_bf = softmax_p.astype(jnp.bfloat16)
        attention = jnp.einsum("hqk,khd->qhd", probs_bf.astype(jnp.float32), value_f)
        row_delta = jnp.sum(grad_f * attention, axis=-1)
        dprobs = jnp.einsum("qhd,khd->hqk", grad_f, value_f)
        dscores = (softmax_p * (dprobs - row_delta.T[:, :, None])).astype(jnp.bfloat16)
        query_part = jnp.einsum("hqk,khd->qhd", dscores.astype(jnp.float32), key_f) * score_scale
        log_total = (row_max[..., 0] + jnp.log(row_total[..., 0])).T
        tile_shape = (TILE_SIDE, TILE_SIDE, WIDTH_CELLS)
        return (attention.reshape(tile_shape + (channels,)), query_part.astype(jnp.bfloat16).reshape(tile_shape + (channels,)),
                log_total.reshape(tile_shape + (HEAD_COUNT,)), row_delta.reshape(tile_shape + (HEAD_COUNT,)))

    tile_ids = jnp.arange(N_TA * N_HA, dtype=jnp.int32)
    attention_t, query_t, total_t, delta_t = lax.map(query_pass, tile_ids)
    attention_grid = to_grid(attention_t)
    query_grad = to_grid(query_t)
    total_pad = jnp.pad(to_grid(total_t), pad_grid)
    delta_pad = jnp.pad(to_grid(delta_t), pad_grid)

    def key_pass(tile_id):
        tile_t = tile_id // N_HA
        tile_h = tile_id % N_HA
        own_start = starts(tile_t * TILE_SIDE + TILE_SIDE, tile_h * TILE_SIDE + TILE_SIDE, 0, 0)
        win_start = starts(tile_t * TILE_SIDE, tile_h * TILE_SIDE, 0, 0)
        own_size = (TILE_SIDE, TILE_SIDE, WIDTH_CELLS, channels)
        win_size = (window_len, window_len, WIDTH_CELLS, channels)
        stat_size = (window_len, window_len, WIDTH_CELLS, HEAD_COUNT)
        key_f = lax.dynamic_slice(key_pad, own_start, own_size).reshape(queries, HEAD_COUNT, HEAD_DIM).astype(jnp.float32)
        value_f = lax.dynamic_slice(value_pad, own_start, own_size).reshape(queries, HEAD_COUNT, HEAD_DIM).astype(jnp.float32)
        near_query = lax.dynamic_slice(query_pad, win_start, win_size).reshape(-1, HEAD_COUNT, HEAD_DIM).astype(jnp.float32)
        grad_window = lax.dynamic_slice(grad_pad, win_start, win_size)
        near_grad = grad_window.reshape(-1, HEAD_COUNT, HEAD_DIM).astype(jnp.float32)
        near_total = lax.dynamic_slice(total_pad, win_start, stat_size).reshape(-1, HEAD_COUNT).T
        near_delta = lax.dynamic_slice(delta_pad, win_start, stat_size).reshape(-1, HEAD_COUNT).T
        nearby = lax.dynamic_slice(mask_pad, starts(tile_t, tile_h, 0), (3, 3, 9)).reshape(9, 9)
        facing = nearby[jnp.arange(9), 8 - jnp.arange(9)].reshape(3, 3)
        query_ok = jnp.broadcast_to((facing[tile_offset][:, tile_offset] == 1)[:, :, None], (window_len, window_len, WIDTH_CELLS)).reshape(-1)
        frame_lens = lax.dynamic_slice(lens_pad, starts(tile_t * TILE_SIDE + TILE_SIDE), (TILE_SIDE,))
        key_ok = jnp.broadcast_to(columns[None, None, :] < frame_lens[:, None, None], (TILE_SIDE, TILE_SIDE, WIDTH_CELLS)).reshape(-1)
        visible = query_ok[:, None] & key_ok[None, :]
        scores = jnp.einsum("qhd,khd->hqk", near_query, key_f) * score_scale
        softmax_p = jnp.exp(jnp.where(visible[None], scores - near_total[:, :, None], -jnp.inf))
        probs_bf = softmax_p.astype(jnp.bfloat16)
        dprobs = jnp.einsum("qhd,khd->hqk", near_grad, value_f)
        dscores = (softmax_p * (dprobs - near_delta[:, :, None])).astype(jnp.bfloat16)
        split_q = (HEAD_COUNT, 3, TILE_SIDE, 3, TILE_SIDE, WIDTH_CELLS, queries)
        split_rows = (3, TILE_SIDE, 3, TILE_SIDE, WIDTH_CELLS, HEAD_COUNT, HEAD_DIM)
        tiles_shape = (3, 3, TILE_SIDE, TILE_SIDE, WIDTH_CELLS, channels)
        key_tiles = jnp.einsum("haibjwk,aibjwhd->abkhd", dscores.astype(jnp.float32).reshape(split_q),
                               near_query.reshape(split_rows)) * score_scale
        value_tiles = jnp.einsum("haibjwk,aibjwhd->abkhd", probs_bf.astype(jnp.float32).reshape(split_q),
                                 near_grad.reshape(split_rows))
        value_tiles = value_tiles.reshape(tiles_shape) + source_conv(grad_window, conv_weight, TILE_SIDE, WIDTH_CELLS)
        return combine_tiles(key_tiles.reshape(tiles_shape)), combine_tiles(value_tiles)

    key_t, value_t = lax.map(key_pass, tile_ids)
    key_grad = to_grid(key_t).astype(jnp.bfloat16)
    one_pad = ((1, 1), (1, 1), (1, 1), (0, 0))
    frames = TILE_SIDE * N_TA
    rows = TILE_SIDE * N_HA
    conv_out = depthwise(jnp.pad(value_states, one_pad), conv_weight, frames, rows, WIDTH_CELLS)
    layer_out = (attention_grid + conv_out).astype(jnp.bfloat16)
    value_grad = to_grid(value_t).astype(jnp.bfloat16)
    return layer_out, query_grad, key_grad, value_grad
```

```python
import functools

import jax
import jax.numpy as jnp
from jax import lax
from jax.experimental import pallas as pl
from jax.experimental.pallas import tpu as pltpu
from jax.sharding import PartitionSpec as P

HEAD_DIM = 128
GROUPS = 2
LOG2E = 1.4426950408889634
ROW_DELTA = 8
STAT_ROWS = 16


CONTRACT_LAST = (((1,), (1,)), ((), ()))


def flip_pairs(count):
    return [(i, i ^ 1) for i in range(count)]


def other_pairs(count):
    pairs = []
    for i in range(count):
        to = i + 1 if i % 2 else i - 1
        pairs.append((i, to if 0 <= to < count else i))
    return pairs


def relay_pairs(count):
    pairs = []
    for i in range(count):
        to = i - 2 if i % 2 else i + 2
        if 0 <= to < count:
            pairs.append((i, to))
    return pairs


def ta_halo(x):
    count = lax.axis_size("ta")
    return lax.ppermute(x, "ta", other_pairs(count)), lax.ppermute(x, "ta", flip_pairs(count))


def window_of(x):
    count = lax.axis_size("ha")
    near = lax.ppermute(x, "ha", flip_pairs(count))
    own_b, own_a = ta_halo(x)
    far = lax.ppermute(near, "ha", relay_pairs(count))
    near_b, near_a = ta_halo(near)
    far_b, far_a = ta_halo(far)
    return [x, near, far, own_a, near_a, far_a, own_b, near_b, far_b]


def stats_window(x):
    count = lax.axis_size("ha")
    near = lax.ppermute(x, "ha", flip_pairs(count))
    far = lax.ppermute(x, "ha", other_pairs(count))
    column = jnp.stack([x, near, far])
    column_b, column_a = ta_halo(column)
    return [column, column_a, column_b]


def offsets(index):
    sign = 1 - 2 * lax.rem(index, 2)
    return (0, sign, -sign)


def inside(index, count):
    return (index >= 0) & (index < count)


def halo_slab(tiles, even_t, even_h, in_t, in_h, width):
    def cell(tile, frame, row):
        start = (2 * frame + row) * width
        return tiles[tile][start : start + width]

    def side_h(slot_t, frame, R):
        if R in (1, 2):
            return cell(3 * slot_t, frame, R - 1)
        row = 1 if R == 0 else 0
        near, far = cell(3 * slot_t + 1, frame, row), cell(3 * slot_t + 2, frame, row)
        picked = jnp.where(even_h, far, near) if R == 0 else jnp.where(even_h, near, far)
        return jnp.where(in_h[0 if R == 0 else 1], picked, 0.0)

    slab = []
    for F in range(4):
        line = []
        for R in range(4):
            if F in (1, 2):
                line.append(side_h(0, F - 1, R))
                continue
            frame = 1 if F == 0 else 0
            first, second = side_h(1, frame, R), side_h(2, frame, R)
            picked = jnp.where(even_t, second, first) if F == 0 else jnp.where(even_t, first, second)
            line.append(jnp.where(in_t[0 if F == 0 else 1], picked, 0.0))
        slab.append(line)
    return slab


def depthwise(slab, weight, flipped, width):
    column = lax.broadcasted_iota(jnp.int32, (width, HEAD_DIM), 0)
    rows = []
    for f in range(2):
        for r in range(2):
            parts = []
            for dw in range(3):
                total = None
                for dt in range(3):
                    for dh in range(3):
                        tap = 9 * dt + 3 * dh + dw
                        tap = 26 - tap if flipped else tap
                        term = weight[tap : tap + 1] * slab[f + dt][r + dh]
                        total = term if total is None else total + term
                parts.append(total)
            before = jnp.where(column == 0, 0.0, pltpu.roll(parts[0], 1, 0))
            after = jnp.where(column == width - 1, 0.0, pltpu.roll(parts[2], width - 1, 0))
            rows.append(parts[1] + before + after)
    return jnp.concatenate(rows, axis=0)


def place(count_t, count_h):
    index_t, index_h = lax.axis_index("ta"), lax.axis_index("ha")
    even_t, even_h = lax.rem(index_t, 2) == 0, lax.rem(index_h, 2) == 0
    in_t = (index_t > 0, index_t < count_t - 1)
    in_h = (index_h > 0, index_h < count_h - 1)
    return index_t, index_h, even_t, even_h, in_t, in_h


def query_kernel(counts, width, n_prev, mask_ref, clip_ref, q_ref, grad_ref, weight_ref, *rest):
    kv = rest[:9]
    out_ref, dq_ref, stat_ref, score = rest[9 + n_prev :]
    count_t, count_h = counts
    index_t, index_h, even_t, even_h, in_t, in_h = place(count_t, count_h)
    queries = q_ref.shape[0]
    head = pl.program_id(0)
    scale = HEAD_DIM**-0.5
    lane = lax.broadcasted_iota(jnp.int32, (1, queries), 1)
    frame = lane // (2 * width)
    column = lax.rem(lane, width)

    q = q_ref[...]
    grad = grad_ref[...]
    top = None
    for slot in range(9):
        a, b = offsets(index_t)[slot // 3], offsets(index_h)[slot % 3]
        t, h = index_t + a, index_h + b
        kept = (mask_ref[index_t, index_h, 3 * (a + 1) + (b + 1)] == 1) & inside(t, count_t) & inside(h, count_h)
        safe = jnp.clip(t, 0, count_t - 1)
        lens = [jnp.where(kept, clip_ref[2 * safe + f], 0) for f in range(2)]
        bias = jnp.where(column < jnp.where(frame == 0, lens[0], lens[1]), 0.0, -jnp.inf)
        s = lax.dot_general(q, kv[slot][0], CONTRACT_LAST, preferred_element_type=jnp.float32)
        s = s * (scale * LOG2E) + bias
        score[slot] = s
        top = s if top is None else jnp.maximum(top, s)
    row_max = jnp.max(top, axis=1, keepdims=True)
    total, acc = None, None
    for slot in range(9):
        e = jnp.exp2(score[slot] - row_max)
        score[slot] = e
        part = jnp.dot(e.astype(jnp.bfloat16), kv[slot][1], preferred_element_type=jnp.float32)
        total = e if total is None else total + e
        acc = part if acc is None else acc + part
    row_total = jnp.sum(total, axis=1, keepdims=True)
    inverse = 1.0 / row_total
    attention = acc * inverse
    delta = jnp.sum(grad.astype(jnp.float32) * attention, axis=1, keepdims=True)
    dq = None
    for slot in range(9):
        dp = lax.dot_general(grad, kv[slot][1], CONTRACT_LAST, preferred_element_type=jnp.float32)
        ds = (score[slot] * (dp - delta)).astype(jnp.bfloat16)
        part = jnp.dot(ds, kv[slot][0], preferred_element_type=jnp.float32)
        dq = part if dq is None else dq + part
    dq_ref[...] = (dq * (inverse * scale)).astype(jnp.bfloat16)

    log_total = row_max + jnp.log2(row_total)
    half = lax.broadcasted_iota(jnp.int32, (queries, HEAD_DIM), 1) < HEAD_DIM // 2
    both = jnp.where(half, log_total, delta)
    pad = -queries % HEAD_DIM
    both = jnp.concatenate([both, jnp.zeros((pad, HEAD_DIM), jnp.float32)], axis=0)
    turned = both.T
    stat_ref[pl.ds(head, 1), :] = turned[0:1, :queries]
    stat_ref[pl.ds(head + ROW_DELTA, 1), :] = turned[HEAD_DIM // 2 : HEAD_DIM // 2 + 1, :queries]

    tiles = [kv[slot][1].astype(jnp.float32) for slot in range(9)]
    slab = halo_slab(tiles, even_t, even_h, in_t, in_h, width)
    conv = depthwise(slab, weight_ref[...].astype(jnp.float32), False, width)
    out_ref[...] = (attention + conv).astype(jnp.bfloat16)


def key_kernel(counts, width, n_prev, mask_ref, clip_ref, kv_ref, weight_ref, *rest):
    qg = rest[:9]
    stats = rest[9:12]
    dk_ref, dv_ref = rest[12 + n_prev :]
    count_t, count_h = counts
    index_t, index_h, even_t, even_h, in_t, in_h = place(count_t, count_h)
    keys = kv_ref.shape[1]
    head = pl.program_id(0)
    scale = HEAD_DIM**-0.5
    k, v = kv_ref[0], kv_ref[1]
    dk, dv = None, None
    for slot in range(9):
        a, b = offsets(index_t)[slot // 3], offsets(index_h)[slot % 3]
        t, h = index_t + a, index_h + b
        safe_t, safe_h = jnp.clip(t, 0, count_t - 1), jnp.clip(h, 0, count_h - 1)
        kept = (mask_ref[safe_t, safe_h, 3 * (1 - a) + (1 - b)] == 1) & inside(t, count_t) & inside(h, count_h)
        log_total = stats[slot // 3][slot % 3, pl.ds(head, 1), :]
        log_total = jnp.where(kept, log_total, jnp.inf)
        delta = stats[slot // 3][slot % 3, pl.ds(head + ROW_DELTA, 1), :]
        q, grad = qg[slot][0], qg[slot][1]
        s = lax.dot_general(k, q, CONTRACT_LAST, preferred_element_type=jnp.float32)
        p = jnp.exp2(s * (scale * LOG2E) - log_total)
        dp = lax.dot_general(v, grad, CONTRACT_LAST, preferred_element_type=jnp.float32)
        ds = (p * (dp - delta)).astype(jnp.bfloat16)
        part_v = jnp.dot(p.astype(jnp.bfloat16), grad, preferred_element_type=jnp.float32)
        part_k = jnp.dot(ds, q, preferred_element_type=jnp.float32)
        dk = part_k if dk is None else dk + part_k
        dv = part_v if dv is None else dv + part_v
    row = lax.broadcasted_iota(jnp.int32, (keys, HEAD_DIM), 0)
    lens = [clip_ref[2 * index_t + f] for f in range(2)]
    live = lax.rem(row, width) < jnp.where(row < 2 * width, lens[0], lens[1])
    dk_ref[...] = jnp.where(live, dk * scale, 0.0).astype(jnp.bfloat16)

    tiles = [qg[slot][1].astype(jnp.float32) for slot in range(9)]
    slab = halo_slab(tiles, even_t, even_h, in_t, in_h, width)
    conv = depthwise(slab, weight_ref[...].astype(jnp.float32), True, width)
    dv_ref[...] = (jnp.where(live, dv, 0.0) + conv).astype(jnp.bfloat16)


def cost(heads, rows, matmuls):
    work = heads * rows * 9 * rows * HEAD_DIM * 2 * matmuls
    return pl.CostEstimate(flops=work, bytes_accessed=heads * rows * HEAD_DIM * 2 * 24, transcendentals=heads * rows * rows * 9)


def shards(query_states, key_states, value_states, conv_weight, out_grad, tile_mask, clip_lengths):
    width, channels = query_states.shape[2:]
    rows = query_states.shape[0] * query_states.shape[1] * width
    counts = (lax.axis_size("ta"), lax.axis_size("ha"))
    heads = channels // HEAD_DIM
    group_heads = heads // GROUPS
    group_width = group_heads * HEAD_DIM
    flat = [x.reshape(rows, channels) for x in (query_states, key_states, value_states, out_grad)]
    query, key, value, grad = flat
    smem = pl.BlockSpec(memory_space=pltpu.SMEM)
    anywhere = pl.BlockSpec(memory_space=pl.ANY)
    pair_spec = pl.BlockSpec((2, rows, HEAD_DIM), lambda h: (0, 0, h))
    params = pltpu.CompilerParams(vmem_limit_bytes=40 * 1024 * 1024)
    full = jax.ShapeDtypeStruct((rows, channels), jnp.bfloat16)

    def part(x, g):
        return x[:, g * group_width : (g + 1) * group_width]

    kvs = [jnp.stack([part(key, g), part(value, g)]) for g in range(GROUPS)]
    qgs = [jnp.stack([part(query, g), part(grad, g)]) for g in range(GROUPS)]
    kv_windows = [window_of(x) for x in kvs]
    qg_windows = [window_of(x) for x in qgs]

    layer_out = query_grad = None
    stats = []
    for g in range(GROUPS):
        first = g * group_heads
        col_spec = pl.BlockSpec((rows, HEAD_DIM), lambda h, first=first: (0, h + first))
        weight_spec = pl.BlockSpec((27, HEAD_DIM), lambda h, first=first: (0, h + first))
        previous = [] if g == 0 else [layer_out, query_grad]
        layer_out, query_grad, stat = pl.pallas_call(
            functools.partial(query_kernel, counts, width, len(previous)),
            grid=(group_heads,),
            in_specs=[smem, smem, col_spec, col_spec, weight_spec] + [pair_spec] * 9 + [anywhere] * len(previous),
            out_specs=[col_spec, col_spec, pl.BlockSpec((STAT_ROWS, rows), lambda h: (0, 0))],
            out_shape=[full, full, jax.ShapeDtypeStruct((STAT_ROWS, rows), jnp.float32)],
            scratch_shapes=[pltpu.VMEM((9, rows, rows), jnp.float32)],
            input_output_aliases={14 + i: i for i in range(len(previous))},
            compiler_params=params,
            cost_estimate=cost(group_heads, rows, 4),
            name="query_side",
        )(tile_mask, clip_lengths, query, grad, conv_weight, *kv_windows[g], *previous)
        stats.append(stats_window(stat))

    key_grad = value_grad = None
    stat_spec = pl.BlockSpec((3, STAT_ROWS, rows), lambda h: (0, 0, 0))
    for g in range(GROUPS):
        first = g * group_heads
        col_spec = pl.BlockSpec((rows, HEAD_DIM), lambda h, first=first: (0, h + first))
        weight_spec = pl.BlockSpec((27, HEAD_DIM), lambda h, first=first: (0, h + first))
        previous = [] if g == 0 else [key_grad, value_grad]
        key_grad, value_grad = pl.pallas_call(
            functools.partial(key_kernel, counts, width, len(previous)),
            grid=(group_heads,),
            in_specs=[smem, smem, pair_spec, weight_spec]
            + [pair_spec] * 9
            + [stat_spec] * 3
            + [anywhere] * len(previous),
            out_specs=[col_spec, col_spec],
            out_shape=[full, full],
            input_output_aliases={16 + i: i for i in range(len(previous))},
            compiler_params=params,
            cost_estimate=cost(group_heads, rows, 4),
            name="key_side",
        )(tile_mask, clip_lengths, kvs[g], conv_weight, *qg_windows[g], *stats[g], *previous)

    return tuple(x.reshape(query_states.shape) for x in (layer_out, query_grad, key_grad, value_grad))


def solution(mesh):
    placed = P("ta", "ha", None, None)
    return jax.shard_map(
        shards,
        mesh=mesh,
        in_specs=(placed, placed, placed, P(), placed, P(), P()),
        out_specs=(placed,) * 4,
        check_vma=False,
    )
```

```python
import functools

import jax
import jax.numpy as jnp
from jax import lax
from jax.experimental import pallas as pl
from jax.experimental.pallas import tpu as pltpu
from jax.sharding import PartitionSpec as P

HEAD_DIM = 128
LOG2E = 1.4426950408889634
ROW_DELTA = 8
STAT_ROWS = 16
UNROLL = 2


CONTRACT_LAST = (((1,), (1,)), ((), ()))


def flip_pairs(count):
    return [(i, i ^ 1) for i in range(count)]


def other_pairs(count):
    pairs = []
    for i in range(count):
        to = i + 1 if i % 2 else i - 1
        pairs.append((i, to if 0 <= to < count else i))
    return pairs


def relay_pairs(count):
    pairs = []
    for i in range(count):
        to = i - 2 if i % 2 else i + 2
        if 0 <= to < count:
            pairs.append((i, to))
    return pairs


def ha_near(x):
    return lax.ppermute(x, "ha", flip_pairs(lax.axis_size("ha")))


def ha_relay(near):
    return lax.ppermute(near, "ha", relay_pairs(lax.axis_size("ha")))


def ha_far(x):
    return lax.ppermute(x, "ha", other_pairs(lax.axis_size("ha")))


def ta_both(x):
    count = lax.axis_size("ta")
    other = lax.ppermute(x, "ta", other_pairs(count))
    return lax.ppermute(x, "ta", flip_pairs(count)), other


def after(x, *earlier):
    return lax.optimization_barrier((x, *earlier))[0]


def offsets(index):
    sign = 1 - 2 * lax.rem(index, 2)
    return (0, sign, -sign)


def inside(index, count):
    return (index >= 0) & (index < count)


def halo_slab(tile, place_now, width):
    even_t, even_h, in_t, in_h = place_now
    tiles = [tile(slot).astype(jnp.float32) for slot in range(9)]

    def cell(slot, frame, row):
        start = (2 * frame + row) * width
        return tiles[slot][start : start + width]

    def side_h(slot_t, frame, R):
        if R in (1, 2):
            return cell(3 * slot_t, frame, R - 1)
        row = 1 if R == 0 else 0
        near, far = cell(3 * slot_t + 1, frame, row), cell(3 * slot_t + 2, frame, row)
        picked = jnp.where(even_h, far, near) if R == 0 else jnp.where(even_h, near, far)
        return jnp.where(in_h[0 if R == 0 else 1], picked, 0.0)

    slab = []
    for F in range(4):
        line = []
        for R in range(4):
            if F in (1, 2):
                line.append(side_h(0, F - 1, R))
                continue
            frame = 1 if F == 0 else 0
            first, second = side_h(1, frame, R), side_h(2, frame, R)
            picked = jnp.where(even_t, second, first) if F == 0 else jnp.where(even_t, first, second)
            line.append(jnp.where(in_t[0 if F == 0 else 1], picked, 0.0))
        slab.append(line)
    return slab


def depthwise(slab, weight, flipped, width):
    column = lax.broadcasted_iota(jnp.int32, (width, HEAD_DIM), 0)
    rows = []
    for f in range(2):
        for r in range(2):
            parts = []
            for dw in range(3):
                total = None
                for dt in range(3):
                    for dh in range(3):
                        tap = 9 * dt + 3 * dh + dw
                        tap = 26 - tap if flipped else tap
                        term = weight[tap : tap + 1] * slab[f + dt][r + dh]
                        total = term if total is None else total + term
                parts.append(total)
            before = jnp.where(column == 0, 0.0, pltpu.roll(parts[0], 1, 0))
            after_ = jnp.where(column == width - 1, 0.0, pltpu.roll(parts[2], width - 1, 0))
            rows.append(parts[1] + before + after_)
    return jnp.concatenate(rows, axis=0)


def place(counts):
    index_t, index_h = lax.axis_index("ta"), lax.axis_index("ha")
    even_t, even_h = lax.rem(index_t, 2) == 0, lax.rem(index_h, 2) == 0
    in_t = (index_t > 0, index_t < counts[0] - 1)
    in_h = (index_h > 0, index_h < counts[1] - 1)
    return index_t, index_h, (even_t, even_h, in_t, in_h)


def head_columns(head):
    return pl.ds(pl.multiple_of(head * HEAD_DIM, HEAD_DIM), HEAD_DIM)


def dot_last(x, y):
    return lax.dot_general(x, y, CONTRACT_LAST, preferred_element_type=jnp.float32)


def dot(x, y):
    return jnp.dot(x, y, preferred_element_type=jnp.float32)


def query_kernel(counts, width, mask_ref, clip_ref, own, other_t, pair_t, weight_ref, near, far, near_a, far_a, near_b,
                 far_b, out_ref, dq_ref, stat_ref, score, bias, stat):
    index_t, index_h, place_now = place(counts)
    rows, channels = own.shape[1:]
    heads = channels // HEAD_DIM
    scale = HEAD_DIM**-0.5
    slots = [own, near, far, pair_t, near_a, far_a, other_t, near_b, far_b]
    lane = lax.broadcasted_iota(jnp.int32, (1, 9 * rows), 1)
    limit = jnp.zeros((1, 9 * rows), jnp.int32)
    for slot in range(9):
        a, b = offsets(index_t)[slot // 3], offsets(index_h)[slot % 3]
        t, h = index_t + a, index_h + b
        kept = (mask_ref[index_t, index_h, 3 * (a + 1) + (b + 1)] == 1) & inside(t, counts[0]) & inside(h, counts[1])
        safe = jnp.clip(t, 0, counts[0] - 1)
        for f in range(2):
            live = jnp.where(kept, clip_ref[2 * safe + f], 0)
            limit = jnp.where(lane >= slot * rows + f * (rows // 2), live, limit)
    bias[...] = jnp.where(lax.rem(lane, width) < limit, 0.0, -jnp.inf)
    which = lax.broadcasted_iota(jnp.int32, (rows, HEAD_DIM), 1)

    def body(step, _):
        hs = [step * UNROLL + u for u in range(UNROLL)]
        cols = [head_columns(h) for h in hs]
        every = range(UNROLL)
        row_max, row_total, acc, dp, dq = ([None] * UNROLL for _ in range(5))
        for u in every:
            keys = jnp.concatenate([ref[0, :, cols[u]] for ref in slots], axis=0)
            s = dot_last(own[2, :, cols[u]], keys) * (scale * LOG2E) + bias[...]
            score[u] = s
            row_max[u] = jnp.max(s, axis=1, keepdims=True)
        for u in every:
            e = jnp.exp2(score[u] - row_max[u])
            score[u] = e
            row_total[u] = jnp.sum(e, axis=1, keepdims=True)
            values = jnp.concatenate([ref[1, :, cols[u]] for ref in slots], axis=0)
            acc[u] = dot(e.astype(jnp.bfloat16), values)
        for u in every:
            grad = own[3, :, cols[u]]
            inverse = 1.0 / row_total[u]
            attention = acc[u] * inverse
            delta = jnp.sum(grad.astype(jnp.float32) * attention, axis=1, keepdims=True)
            values = jnp.concatenate([ref[1, :, cols[u]] for ref in slots], axis=0)
            ds = (score[u] * (dot_last(grad, values) - delta)).astype(jnp.bfloat16)
            keys = jnp.concatenate([ref[0, :, cols[u]] for ref in slots], axis=0)
            dq_ref[:, cols[u]] = (dot(ds, keys) * (inverse * scale)).astype(jnp.bfloat16)
            log_total = row_max[u] + jnp.log2(row_total[u])
            marked = jnp.where(which == hs[u], log_total, stat[...])
            stat[...] = jnp.where(which == hs[u] + ROW_DELTA, delta, marked)
            slab = halo_slab(lambda slot: slots[slot][1, :, cols[u]], place_now, width)
            conv = depthwise(slab, weight_ref[:, cols[u]].astype(jnp.float32), False, width)
            out_ref[:, cols[u]] = (attention + conv).astype(jnp.bfloat16)
        return 0

    stat[...] = jnp.zeros_like(stat)
    lax.fori_loop(0, heads // UNROLL, body, 0)
    pad = jnp.zeros((-rows % HEAD_DIM, HEAD_DIM), jnp.float32)
    turned = jnp.concatenate([stat[...], pad], axis=0).T
    stat_ref[...] = turned[:STAT_ROWS, :rows]


def key_kernel(counts, width, mask_ref, clip_ref, own, other_t, pair_t, weight_ref, near, far, near_a, far_a, near_b,
               far_b, stat_ref, dk_ref, dv_ref, stats):
    index_t, index_h, place_now = place(counts)
    rows, channels = own.shape[1:]
    heads = channels // HEAD_DIM
    scale = HEAD_DIM**-0.5
    slots = [own, near, far, pair_t, near_a, far_a, other_t, near_b, far_b]

    def part(slot, what, cols):
        return slots[slot][what + 2 if slot % 3 == 0 else what, :, cols]

    lane = lax.broadcasted_iota(jnp.int32, (STAT_ROWS, 9 * rows), 1)
    line = lax.broadcasted_iota(jnp.int32, (STAT_ROWS, 9 * rows), 0)
    use = jnp.zeros((STAT_ROWS, 9 * rows), jnp.int32)
    for slot in range(9):
        a, b = offsets(index_t)[slot // 3], offsets(index_h)[slot % 3]
        t, h = index_t + a, index_h + b
        safe_t, safe_h = jnp.clip(t, 0, counts[0] - 1), jnp.clip(h, 0, counts[1] - 1)
        kept = (mask_ref[safe_t, safe_h, 3 * (1 - a) + (1 - b)] == 1) & inside(t, counts[0]) & inside(h, counts[1])
        use = jnp.where(lane >= slot * rows, kept.astype(jnp.int32), use)
    stats[...] = jnp.where((use == 1) | (line >= ROW_DELTA), stat_ref[...], jnp.inf)
    row = lax.broadcasted_iota(jnp.int32, (rows, HEAD_DIM), 0)
    lens = [clip_ref[2 * index_t + f] for f in range(2)]
    live = lax.rem(row, width) < jnp.where(row < 2 * width, lens[0], lens[1])

    def body(step, _):
        for u in range(UNROLL):
            head = step * UNROLL + u
            cols = head_columns(head)
            queries = jnp.concatenate([part(slot, 0, cols) for slot in range(9)], axis=0)
            grads = jnp.concatenate([part(slot, 1, cols) for slot in range(9)], axis=0)
            s = dot_last(own[0, :, cols], queries)
            p = jnp.exp2(s * (scale * LOG2E) - stats[pl.ds(head, 1), :])
            dp = dot_last(own[1, :, cols], grads)
            ds = (p * (dp - stats[pl.ds(head + ROW_DELTA, 1), :])).astype(jnp.bfloat16)
            dv = jnp.where(live, dot(p.astype(jnp.bfloat16), grads), 0.0)
            dk = jnp.where(live, dot(ds, queries) * scale, 0.0)
            dk_ref[:, cols] = dk.astype(jnp.bfloat16)
            slab = halo_slab(lambda slot: part(slot, 1, cols), place_now, width)
            conv = depthwise(slab, weight_ref[:, cols].astype(jnp.float32), True, width)
            dv_ref[:, cols] = (dv + conv).astype(jnp.bfloat16)
        return 0

    lax.fori_loop(0, heads // UNROLL, body, 0)


def cost(heads, rows, matmuls):
    work = heads * rows * 9 * rows * HEAD_DIM * 2 * matmuls
    return pl.CostEstimate(flops=work, bytes_accessed=heads * rows * HEAD_DIM * 2 * 24, transcendentals=heads * rows * rows * 9)


def shards(query_states, key_states, value_states, conv_weight, out_grad, tile_mask, clip_lengths):
    width, channels = query_states.shape[2:]
    rows = query_states.shape[0] * query_states.shape[1] * width
    counts = (lax.axis_size("ta"), lax.axis_size("ha"))
    heads = channels // HEAD_DIM
    query, key, value, grad = [x.reshape(rows, channels) for x in (query_states, key_states, value_states, out_grad)]

    kv = jnp.stack([key, value])
    own = jnp.stack([key, value, query, grad])
    near_kv = ha_near(kv)
    pair_t, other_t = ta_both(own)
    far_kv = ha_relay(near_kv)
    near_kv_a, near_kv_b = ta_both(near_kv)
    near_qg = ha_near(after(jnp.stack([query, grad]), near_kv))
    far_kv_a, far_kv_b = ta_both(far_kv)
    far_qg = ha_relay(after(near_qg, far_kv))
    near_qg_a, near_qg_b = ta_both(near_qg)
    far_qg_a, far_qg_b = ta_both(far_qg)

    smem = pl.BlockSpec(memory_space=pltpu.SMEM)
    vmem = pl.BlockSpec(memory_space=pltpu.VMEM)
    params = pltpu.CompilerParams(vmem_limit_bytes=32 * 1024 * 1024)
    full = jax.ShapeDtypeStruct((rows, channels), jnp.bfloat16)
    layer_out, query_grad, stat = pl.pallas_call(
        functools.partial(query_kernel, counts, width),
        in_specs=[smem, smem] + [vmem] * 10,
        out_specs=[vmem] * 3,
        out_shape=[full, full, jax.ShapeDtypeStruct((STAT_ROWS, rows), jnp.float32)],
        scratch_shapes=[
            pltpu.VMEM((UNROLL, rows, 9 * rows), jnp.float32),
            pltpu.VMEM((1, 9 * rows), jnp.float32),
            pltpu.VMEM((rows, HEAD_DIM), jnp.float32),
        ],
        compiler_params=params,
        cost_estimate=cost(heads, rows, 4),
        name="query_side",
    )(tile_mask, clip_lengths, own, other_t, pair_t, conv_weight, near_kv, far_kv, near_kv_a, far_kv_a, near_kv_b, far_kv_b)

    column = jnp.concatenate([stat, ha_near(stat), ha_far(stat)], axis=1)
    column_a, column_b = ta_both(column)
    stats = jnp.concatenate([column, column_a, column_b], axis=1)
    key_grad, value_grad = pl.pallas_call(
        functools.partial(key_kernel, counts, width),
        in_specs=[smem, smem] + [vmem] * 11,
        out_specs=[vmem] * 2,
        out_shape=[full, full],
        scratch_shapes=[pltpu.VMEM((STAT_ROWS, 9 * rows), jnp.float32)],
        compiler_params=params,
        cost_estimate=cost(heads, rows, 4),
        name="key_side",
    )(tile_mask, clip_lengths, own, other_t, pair_t, conv_weight, near_qg, far_qg, near_qg_a, far_qg_a, near_qg_b, far_qg_b, stats)

    return tuple(x.reshape(query_states.shape) for x in (layer_out, query_grad, key_grad, value_grad))


def solution(mesh):
    placed = P("ta", "ha", None, None)
    return jax.shard_map(
        shards,
        mesh=mesh,
        in_specs=(placed, placed, placed, P(), placed, P(), P()),
        out_specs=(placed,) * 4,
        check_vma=False,
    )
```

```python
import functools

import jax
import jax.numpy as jnp
from jax import lax
from jax.experimental import pallas as pl
from jax.experimental.pallas import tpu as pltpu
from jax.sharding import PartitionSpec as P

HEAD_DIM = 128
LOG2E = 1.4426950408889634
ROW_DELTA = 8
STAT_ROWS = 16
UNROLL = 2
FLOOR = -1e30


CONTRACT_LAST = (((1,), (1,)), ((), ()))


def flip_pairs(count):
    return [(i, i ^ 1) for i in range(count)]


def other_pairs(count):
    pairs = []
    for i in range(count):
        to = i + 1 if i % 2 else i - 1
        pairs.append((i, to if 0 <= to < count else i))
    return pairs


def relay_pairs(count):
    pairs = []
    for i in range(count):
        to = i - 2 if i % 2 else i + 2
        if 0 <= to < count:
            pairs.append((i, to))
    return pairs


def ha_near(x):
    return lax.ppermute(x, "ha", flip_pairs(lax.axis_size("ha")))


def ha_relay(near):
    return lax.ppermute(near, "ha", relay_pairs(lax.axis_size("ha")))


def ha_far(x):
    return lax.ppermute(x, "ha", other_pairs(lax.axis_size("ha")))


def ta_pair(x):
    return lax.ppermute(x, "ta", flip_pairs(lax.axis_size("ta")))


def ta_other(x):
    return lax.ppermute(x, "ta", other_pairs(lax.axis_size("ta")))


def offsets(index):
    sign = 1 - 2 * lax.rem(index, 2)
    return (0, sign, -sign)


def inside(index, count):
    return (index >= 0) & (index < count)


def halo_slab(tile, place_now, width):
    even_t, even_h, in_t, in_h = place_now
    tiles = [tile(slot).astype(jnp.float32) for slot in range(9)]

    def cell(slot, frame, row):
        start = (2 * frame + row) * width
        return tiles[slot][start : start + width]

    def side_h(slot_t, frame, R):
        if R in (1, 2):
            return cell(3 * slot_t, frame, R - 1)
        row = 1 if R == 0 else 0
        near, far = cell(3 * slot_t + 1, frame, row), cell(3 * slot_t + 2, frame, row)
        picked = jnp.where(even_h, far, near) if R == 0 else jnp.where(even_h, near, far)
        return jnp.where(in_h[0 if R == 0 else 1], picked, 0.0)

    slab = []
    for F in range(4):
        line = []
        for R in range(4):
            if F in (1, 2):
                line.append(side_h(0, F - 1, R))
                continue
            frame = 1 if F == 0 else 0
            first, second = side_h(1, frame, R), side_h(2, frame, R)
            picked = jnp.where(even_t, second, first) if F == 0 else jnp.where(even_t, first, second)
            line.append(jnp.where(in_t[0 if F == 0 else 1], picked, 0.0))
        slab.append(line)
    return slab


def depthwise(slab, weight, flipped, width):
    column = lax.broadcasted_iota(jnp.int32, (width, HEAD_DIM), 0)
    rows = []
    for f in range(2):
        for r in range(2):
            parts = []
            for dw in range(3):
                total = None
                for dt in range(3):
                    for dh in range(3):
                        tap = 9 * dt + 3 * dh + dw
                        tap = 26 - tap if flipped else tap
                        term = weight[tap : tap + 1] * slab[f + dt][r + dh]
                        total = term if total is None else total + term
                parts.append(total)
            before = jnp.where(column == 0, 0.0, pltpu.roll(parts[0], 1, 0))
            after_ = jnp.where(column == width - 1, 0.0, pltpu.roll(parts[2], width - 1, 0))
            rows.append(parts[1] + before + after_)
    return jnp.concatenate(rows, axis=0)


def place(counts):
    index_t, index_h = lax.axis_index("ta"), lax.axis_index("ha")
    even_t, even_h = lax.rem(index_t, 2) == 0, lax.rem(index_h, 2) == 0
    in_t = (index_t > 0, index_t < counts[0] - 1)
    in_h = (index_h > 0, index_h < counts[1] - 1)
    return index_t, index_h, (even_t, even_h, in_t, in_h)


def head_columns(head):
    return pl.ds(pl.multiple_of(head * HEAD_DIM, HEAD_DIM), HEAD_DIM)


def dot_last(x, y):
    return lax.dot_general(x, y, CONTRACT_LAST, preferred_element_type=jnp.float32)


def dot(x, y):
    return jnp.dot(x, y, preferred_element_type=jnp.float32)


def column_kernel(counts, width, column, last, mask_ref, clip_ref, query_ref, own, pair, other, *rest):
    slots = [own, pair, other]
    if last:
        grad_ref, sums, tops, totals = rest[0], (rest[1], rest[4]), (rest[2], rest[5]), (rest[3], rest[6])
        exp_ref, att_ref, fac_own, fac_near, fac_far, delta_ref, stat_ref, bias, stat = rest[7:]
    else:
        exp_ref, sum_ref, top_ref, total_ref, bias = rest
    index_t, index_h, _ = place(counts)
    rows, channels = query_ref.shape
    heads = channels // HEAD_DIM
    scale = HEAD_DIM**-0.5
    lane = lax.broadcasted_iota(jnp.int32, (1, 3 * rows), 1)
    limit = jnp.zeros((1, 3 * rows), jnp.int32)
    for slot in range(3):
        a, b = offsets(index_t)[slot], offsets(index_h)[column]
        t, h = index_t + a, index_h + b
        kept = (mask_ref[index_t, index_h, 3 * (a + 1) + (b + 1)] == 1) & inside(t, counts[0]) & inside(h, counts[1])
        safe = jnp.clip(t, 0, counts[0] - 1)
        for f in range(2):
            live = jnp.where(kept, clip_ref[2 * safe + f], 0)
            limit = jnp.where(lane >= slot * rows + f * (rows // 2), live, limit)
    bias[...] = jnp.where(lax.rem(lane, width) < limit, 0.0, -jnp.inf)
    which = lax.broadcasted_iota(jnp.int32, (rows, HEAD_DIM), 1)

    def body(step, _):
        hs = [step * UNROLL + u for u in range(UNROLL)]
        for h in hs:
            cols = head_columns(h)
            keys = jnp.concatenate([ref[0, :, cols] for ref in slots], axis=0)
            values = jnp.concatenate([ref[1, :, cols] for ref in slots], axis=0)
            s = dot_last(query_ref[:, cols], keys) * (scale * LOG2E) + bias[...]
            top = jnp.maximum(jnp.max(s, axis=1, keepdims=True), FLOOR)
            e = jnp.exp2(s - top)
            total = jnp.sum(e, axis=1, keepdims=True)
            e = e.astype(jnp.bfloat16)
            exp_ref[h] = e
            acc = dot(e, values)
            top = jnp.broadcast_to(top, (rows, HEAD_DIM))
            total = jnp.broadcast_to(total, (rows, HEAD_DIM))
            if not last:
                sum_ref[:, cols], top_ref[:, cols], total_ref[:, cols] = acc, top, total
                continue
            near_top, own_top = tops[1][:, cols], tops[0][:, cols]
            row_max = jnp.maximum(jnp.maximum(own_top, near_top), top)
            row_total = total * jnp.exp2(top - row_max) + totals[0][:, cols] * jnp.exp2(own_top - row_max)
            row_total = row_total + totals[1][:, cols] * jnp.exp2(near_top - row_max)
            log_total = row_max + jnp.log2(row_total)
            factors = [jnp.exp2(x - log_total) for x in (own_top, near_top, top)]
            for ref, factor in zip((fac_own, fac_near, fac_far), factors):
                ref[:, cols] = factor
            attention = sums[0][:, cols] * factors[0] + sums[1][:, cols] * factors[1] + acc * factors[2]
            att_ref[:, cols] = attention
            delta = jnp.sum(grad_ref[:, cols].astype(jnp.float32) * attention, axis=1, keepdims=True)
            delta = jnp.broadcast_to(delta, (rows, HEAD_DIM))
            delta_ref[:, cols] = delta
            marked = jnp.where(which == h, log_total, stat[...])
            stat[...] = jnp.where(which == h + ROW_DELTA, delta, marked)
        return 0

    if last:
        stat[...] = jnp.zeros_like(stat)
    lax.fori_loop(0, heads // UNROLL, body, 0)
    if last:
        pad = jnp.zeros((-rows % HEAD_DIM, HEAD_DIM), jnp.float32)
        turned = jnp.concatenate([stat[...], pad], axis=0).T
        stat_ref[...] = turned[:STAT_ROWS, :rows]


def query_kernel(counts, width, grad_ref, weight_ref, *rest):
    slots, exps, factors = rest[:9], rest[9:12], rest[12:15]
    att_ref, delta_ref, _, out_ref, dq_ref, done_ref = rest[15:]
    done_ref[...] = jnp.zeros_like(done_ref)
    _, _, place_now = place(counts)
    rows, channels = grad_ref.shape
    heads = channels // HEAD_DIM
    scale = HEAD_DIM**-0.5
    wide = -(-3 * rows // HEAD_DIM)

    def body(step, _):
        for u in range(UNROLL):
            h = step * UNROLL + u
            cols = head_columns(h)
            grad = grad_ref[:, cols]
            delta = jnp.concatenate([delta_ref[:, cols]] * wide, axis=1)[:, : 3 * rows]
            dq = None
            for column in range(3):
                refs = slots[column::3]
                values = jnp.concatenate([ref[1, :, cols] for ref in refs], axis=0)
                keys = jnp.concatenate([ref[0, :, cols] for ref in refs], axis=0)
                ds = exps[column][h].astype(jnp.float32) * (dot_last(grad, values) - delta)
                part = dot(ds.astype(jnp.bfloat16), keys) * (factors[column][:, cols] * scale)
                dq = part if dq is None else dq + part
            dq_ref[:, cols] = dq.astype(jnp.bfloat16)
            slab = halo_slab(lambda slot: slots[slot][1, :, cols], place_now, width)
            conv = depthwise(slab, weight_ref[:, cols].astype(jnp.float32), False, width)
            out_ref[:, cols] = (att_ref[:, cols] + conv).astype(jnp.bfloat16)
        return 0

    lax.fori_loop(0, heads // UNROLL, body, 0)


def key_kernel(counts, width, columns, last, mask_ref, clip_ref, own, stat_own, stat_pair, stat_other, *rest):
    count = 3 * len(columns)
    slots, rest = rest[:count], rest[count:]
    if last:
        weight_ref, *edges, dk_sum, dv_sum, dk_ref, dv_ref, stats = rest
    else:
        dk_ref, dv_ref, stats = rest
    index_t, index_h, place_now = place(counts)
    rows, channels = own.shape[1:]
    heads = channels // HEAD_DIM
    scale = HEAD_DIM**-0.5
    line = lax.broadcasted_iota(jnp.int32, (STAT_ROWS, rows), 0)
    pieces = []
    for column in columns:
        for slot, ref in enumerate((stat_own, stat_pair, stat_other)):
            a, b = offsets(index_t)[slot], offsets(index_h)[column]
            t, h = index_t + a, index_h + b
            safe_t, safe_h = jnp.clip(t, 0, counts[0] - 1), jnp.clip(h, 0, counts[1] - 1)
            kept = (mask_ref[safe_t, safe_h, 3 * (1 - a) + (1 - b)] == 1) & inside(t, counts[0]) & inside(h, counts[1])
            pieces.append(jnp.where(kept | (line >= ROW_DELTA), ref[column], jnp.inf))
    stats[...] = jnp.concatenate(pieces, axis=1)
    row = lax.broadcasted_iota(jnp.int32, (rows, HEAD_DIM), 0)
    lens = [clip_ref[2 * index_t + f] for f in range(2)]
    live = lax.rem(row, width) < jnp.where(row < 2 * width, lens[0], lens[1])

    def body(step, _):
        for u in range(UNROLL):
            head = step * UNROLL + u
            cols = head_columns(head)
            queries = jnp.concatenate([ref[0, :, cols] for ref in slots], axis=0)
            grads = jnp.concatenate([ref[1, :, cols] for ref in slots], axis=0)
            s = dot_last(own[0, :, cols], queries)
            p = jnp.exp2(s * (scale * LOG2E) - stats[pl.ds(head, 1), :])
            dp = dot_last(own[1, :, cols], grads)
            ds = (p * (dp - stats[pl.ds(head + ROW_DELTA, 1), :])).astype(jnp.bfloat16)
            dv = dot(p.astype(jnp.bfloat16), grads)
            dk = dot(ds, queries)
            if not last:
                dk_ref[:, cols], dv_ref[:, cols] = dk, dv
                continue
            dk = jnp.where(live, (dk + dk_sum[:, cols]) * scale, 0.0)
            dv = jnp.where(live, dv + dv_sum[:, cols], 0.0)
            dk_ref[:, cols] = dk.astype(jnp.bfloat16)
            around = [edges[0], edges[3], slots[0], edges[1], edges[4], slots[1], edges[2], edges[5], slots[2]]
            slab = halo_slab(lambda slot: around[slot][1, :, cols], place_now, width)
            conv = depthwise(slab, weight_ref[:, cols].astype(jnp.float32), True, width)
            dv_ref[:, cols] = (dv + conv).astype(jnp.bfloat16)
        return 0

    lax.fori_loop(0, heads // UNROLL, body, 0)


def cost(heads, rows, matmuls, columns):
    work = heads * rows * 3 * columns * rows * HEAD_DIM * 2 * matmuls
    moved = heads * rows * HEAD_DIM * 2 * 8 * columns
    return pl.CostEstimate(flops=work, bytes_accessed=moved, transcendentals=heads * rows * rows * 3 * columns)


def shards(query_states, key_states, value_states, conv_weight, out_grad, tile_mask, clip_lengths):
    width, channels = query_states.shape[2:]
    rows = query_states.shape[0] * query_states.shape[1] * width
    counts = (lax.axis_size("ta"), lax.axis_size("ha"))
    heads = channels // HEAD_DIM
    query, key, value, grad = [x.reshape(rows, channels) for x in (query_states, key_states, value_states, out_grad)]

    smem = pl.BlockSpec(memory_space=pltpu.SMEM)
    vmem = pl.BlockSpec(memory_space=pltpu.VMEM)
    params = pltpu.CompilerParams(vmem_limit_bytes=16 * 1024 * 1024)
    half = jax.ShapeDtypeStruct((rows, channels), jnp.bfloat16)
    full = jax.ShapeDtypeStruct((rows, channels), jnp.float32)
    exps = jax.ShapeDtypeStruct((heads, rows, 3 * rows), jnp.bfloat16)
    bias = pltpu.VMEM((1, 3 * rows), jnp.float32)

    def call(kernel, name, out_shape, scratch, work, *args):
        scalars = 2 if args[0] is tile_mask else 0
        return pl.pallas_call(
            kernel,
            in_specs=[smem] * scalars + [vmem] * (len(args) - scalars),
            out_specs=[vmem] * len(out_shape),
            out_shape=out_shape,
            scratch_shapes=scratch,
            compiler_params=params,
            cost_estimate=work,
            name=name,
        )(*args)

    def scores(column, tiles):
        kernel = functools.partial(column_kernel, counts, width, column, False)
        work = cost(heads, rows, 2, 1)
        return call(kernel, f"scores_{column}", [exps, full, full, full], [bias], work, tile_mask, clip_lengths, query, *tiles)

    def pair_up(x, y, *earlier):
        def kernel(x_ref, y_ref, *rest):
            rest[-1][0] = x_ref[...]
            rest[-1][1] = y_ref[...]

        return pl.pallas_call(
            kernel,
            in_specs=[vmem] * 2 + [pl.BlockSpec(memory_space=pl.ANY)] * len(earlier),
            out_specs=vmem,
            out_shape=jax.ShapeDtypeStruct((2,) + x.shape, x.dtype),
            name="pair_up",
        )(x, y, *earlier)

    def gate(x, *earlier):
        return pl.pallas_call(
            lambda *refs: None,
            in_specs=[pl.BlockSpec(memory_space=pl.ANY)] * (1 + len(earlier)),
            out_specs=pl.BlockSpec(memory_space=pl.ANY),
            out_shape=jax.ShapeDtypeStruct(x.shape, x.dtype),
            input_output_aliases={0: 0},
            name="gate",
        )(x, *earlier)

    near_k = ha_near(key)
    near_v = ha_near(gate(value, near_k))
    kv = pair_up(key, value)
    kv_b = ta_other(kv)
    far_k = ha_relay(near_k)
    kv_a = ta_pair(kv)
    qg = pair_up(query, grad, kv_a)
    qg_a, qg_b = ta_pair(qg), ta_other(qg)
    exp_own, *own_parts = scores(0, (kv, kv_a, kv_b))

    near_v = gate(near_v, own_parts[0])
    far_v = ha_relay(near_v)
    near_kv = pair_up(near_k, near_v, qg_a, qg_b)
    near_kv_a, near_kv_b = ta_pair(near_kv), ta_other(near_kv)
    near_qg = ha_near(pair_up(query, grad, near_v))
    far_kv = jnp.stack([far_k, far_v])
    far_kv_a, far_kv_b = ta_pair(far_kv), ta_other(far_kv)
    exp_near, *near_parts = scores(1, (near_kv, near_kv_a, near_kv_b))

    near_qg = gate(near_qg, near_parts[0])
    far_qg = ha_relay(near_qg)
    near_qg_a, near_qg_b = ta_pair(near_qg), ta_other(near_qg)
    exp_far, attention, fac_own, fac_near, fac_far, delta, stat = call(
        functools.partial(column_kernel, counts, width, 2, True),
        "scores_2",
        [exps] + [full] * 5 + [jax.ShapeDtypeStruct((STAT_ROWS, rows), jnp.float32)],
        [bias, pltpu.VMEM((rows, HEAD_DIM), jnp.float32)],
        cost(heads, rows, 2, 1),
        tile_mask, clip_lengths, query, far_kv, far_kv_a, far_kv_b, grad, *own_parts, *near_parts,
    )
    column = jnp.stack([stat, ha_near(stat), ha_far(stat)])
    column_a, column_b = ta_pair(column), ta_other(column)
    layer_out, query_grad, done = call(
        functools.partial(query_kernel, counts, width),
        "query_side",
        [half, half, jax.ShapeDtypeStruct((8, HEAD_DIM), jnp.float32)],
        [],
        cost(heads, rows, 2, 3),
        grad, conv_weight, kv, near_kv, far_kv, kv_a, near_kv_a, far_kv_a, kv_b, near_kv_b, far_kv_b,
        exp_own, exp_near, exp_far, fac_own, fac_near, fac_far, attention, delta, column,
    )
    far_qg = gate(far_qg, done, column_a, column_b)
    far_qg_a, far_qg_b = ta_pair(far_qg), ta_other(far_qg)

    first = (qg, qg_a, qg_b, near_qg, near_qg_a, near_qg_b)
    dk_sum, dv_sum = call(
        functools.partial(key_kernel, counts, width, (0, 1), False),
        "key_side_0",
        [full, full],
        [pltpu.VMEM((STAT_ROWS, 6 * rows), jnp.float32)],
        cost(heads, rows, 4, 2),
        tile_mask, clip_lengths, kv, column, column_a, column_b, *first,
    )
    key_grad, value_grad = call(
        functools.partial(key_kernel, counts, width, (2,), True),
        "key_side_1",
        [half, half],
        [pltpu.VMEM((STAT_ROWS, 3 * rows), jnp.float32)],
        cost(heads, rows, 4, 1),
        tile_mask, clip_lengths, kv, column, column_a, column_b, far_qg, far_qg_a, far_qg_b, conv_weight, *first, dk_sum, dv_sum,
    )
    return tuple(x.reshape(query_states.shape) for x in (layer_out, query_grad, key_grad, value_grad))


def solution(mesh):
    placed = P("ta", "ha", None, None)
    return jax.shard_map(
        shards,
        mesh=mesh,
        in_specs=(placed, placed, placed, P(), placed, P(), P()),
        out_specs=(placed,) * 4,
        check_vma=False,
    )
```

```python
import functools

import jax
import jax.numpy as jnp
from jax import lax
from jax.experimental import pallas as pl
from jax.experimental.pallas import tpu as pltpu
from jax.sharding import PartitionSpec as P

HEAD_DIM = 128
LOG2E = 1.4426950408889634
ROW_DELTA = 8
STAT_ROWS = 16
UNROLL = 2
FLOOR = -1e30
SMALL = 2 * 1024 * 1024
LARGE = 8 * 1024 * 1024


CONTRACT_LAST = (((1,), (1,)), ((), ()))


def flip_pairs(count):
    return [(i, i ^ 1) for i in range(count)]


def other_pairs(count):
    pairs = []
    for i in range(count):
        to = i + 1 if i % 2 else i - 1
        pairs.append((i, to if 0 <= to < count else i))
    return pairs


def relay_pairs(count):
    pairs = []
    for i in range(count):
        to = i - 2 if i % 2 else i + 2
        if 0 <= to < count:
            pairs.append((i, to))
    return pairs


def ha_near(x):
    return lax.ppermute(x, "ha", flip_pairs(lax.axis_size("ha")))


def ha_relay(near):
    return lax.ppermute(near, "ha", relay_pairs(lax.axis_size("ha")))


def ha_far(x):
    return lax.ppermute(x, "ha", other_pairs(lax.axis_size("ha")))


def ta_pair(x):
    return lax.ppermute(x, "ta", flip_pairs(lax.axis_size("ta")))


def ta_other(x):
    return lax.ppermute(x, "ta", other_pairs(lax.axis_size("ta")))


def offsets(index):
    sign = 1 - 2 * lax.rem(index, 2)
    return (0, sign, -sign)


def inside(index, count):
    return (index >= 0) & (index < count)


def halo_slab(tile, place_now, width):
    even_t, even_h, in_t, in_h = place_now
    tiles = [tile(slot).astype(jnp.float32) for slot in range(9)]

    def cell(slot, frame, row):
        start = (2 * frame + row) * width
        return tiles[slot][start : start + width]

    def side_h(slot_t, frame, R):
        if R in (1, 2):
            return cell(3 * slot_t, frame, R - 1)
        row = 1 if R == 0 else 0
        near, far = cell(3 * slot_t + 1, frame, row), cell(3 * slot_t + 2, frame, row)
        picked = jnp.where(even_h, far, near) if R == 0 else jnp.where(even_h, near, far)
        return jnp.where(in_h[0 if R == 0 else 1], picked, 0.0)

    slab = []
    for F in range(4):
        line = []
        for R in range(4):
            if F in (1, 2):
                line.append(side_h(0, F - 1, R))
                continue
            frame = 1 if F == 0 else 0
            first, second = side_h(1, frame, R), side_h(2, frame, R)
            picked = jnp.where(even_t, second, first) if F == 0 else jnp.where(even_t, first, second)
            line.append(jnp.where(in_t[0 if F == 0 else 1], picked, 0.0))
        slab.append(line)
    return slab


def depthwise(slab, weight, flipped, width):
    column = lax.broadcasted_iota(jnp.int32, (width, HEAD_DIM), 0)
    rows = []
    for f in range(2):
        for r in range(2):
            parts = []
            for dw in range(3):
                total = None
                for dt in range(3):
                    for dh in range(3):
                        tap = 9 * dt + 3 * dh + dw
                        tap = 26 - tap if flipped else tap
                        term = weight[tap : tap + 1] * slab[f + dt][r + dh]
                        total = term if total is None else total + term
                parts.append(total)
            before = jnp.where(column == 0, 0.0, pltpu.roll(parts[0], 1, 0))
            after_ = jnp.where(column == width - 1, 0.0, pltpu.roll(parts[2], width - 1, 0))
            rows.append(parts[1] + before + after_)
    return jnp.concatenate(rows, axis=0)


def place(counts):
    index_t, index_h = lax.axis_index("ta"), lax.axis_index("ha")
    even_t, even_h = lax.rem(index_t, 2) == 0, lax.rem(index_h, 2) == 0
    in_t = (index_t > 0, index_t < counts[0] - 1)
    in_h = (index_h > 0, index_h < counts[1] - 1)
    return index_t, index_h, (even_t, even_h, in_t, in_h)


def head_columns(head):
    return pl.ds(pl.multiple_of(head * HEAD_DIM, HEAD_DIM), HEAD_DIM)


def dot_last(x, y):
    return lax.dot_general(x, y, CONTRACT_LAST, preferred_element_type=jnp.float32)


def dot(x, y):
    return jnp.dot(x, y, preferred_element_type=jnp.float32)


def column_kernel(counts, width, column, last, mask_ref, clip_ref, query_ref, own, pair, other, *rest):
    slots = [own, pair, other]
    if last:
        grad_ref, sums, tops, totals = rest[0], (rest[1], rest[4]), (rest[2], rest[5]), (rest[3], rest[6])
        exp_ref, att_ref, fac_own, fac_near, fac_far, delta_ref, stat_ref, bias, stat = rest[7:]
    else:
        exp_ref, sum_ref, top_ref, total_ref, bias = rest
    index_t, index_h, _ = place(counts)
    rows, channels = query_ref.shape
    heads = channels // HEAD_DIM
    scale = HEAD_DIM**-0.5
    lane = lax.broadcasted_iota(jnp.int32, (1, 3 * rows), 1)
    limit = jnp.zeros((1, 3 * rows), jnp.int32)
    for slot in range(3):
        a, b = offsets(index_t)[slot], offsets(index_h)[column]
        t, h = index_t + a, index_h + b
        kept = (mask_ref[index_t, index_h, 3 * (a + 1) + (b + 1)] == 1) & inside(t, counts[0]) & inside(h, counts[1])
        safe = jnp.clip(t, 0, counts[0] - 1)
        for f in range(2):
            live = jnp.where(kept, clip_ref[2 * safe + f], 0)
            limit = jnp.where(lane >= slot * rows + f * (rows // 2), live, limit)
    bias[...] = jnp.where(lax.rem(lane, width) < limit, 0.0, -jnp.inf)
    which = lax.broadcasted_iota(jnp.int32, (rows, HEAD_DIM), 1)

    def body(step, _):
        hs = [step * UNROLL + u for u in range(UNROLL)]
        for h in hs:
            cols = head_columns(h)
            keys = jnp.concatenate([ref[0, :, cols] for ref in slots], axis=0)
            values = jnp.concatenate([ref[1, :, cols] for ref in slots], axis=0)
            s = dot_last(query_ref[:, cols], keys) * (scale * LOG2E) + bias[...]
            top = jnp.maximum(jnp.max(s, axis=1, keepdims=True), FLOOR)
            e = jnp.exp2(s - top)
            total = jnp.sum(e, axis=1, keepdims=True)
            e = e.astype(jnp.bfloat16)
            exp_ref[h] = e
            acc = dot(e, values)
            top = jnp.broadcast_to(top, (rows, HEAD_DIM))
            total = jnp.broadcast_to(total, (rows, HEAD_DIM))
            if not last:
                sum_ref[:, cols], top_ref[:, cols], total_ref[:, cols] = acc, top, total
                continue
            near_top, own_top = tops[1][:, cols], tops[0][:, cols]
            row_max = jnp.maximum(jnp.maximum(own_top, near_top), top)
            row_total = total * jnp.exp2(top - row_max) + totals[0][:, cols] * jnp.exp2(own_top - row_max)
            row_total = row_total + totals[1][:, cols] * jnp.exp2(near_top - row_max)
            log_total = row_max + jnp.log2(row_total)
            factors = [jnp.exp2(x - log_total) for x in (own_top, near_top, top)]
            for ref, factor in zip((fac_own, fac_near, fac_far), factors):
                ref[:, cols] = factor
            attention = sums[0][:, cols] * factors[0] + sums[1][:, cols] * factors[1] + acc * factors[2]
            att_ref[:, cols] = attention
            delta = jnp.sum(grad_ref[:, cols].astype(jnp.float32) * attention, axis=1, keepdims=True)
            delta = jnp.broadcast_to(delta, (rows, HEAD_DIM))
            delta_ref[:, cols] = delta
            marked = jnp.where(which == h, log_total, stat[...])
            stat[...] = jnp.where(which == h + ROW_DELTA, delta, marked)
        return 0

    if last:
        stat[...] = jnp.zeros_like(stat)
    lax.fori_loop(0, heads // UNROLL, body, 0)
    if last:
        pad = jnp.zeros((-rows % HEAD_DIM, HEAD_DIM), jnp.float32)
        turned = jnp.concatenate([stat[...], pad], axis=0).T
        stat_ref[...] = turned[:STAT_ROWS, :rows]


def query_kernel(counts, width, grad_ref, weight_ref, *rest):
    slots, exps, factors = rest[:9], rest[9:12], rest[12:15]
    att_ref, delta_ref, _, out_ref, dq_ref, done_ref = rest[15:]
    done_ref[...] = jnp.zeros_like(done_ref)
    _, _, place_now = place(counts)
    rows, channels = grad_ref.shape
    heads = channels // HEAD_DIM
    scale = HEAD_DIM**-0.5
    wide = -(-3 * rows // HEAD_DIM)

    def body(step, _):
        for u in range(UNROLL):
            h = step * UNROLL + u
            cols = head_columns(h)
            grad = grad_ref[:, cols]
            delta = jnp.concatenate([delta_ref[:, cols]] * wide, axis=1)[:, : 3 * rows]
            dq = None
            for column in range(3):
                refs = slots[column::3]
                values = jnp.concatenate([ref[1, :, cols] for ref in refs], axis=0)
                keys = jnp.concatenate([ref[0, :, cols] for ref in refs], axis=0)
                ds = exps[column][h].astype(jnp.float32) * (dot_last(grad, values) - delta)
                part = dot(ds.astype(jnp.bfloat16), keys) * (factors[column][:, cols] * scale)
                dq = part if dq is None else dq + part
            dq_ref[:, cols] = dq.astype(jnp.bfloat16)
            slab = halo_slab(lambda slot: slots[slot][1, :, cols], place_now, width)
            conv = depthwise(slab, weight_ref[:, cols].astype(jnp.float32), False, width)
            out_ref[:, cols] = (att_ref[:, cols] + conv).astype(jnp.bfloat16)
        return 0

    lax.fori_loop(0, heads // UNROLL, body, 0)


def key_kernel(counts, width, columns, last, mask_ref, clip_ref, own, stat_own, stat_pair, stat_other, *rest):
    count = 3 * len(columns)
    slots, rest = rest[:count], rest[count:]
    if last:
        weight_ref, *edges, dk_sum, dv_sum, dk_ref, dv_ref, stats = rest
    else:
        dk_ref, dv_ref, stats = rest
    index_t, index_h, place_now = place(counts)
    rows, channels = own.shape[1:]
    heads = channels // HEAD_DIM
    scale = HEAD_DIM**-0.5
    line = lax.broadcasted_iota(jnp.int32, (STAT_ROWS, rows), 0)
    pieces = []
    for column in columns:
        for slot, ref in enumerate((stat_own, stat_pair, stat_other)):
            a, b = offsets(index_t)[slot], offsets(index_h)[column]
            t, h = index_t + a, index_h + b
            safe_t, safe_h = jnp.clip(t, 0, counts[0] - 1), jnp.clip(h, 0, counts[1] - 1)
            kept = (mask_ref[safe_t, safe_h, 3 * (1 - a) + (1 - b)] == 1) & inside(t, counts[0]) & inside(h, counts[1])
            pieces.append(jnp.where(kept | (line >= ROW_DELTA), ref[column], jnp.inf))
    stats[...] = jnp.concatenate(pieces, axis=1)
    row = lax.broadcasted_iota(jnp.int32, (rows, HEAD_DIM), 0)
    lens = [clip_ref[2 * index_t + f] for f in range(2)]
    live = lax.rem(row, width) < jnp.where(row < 2 * width, lens[0], lens[1])

    def body(step, _):
        for u in range(UNROLL):
            head = step * UNROLL + u
            cols = head_columns(head)
            queries = jnp.concatenate([ref[0, :, cols] for ref in slots], axis=0)
            grads = jnp.concatenate([ref[1, :, cols] for ref in slots], axis=0)
            s = dot_last(own[0, :, cols], queries)
            p = jnp.exp2(s * (scale * LOG2E) - stats[pl.ds(head, 1), :])
            dp = dot_last(own[1, :, cols], grads)
            ds = (p * (dp - stats[pl.ds(head + ROW_DELTA, 1), :])).astype(jnp.bfloat16)
            dv = dot(p.astype(jnp.bfloat16), grads)
            dk = dot(ds, queries)
            if not last:
                dk_ref[:, cols], dv_ref[:, cols] = dk, dv
                continue
            dk = jnp.where(live, (dk + dk_sum[:, cols]) * scale, 0.0)
            dv = jnp.where(live, dv + dv_sum[:, cols], 0.0)
            dk_ref[:, cols] = dk.astype(jnp.bfloat16)
            around = [edges[0], edges[3], slots[0], edges[1], edges[4], slots[1], edges[2], edges[5], slots[2]]
            slab = halo_slab(lambda slot: around[slot][1, :, cols], place_now, width)
            conv = depthwise(slab, weight_ref[:, cols].astype(jnp.float32), True, width)
            dv_ref[:, cols] = (dv + conv).astype(jnp.bfloat16)
        return 0

    lax.fori_loop(0, heads // UNROLL, body, 0)


def cost(heads, rows, matmuls, columns):
    work = heads * rows * 3 * columns * rows * HEAD_DIM * 2 * matmuls
    moved = heads * rows * HEAD_DIM * 2 * 8 * columns
    return pl.CostEstimate(flops=work, bytes_accessed=moved, transcendentals=heads * rows * rows * 3 * columns)


def shards(query_states, key_states, value_states, conv_weight, out_grad, tile_mask, clip_lengths):
    width, channels = query_states.shape[2:]
    rows = query_states.shape[0] * query_states.shape[1] * width
    counts = (lax.axis_size("ta"), lax.axis_size("ha"))
    heads = channels // HEAD_DIM
    query, key, value, grad = [x.reshape(rows, channels) for x in (query_states, key_states, value_states, out_grad)]

    smem = pl.BlockSpec(memory_space=pltpu.SMEM)
    vmem = pl.BlockSpec(memory_space=pltpu.VMEM)
    params = pltpu.CompilerParams(vmem_limit_bytes=LARGE)
    half = jax.ShapeDtypeStruct((rows, channels), jnp.bfloat16)
    full = jax.ShapeDtypeStruct((rows, channels), jnp.float32)
    exps = jax.ShapeDtypeStruct((heads, rows, 3 * rows), jnp.bfloat16)
    bias = pltpu.VMEM((1, 3 * rows), jnp.float32)

    def call(kernel, name, out_shape, scratch, work, *args):
        scalars = 2 if args[0] is tile_mask else 0
        return pl.pallas_call(
            kernel,
            in_specs=[smem] * scalars + [vmem] * (len(args) - scalars),
            out_specs=[vmem] * len(out_shape),
            out_shape=out_shape,
            scratch_shapes=scratch,
            compiler_params=params,
            cost_estimate=work,
            name=name,
        )(*args)

    def scores(column, tiles):
        kernel = functools.partial(column_kernel, counts, width, column, False)
        work = cost(heads, rows, 2, 1)
        return call(kernel, f"scores_{column}", [exps, full, full, full], [bias], work, tile_mask, clip_lengths, query, *tiles)

    def pair_up(x, y, *earlier):
        def kernel(x_ref, y_ref, *rest):
            rest[-1][0] = x_ref[...]
            rest[-1][1] = y_ref[...]

        return pl.pallas_call(
            kernel,
            in_specs=[vmem] * 2 + [pl.BlockSpec(memory_space=pl.ANY)] * len(earlier),
            out_specs=vmem,
            out_shape=jax.ShapeDtypeStruct((2,) + x.shape, x.dtype),
            compiler_params=pltpu.CompilerParams(vmem_limit_bytes=SMALL),
            name="pair_up",
        )(x, y, *earlier)

    def gate(x, *earlier):
        return pl.pallas_call(
            lambda *refs: None,
            in_specs=[pl.BlockSpec(memory_space=pl.ANY)] * (1 + len(earlier)),
            out_specs=pl.BlockSpec(memory_space=pl.ANY),
            out_shape=jax.ShapeDtypeStruct(x.shape, x.dtype),
            input_output_aliases={0: 0},
            compiler_params=pltpu.CompilerParams(vmem_limit_bytes=SMALL),
            name="gate",
        )(x, *earlier)

    near_k = ha_near(key)
    near_v = ha_near(gate(value, near_k))
    kv = pair_up(key, value)
    kv_b = ta_other(kv)
    far_k = ha_relay(near_k)
    kv_a = ta_pair(kv)
    qg = pair_up(query, grad, kv_a)
    qg_a, qg_b = ta_pair(qg), ta_other(qg)
    exp_own, *own_parts = scores(0, (kv, kv_a, kv_b))

    near_v = gate(near_v, own_parts[0])
    far_v = ha_relay(near_v)
    near_kv = pair_up(near_k, near_v, qg_a, qg_b)
    near_kv_a, near_kv_b = ta_pair(near_kv), ta_other(near_kv)
    near_qg = ha_near(pair_up(query, grad, near_v))
    far_kv = jnp.stack([far_k, far_v])
    far_kv_a, far_kv_b = ta_pair(far_kv), ta_other(far_kv)
    exp_near, *near_parts = scores(1, (near_kv, near_kv_a, near_kv_b))

    near_qg = gate(near_qg, near_parts[0])
    far_qg = ha_relay(near_qg)
    near_qg_a, near_qg_b = ta_pair(near_qg), ta_other(near_qg)
    exp_far, attention, fac_own, fac_near, fac_far, delta, stat = call(
        functools.partial(column_kernel, counts, width, 2, True),
        "scores_2",
        [exps] + [full] * 5 + [jax.ShapeDtypeStruct((STAT_ROWS, rows), jnp.float32)],
        [bias, pltpu.VMEM((rows, HEAD_DIM), jnp.float32)],
        cost(heads, rows, 2, 1),
        tile_mask, clip_lengths, query, far_kv, far_kv_a, far_kv_b, grad, *own_parts, *near_parts,
    )
    column = jnp.stack([stat, ha_near(stat), ha_far(stat)])
    column_a, column_b = ta_pair(column), ta_other(column)
    layer_out, query_grad, done = call(
        functools.partial(query_kernel, counts, width),
        "query_side",
        [half, half, jax.ShapeDtypeStruct((8, HEAD_DIM), jnp.float32)],
        [],
        cost(heads, rows, 2, 3),
        grad, conv_weight, kv, near_kv, far_kv, kv_a, near_kv_a, far_kv_a, kv_b, near_kv_b, far_kv_b,
        exp_own, exp_near, exp_far, fac_own, fac_near, fac_far, attention, delta, column,
    )
    far_qg = gate(far_qg, done, column_a, column_b)
    far_qg_a, far_qg_b = ta_pair(far_qg), ta_other(far_qg)

    first = (qg, qg_a, qg_b, near_qg, near_qg_a, near_qg_b)
    dk_sum, dv_sum = call(
        functools.partial(key_kernel, counts, width, (0, 1), False),
        "key_side_0",
        [full, full],
        [pltpu.VMEM((STAT_ROWS, 6 * rows), jnp.float32)],
        cost(heads, rows, 4, 2),
        tile_mask, clip_lengths, kv, column, column_a, column_b, *first,
    )
    key_grad, value_grad = call(
        functools.partial(key_kernel, counts, width, (2,), True),
        "key_side_1",
        [half, half],
        [pltpu.VMEM((STAT_ROWS, 3 * rows), jnp.float32)],
        cost(heads, rows, 4, 1),
        tile_mask, clip_lengths, kv, column, column_a, column_b, far_qg, far_qg_a, far_qg_b, conv_weight, *first, dk_sum, dv_sum,
    )
    return tuple(x.reshape(query_states.shape) for x in (layer_out, query_grad, key_grad, value_grad))


def solution(mesh):
    placed = P("ta", "ha", None, None)
    return jax.shard_map(
        shards,
        mesh=mesh,
        in_specs=(placed, placed, placed, P(), placed, P(), P()),
        out_specs=(placed,) * 4,
        check_vma=False,
    )
```

```python
import functools

import jax
import jax.numpy as jnp
from jax import lax
from jax.experimental import pallas as pl
from jax.experimental.pallas import tpu as pltpu
from jax.sharding import PartitionSpec as P

HEAD_DIM = 128
LOG2E = 1.4426950408889634
ROW_DELTA = 8
STAT_ROWS = 16
UNROLL = 2
FLOOR = -1e30
SMALL = 2 * 1024 * 1024
LARGE = 8 * 1024 * 1024


CONTRACT_LAST = (((1,), (1,)), ((), ()))


def flip_pairs(count):
    return [(i, i ^ 1) for i in range(count)]


def other_pairs(count):
    pairs = []
    for i in range(count):
        to = i + 1 if i % 2 else i - 1
        pairs.append((i, to if 0 <= to < count else i))
    return pairs


def relay_pairs(count):
    pairs = []
    for i in range(count):
        to = i - 2 if i % 2 else i + 2
        if 0 <= to < count:
            pairs.append((i, to))
    return pairs


def ha_near(x):
    return lax.ppermute(x, "ha", flip_pairs(lax.axis_size("ha")))


def ha_relay(near):
    return lax.ppermute(near, "ha", relay_pairs(lax.axis_size("ha")))


def ha_far(x):
    return lax.ppermute(x, "ha", other_pairs(lax.axis_size("ha")))


def ta_pair(x):
    return lax.ppermute(x, "ta", flip_pairs(lax.axis_size("ta")))


def ta_other(x):
    return lax.ppermute(x, "ta", other_pairs(lax.axis_size("ta")))


def offsets(index):
    sign = 1 - 2 * lax.rem(index, 2)
    return (0, sign, -sign)


def inside(index, count):
    return (index >= 0) & (index < count)


def halo_slab(tile, place_now, width):
    even_t, even_h, in_t, in_h = place_now
    tiles = [tile(slot).astype(jnp.float32) for slot in range(9)]

    def cell(slot, frame, row):
        start = (2 * frame + row) * width
        return tiles[slot][start : start + width]

    def side_h(slot_t, frame, R):
        if R in (1, 2):
            return cell(3 * slot_t, frame, R - 1)
        row = 1 if R == 0 else 0
        near, far = cell(3 * slot_t + 1, frame, row), cell(3 * slot_t + 2, frame, row)
        picked = jnp.where(even_h, far, near) if R == 0 else jnp.where(even_h, near, far)
        return jnp.where(in_h[0 if R == 0 else 1], picked, 0.0)

    slab = []
    for F in range(4):
        line = []
        for R in range(4):
            if F in (1, 2):
                line.append(side_h(0, F - 1, R))
                continue
            frame = 1 if F == 0 else 0
            first, second = side_h(1, frame, R), side_h(2, frame, R)
            picked = jnp.where(even_t, second, first) if F == 0 else jnp.where(even_t, first, second)
            line.append(jnp.where(in_t[0 if F == 0 else 1], picked, 0.0))
        slab.append(line)
    return slab


def depthwise(slab, weight, flipped, width):
    column = lax.broadcasted_iota(jnp.int32, (width, HEAD_DIM), 0)
    rows = []
    for f in range(2):
        for r in range(2):
            parts = []
            for dw in range(3):
                total = None
                for dt in range(3):
                    for dh in range(3):
                        tap = 9 * dt + 3 * dh + dw
                        tap = 26 - tap if flipped else tap
                        term = weight[tap : tap + 1] * slab[f + dt][r + dh]
                        total = term if total is None else total + term
                parts.append(total)
            before = jnp.where(column == 0, 0.0, pltpu.roll(parts[0], 1, 0))
            after_ = jnp.where(column == width - 1, 0.0, pltpu.roll(parts[2], width - 1, 0))
            rows.append(parts[1] + before + after_)
    return jnp.concatenate(rows, axis=0)


def place(counts):
    index_t, index_h = lax.axis_index("ta"), lax.axis_index("ha")
    even_t, even_h = lax.rem(index_t, 2) == 0, lax.rem(index_h, 2) == 0
    in_t = (index_t > 0, index_t < counts[0] - 1)
    in_h = (index_h > 0, index_h < counts[1] - 1)
    return index_t, index_h, (even_t, even_h, in_t, in_h)


def head_columns(head):
    return pl.ds(pl.multiple_of(head * HEAD_DIM, HEAD_DIM), HEAD_DIM)


def dot_last(x, y):
    return lax.dot_general(x, y, CONTRACT_LAST, preferred_element_type=jnp.float32)


def dot(x, y):
    return jnp.dot(x, y, preferred_element_type=jnp.float32)


def column_kernel(counts, width, column, last, mask_ref, clip_ref, query_ref, own, pair, other, *rest):
    slots = [own, pair, other]
    if last:
        grad_ref, sums, tops, totals = rest[0], (rest[1], rest[4]), (rest[2], rest[5]), (rest[3], rest[6])
        exp_ref, att_ref, fac_own, fac_near, fac_far, delta_ref, stat_ref, bias, stat = rest[7:]
    else:
        exp_ref, sum_ref, top_ref, total_ref, bias = rest
    index_t, index_h, _ = place(counts)
    rows, channels = query_ref.shape
    heads = channels // HEAD_DIM
    scale = HEAD_DIM**-0.5
    lane = lax.broadcasted_iota(jnp.int32, (1, 3 * rows), 1)
    limit = jnp.zeros((1, 3 * rows), jnp.int32)
    for slot in range(3):
        a, b = offsets(index_t)[slot], offsets(index_h)[column]
        t, h = index_t + a, index_h + b
        kept = (mask_ref[index_t, index_h, 3 * (a + 1) + (b + 1)] == 1) & inside(t, counts[0]) & inside(h, counts[1])
        safe = jnp.clip(t, 0, counts[0] - 1)
        for f in range(2):
            live = jnp.where(kept, clip_ref[2 * safe + f], 0)
            limit = jnp.where(lane >= slot * rows + f * (rows // 2), live, limit)
    bias[...] = jnp.where(lax.rem(lane, width) < limit, 0.0, -jnp.inf)
    which = lax.broadcasted_iota(jnp.int32, (rows, HEAD_DIM), 1)

    def body(step, _):
        hs = [step * UNROLL + u for u in range(UNROLL)]
        for h in hs:
            cols = head_columns(h)
            keys = jnp.concatenate([ref[0, :, cols] for ref in slots], axis=0)
            values = jnp.concatenate([ref[1, :, cols] for ref in slots], axis=0)
            s = dot_last(query_ref[:, cols], keys) * (scale * LOG2E) + bias[...]
            top = jnp.maximum(jnp.max(s, axis=1, keepdims=True), FLOOR)
            e = jnp.exp2(s - top)
            total = jnp.sum(e, axis=1, keepdims=True)
            e = e.astype(jnp.bfloat16)
            exp_ref[h] = e
            acc = dot(e, values)
            top = jnp.broadcast_to(top, (rows, HEAD_DIM))
            total = jnp.broadcast_to(total, (rows, HEAD_DIM))
            if not last:
                sum_ref[:, cols], top_ref[:, cols], total_ref[:, cols] = acc, top, total
                continue
            near_top, own_top = tops[1][:, cols], tops[0][:, cols]
            row_max = jnp.maximum(jnp.maximum(own_top, near_top), top)
            row_total = total * jnp.exp2(top - row_max) + totals[0][:, cols] * jnp.exp2(own_top - row_max)
            row_total = row_total + totals[1][:, cols] * jnp.exp2(near_top - row_max)
            log_total = row_max + jnp.log2(row_total)
            factors = [jnp.exp2(x - log_total) for x in (own_top, near_top, top)]
            for ref, factor in zip((fac_own, fac_near, fac_far), factors):
                ref[:, cols] = factor
            attention = sums[0][:, cols] * factors[0] + sums[1][:, cols] * factors[1] + acc * factors[2]
            att_ref[:, cols] = attention
            delta = jnp.sum(grad_ref[:, cols].astype(jnp.float32) * attention, axis=1, keepdims=True)
            delta = jnp.broadcast_to(delta, (rows, HEAD_DIM))
            delta_ref[:, cols] = delta
            marked = jnp.where(which == h, log_total, stat[...])
            stat[...] = jnp.where(which == h + ROW_DELTA, delta, marked)
        return 0

    if last:
        stat[...] = jnp.zeros_like(stat)
    lax.fori_loop(0, heads // UNROLL, body, 0)
    if last:
        pad = jnp.zeros((-rows % HEAD_DIM, HEAD_DIM), jnp.float32)
        turned = jnp.concatenate([stat[...], pad], axis=0).T
        stat_ref[...] = turned[:STAT_ROWS, :rows]


def query_kernel(counts, width, grad_ref, weight_ref, *rest):
    slots, exps, factors = rest[:9], rest[9:12], rest[12:15]
    att_ref, delta_ref, out_ref, dq_ref, done_ref = rest[15:]
    done_ref[...] = jnp.zeros_like(done_ref)
    _, _, place_now = place(counts)
    rows, channels = grad_ref.shape
    heads = channels // HEAD_DIM
    scale = HEAD_DIM**-0.5
    wide = -(-3 * rows // HEAD_DIM)

    def body(step, _):
        for u in range(UNROLL):
            h = step * UNROLL + u
            cols = head_columns(h)
            grad = grad_ref[:, cols]
            delta = jnp.concatenate([delta_ref[:, cols]] * wide, axis=1)[:, : 3 * rows]
            dq = None
            for column in range(3):
                refs = slots[column::3]
                values = jnp.concatenate([ref[1, :, cols] for ref in refs], axis=0)
                keys = jnp.concatenate([ref[0, :, cols] for ref in refs], axis=0)
                ds = exps[column][h].astype(jnp.float32) * (dot_last(grad, values) - delta)
                part = dot(ds.astype(jnp.bfloat16), keys) * (factors[column][:, cols] * scale)
                dq = part if dq is None else dq + part
            dq_ref[:, cols] = dq.astype(jnp.bfloat16)
            slab = halo_slab(lambda slot: slots[slot][1, :, cols], place_now, width)
            conv = depthwise(slab, weight_ref[:, cols].astype(jnp.float32), False, width)
            out_ref[:, cols] = (att_ref[:, cols] + conv).astype(jnp.bfloat16)
        return 0

    lax.fori_loop(0, heads // UNROLL, body, 0)


def key_kernel(counts, width, columns, last, mask_ref, clip_ref, own, stat_ref, *rest):
    count = 3 * len(columns)
    slots, rest = rest[:count], rest[count:]
    if last:
        weight_ref, *edges, dk_sum, dv_sum, dk_ref, dv_ref, stats, landed, sems = rest
    else:
        dk_ref, dv_ref, stats, landed, sems = rest
    index_t, index_h, place_now = place(counts)
    rows, channels = own.shape[1:]
    heads = channels // HEAD_DIM
    scale = HEAD_DIM**-0.5
    line = lax.broadcasted_iota(jnp.int32, (STAT_ROWS, rows), 0)
    copies, kept = [], []
    for column in columns:
        for slot in range(3):
            a, b = offsets(index_t)[slot], offsets(index_h)[column]
            t, h = index_t + a, index_h + b
            safe_t, safe_h = jnp.clip(t, 0, counts[0] - 1), jnp.clip(h, 0, counts[1] - 1)
            keep = mask_ref[safe_t, safe_h, 3 * (1 - a) + (1 - b)] == 1
            kept.append(keep & inside(t, counts[0]) & inside(h, counts[1]))
            i = len(copies)
            copies.append(pltpu.make_async_copy(stat_ref.at[safe_t * counts[1] + safe_h], landed.at[i], sems.at[i]))
    for copy in copies:
        copy.start()
    for copy in copies:
        copy.wait()
    pieces = [jnp.where(kept[i] | (line >= ROW_DELTA), landed[i], jnp.inf) for i in range(len(copies))]
    stats[...] = jnp.concatenate(pieces, axis=1)
    row = lax.broadcasted_iota(jnp.int32, (rows, HEAD_DIM), 0)
    lens = [clip_ref[2 * index_t + f] for f in range(2)]
    live = lax.rem(row, width) < jnp.where(row < 2 * width, lens[0], lens[1])

    def body(step, _):
        for u in range(UNROLL):
            head = step * UNROLL + u
            cols = head_columns(head)
            queries = jnp.concatenate([ref[0, :, cols] for ref in slots], axis=0)
            grads = jnp.concatenate([ref[1, :, cols] for ref in slots], axis=0)
            s = dot_last(own[0, :, cols], queries)
            p = jnp.exp2(s * (scale * LOG2E) - stats[pl.ds(head, 1), :])
            dp = dot_last(own[1, :, cols], grads)
            ds = (p * (dp - stats[pl.ds(head + ROW_DELTA, 1), :])).astype(jnp.bfloat16)
            dv = dot(p.astype(jnp.bfloat16), grads)
            dk = dot(ds, queries)
            if not last:
                dk_ref[:, cols], dv_ref[:, cols] = dk, dv
                continue
            dk = jnp.where(live, (dk + dk_sum[:, cols]) * scale, 0.0)
            dv = jnp.where(live, dv + dv_sum[:, cols], 0.0)
            dk_ref[:, cols] = dk.astype(jnp.bfloat16)
            around = [edges[0], edges[3], slots[0], edges[1], edges[4], slots[1], edges[2], edges[5], slots[2]]
            slab = halo_slab(lambda slot: around[slot][1, :, cols], place_now, width)
            conv = depthwise(slab, weight_ref[:, cols].astype(jnp.float32), True, width)
            dv_ref[:, cols] = (dv + conv).astype(jnp.bfloat16)
        return 0

    lax.fori_loop(0, heads // UNROLL, body, 0)


def cost(heads, rows, matmuls, columns):
    work = heads * rows * 3 * columns * rows * HEAD_DIM * 2 * matmuls
    moved = heads * rows * HEAD_DIM * 2 * 8 * columns
    return pl.CostEstimate(flops=work, bytes_accessed=moved, transcendentals=heads * rows * rows * 3 * columns)


def shards(query_states, key_states, value_states, conv_weight, out_grad, tile_mask, clip_lengths):
    width, channels = query_states.shape[2:]
    rows = query_states.shape[0] * query_states.shape[1] * width
    counts = (lax.axis_size("ta"), lax.axis_size("ha"))
    heads = channels // HEAD_DIM
    query, key, value, grad = [x.reshape(rows, channels) for x in (query_states, key_states, value_states, out_grad)]

    smem = pl.BlockSpec(memory_space=pltpu.SMEM)
    vmem = pl.BlockSpec(memory_space=pltpu.VMEM)
    params = pltpu.CompilerParams(vmem_limit_bytes=LARGE)
    half = jax.ShapeDtypeStruct((rows, channels), jnp.bfloat16)
    full = jax.ShapeDtypeStruct((rows, channels), jnp.float32)
    exps = jax.ShapeDtypeStruct((heads, rows, 3 * rows), jnp.bfloat16)
    bias = pltpu.VMEM((1, 3 * rows), jnp.float32)

    stats = None

    def call(kernel, name, out_shape, scratch, work, *args):
        scalars = 2 if args[0] is tile_mask else 0
        return pl.pallas_call(
            kernel,
            in_specs=[smem] * scalars + [pl.BlockSpec(memory_space=pl.ANY) if x is stats else vmem for x in args[scalars:]],
            out_specs=[vmem] * len(out_shape),
            out_shape=out_shape,
            scratch_shapes=scratch,
            compiler_params=params,
            cost_estimate=work,
            name=name,
        )(*args)

    def scores(column, tiles):
        kernel = functools.partial(column_kernel, counts, width, column, False)
        work = cost(heads, rows, 2, 1)
        return call(kernel, f"scores_{column}", [exps, full, full, full], [bias], work, tile_mask, clip_lengths, query, *tiles)

    def later(x, *earlier):
        def kernel(x_ref, *rest):
            rest[-1][...] = x_ref[...]

        return pl.pallas_call(
            kernel,
            in_specs=[vmem] + [pl.BlockSpec(memory_space=pl.ANY)] * len(earlier),
            out_specs=vmem,
            out_shape=jax.ShapeDtypeStruct(x.shape, x.dtype),
            compiler_params=pltpu.CompilerParams(vmem_limit_bytes=SMALL),
            name="later",
        )(x, *earlier)

    def pair_up(x, y, *earlier):
        def kernel(x_ref, y_ref, *rest):
            rest[-1][0] = x_ref[...]
            rest[-1][1] = y_ref[...]

        return pl.pallas_call(
            kernel,
            in_specs=[vmem] * 2 + [pl.BlockSpec(memory_space=pl.ANY)] * len(earlier),
            out_specs=vmem,
            out_shape=jax.ShapeDtypeStruct((2,) + x.shape, x.dtype),
            compiler_params=pltpu.CompilerParams(vmem_limit_bytes=SMALL),
            name="pair_up",
        )(x, y, *earlier)

    def gate(x, *earlier):
        return pl.pallas_call(
            lambda *refs: None,
            in_specs=[pl.BlockSpec(memory_space=pl.ANY)] * (1 + len(earlier)),
            out_specs=pl.BlockSpec(memory_space=pl.ANY),
            out_shape=jax.ShapeDtypeStruct(x.shape, x.dtype),
            input_output_aliases={0: 0},
            compiler_params=pltpu.CompilerParams(vmem_limit_bytes=SMALL),
            name="gate",
        )(x, *earlier)

    kv = jnp.stack([key, value])
    near_kv = ha_near(kv)
    kv_a, kv_b = ta_pair(kv), ta_other(kv)
    qg = pair_up(query, grad, kv_a)
    qg_a, qg_b = ta_pair(qg), ta_other(qg)
    exp_own, *own_parts = scores(0, (kv, kv_a, kv_b))

    far_kv = ha_relay(near_kv)
    near_kv_again = later(near_kv, qg_a, qg_b)
    near_kv_a, near_kv_b = ta_pair(near_kv_again), ta_other(near_kv_again)
    near_qg = ha_near(pair_up(query, grad, near_kv))
    exp_near, *near_parts = scores(1, (near_kv, near_kv_a, near_kv_b))

    far_kv = gate(far_kv, own_parts[0])
    far_kv_a, far_kv_b = ta_pair(far_kv), ta_other(far_kv)
    near_qg = gate(near_qg, near_parts[0])
    far_qg = ha_relay(near_qg)
    near_qg_a, near_qg_b = ta_pair(near_qg), ta_other(near_qg)
    exp_far, attention, fac_own, fac_near, fac_far, delta, stat = call(
        functools.partial(column_kernel, counts, width, 2, True),
        "scores_2",
        [exps] + [full] * 5 + [jax.ShapeDtypeStruct((STAT_ROWS, rows), jnp.float32)],
        [bias, pltpu.VMEM((rows, HEAD_DIM), jnp.float32)],
        cost(heads, rows, 2, 1),
        tile_mask, clip_lengths, query, far_kv, far_kv_a, far_kv_b, grad, *own_parts, *near_parts,
    )
    stats = lax.all_gather(stat, ("ta", "ha"))
    layer_out, query_grad, done = call(
        functools.partial(query_kernel, counts, width),
        "query_side",
        [half, half, jax.ShapeDtypeStruct((8, HEAD_DIM), jnp.float32)],
        [],
        cost(heads, rows, 2, 3),
        grad, conv_weight, kv, near_kv, far_kv, kv_a, near_kv_a, far_kv_a, kv_b, near_kv_b, far_kv_b,
        exp_own, exp_near, exp_far, fac_own, fac_near, fac_far, attention, delta,
    )
    far_qg = gate(far_qg, done)
    far_qg_a, far_qg_b = ta_pair(far_qg), ta_other(far_qg)

    def stat_scratch(count):
        return [
            pltpu.VMEM((STAT_ROWS, count * rows), jnp.float32),
            pltpu.VMEM((count, STAT_ROWS, rows), jnp.float32),
            pltpu.SemaphoreType.DMA((count,)),
        ]

    first = (qg, qg_a, qg_b, near_qg, near_qg_a, near_qg_b)
    dk_sum, dv_sum = call(
        functools.partial(key_kernel, counts, width, (0, 1), False),
        "key_side_0",
        [full, full],
        stat_scratch(6),
        cost(heads, rows, 4, 2),
        tile_mask, clip_lengths, kv, stats, *first,
    )
    key_grad, value_grad = call(
        functools.partial(key_kernel, counts, width, (2,), True),
        "key_side_1",
        [half, half],
        stat_scratch(3),
        cost(heads, rows, 4, 1),
        tile_mask, clip_lengths, kv, stats, far_qg, far_qg_a, far_qg_b, conv_weight, *first, dk_sum, dv_sum,
    )
    return tuple(x.reshape(query_states.shape) for x in (layer_out, query_grad, key_grad, value_grad))


def solution(mesh):
    placed = P("ta", "ha", None, None)
    return jax.shard_map(
        shards,
        mesh=mesh,
        in_specs=(placed, placed, placed, P(), placed, P(), P()),
        out_specs=(placed,) * 4,
        check_vma=False,
    )
```

```python
import functools

import jax
import jax.numpy as jnp
from jax import lax
from jax.experimental import pallas as pl
from jax.experimental.pallas import tpu as pltpu
from jax.sharding import PartitionSpec as P

HEAD_DIM = 128
LOG2E = 1.4426950408889634
ROW_DELTA = 8
STAT_ROWS = 16
STAT_LANES = 256
UNROLL = 2
FLOOR = -1e30
SMALL = 2 * 1024 * 1024
LARGE = 8 * 1024 * 1024


CONTRACT_LAST = (((1,), (1,)), ((), ()))


def flip_pairs(count):
    return [(i, i ^ 1) for i in range(count)]


def other_pairs(count):
    pairs = []
    for i in range(count):
        to = i + 1 if i % 2 else i - 1
        pairs.append((i, to if 0 <= to < count else i))
    return pairs


def relay_pairs(count):
    pairs = []
    for i in range(count):
        to = i - 2 if i % 2 else i + 2
        if 0 <= to < count:
            pairs.append((i, to))
    return pairs


def ha_near(x):
    return lax.ppermute(x, "ha", flip_pairs(lax.axis_size("ha")))


def ha_relay(near):
    return lax.ppermute(near, "ha", relay_pairs(lax.axis_size("ha")))


def ha_far(x):
    return lax.ppermute(x, "ha", other_pairs(lax.axis_size("ha")))


def ta_pair(x):
    return lax.ppermute(x, "ta", flip_pairs(lax.axis_size("ta")))


def ta_other(x):
    return lax.ppermute(x, "ta", other_pairs(lax.axis_size("ta")))


def offsets(index):
    sign = 1 - 2 * lax.rem(index, 2)
    return (0, sign, -sign)


def inside(index, count):
    return (index >= 0) & (index < count)


def halo_slab(tile, place_now, width):
    even_t, even_h, in_t, in_h = place_now
    tiles = [tile(slot).astype(jnp.float32) for slot in range(9)]

    def cell(slot, frame, row):
        start = (2 * frame + row) * width
        return tiles[slot][start : start + width]

    def side_h(slot_t, frame, R):
        if R in (1, 2):
            return cell(3 * slot_t, frame, R - 1)
        row = 1 if R == 0 else 0
        near, far = cell(3 * slot_t + 1, frame, row), cell(3 * slot_t + 2, frame, row)
        picked = jnp.where(even_h, far, near) if R == 0 else jnp.where(even_h, near, far)
        return jnp.where(in_h[0 if R == 0 else 1], picked, 0.0)

    slab = []
    for F in range(4):
        line = []
        for R in range(4):
            if F in (1, 2):
                line.append(side_h(0, F - 1, R))
                continue
            frame = 1 if F == 0 else 0
            first, second = side_h(1, frame, R), side_h(2, frame, R)
            picked = jnp.where(even_t, second, first) if F == 0 else jnp.where(even_t, first, second)
            line.append(jnp.where(in_t[0 if F == 0 else 1], picked, 0.0))
        slab.append(line)
    return slab


def depthwise(slab, weight, flipped, width):
    column = lax.broadcasted_iota(jnp.int32, (width, HEAD_DIM), 0)
    rows = []
    for f in range(2):
        for r in range(2):
            parts = []
            for dw in range(3):
                total = None
                for dt in range(3):
                    for dh in range(3):
                        tap = 9 * dt + 3 * dh + dw
                        tap = 26 - tap if flipped else tap
                        term = weight[tap : tap + 1] * slab[f + dt][r + dh]
                        total = term if total is None else total + term
                parts.append(total)
            before = jnp.where(column == 0, 0.0, pltpu.roll(parts[0], 1, 0))
            after_ = jnp.where(column == width - 1, 0.0, pltpu.roll(parts[2], width - 1, 0))
            rows.append(parts[1] + before + after_)
    return jnp.concatenate(rows, axis=0)


def place(counts):
    index_t, index_h = lax.axis_index("ta"), lax.axis_index("ha")
    even_t, even_h = lax.rem(index_t, 2) == 0, lax.rem(index_h, 2) == 0
    in_t = (index_t > 0, index_t < counts[0] - 1)
    in_h = (index_h > 0, index_h < counts[1] - 1)
    return index_t, index_h, (even_t, even_h, in_t, in_h)


def head_columns(head):
    return pl.ds(pl.multiple_of(head * HEAD_DIM, HEAD_DIM), HEAD_DIM)


def dot_last(x, y):
    return lax.dot_general(x, y, CONTRACT_LAST, preferred_element_type=jnp.float32)


def dot(x, y):
    return jnp.dot(x, y, preferred_element_type=jnp.float32)


def column_kernel(counts, width, column, last, mask_ref, clip_ref, query_ref, own, pair, other, *rest):
    slots = [own, pair, other]
    if last:
        grad_ref, sums, tops, totals = rest[0], (rest[1], rest[4]), (rest[2], rest[5]), (rest[3], rest[6])
        exp_ref, att_ref, fac_own, fac_near, fac_far, delta_ref, stat_ref, bias, stat = rest[7:]
    else:
        exp_ref, sum_ref, top_ref, total_ref, bias = rest
    index_t, index_h, _ = place(counts)
    rows, channels = query_ref.shape
    heads = channels // HEAD_DIM
    scale = HEAD_DIM**-0.5
    lane = lax.broadcasted_iota(jnp.int32, (1, 3 * rows), 1)
    limit = jnp.zeros((1, 3 * rows), jnp.int32)
    for slot in range(3):
        a, b = offsets(index_t)[slot], offsets(index_h)[column]
        t, h = index_t + a, index_h + b
        kept = (mask_ref[index_t, index_h, 3 * (a + 1) + (b + 1)] == 1) & inside(t, counts[0]) & inside(h, counts[1])
        safe = jnp.clip(t, 0, counts[0] - 1)
        for f in range(2):
            live = jnp.where(kept, clip_ref[2 * safe + f], 0)
            limit = jnp.where(lane >= slot * rows + f * (rows // 2), live, limit)
    bias[...] = jnp.where(lax.rem(lane, width) < limit, 0.0, -jnp.inf)
    which = lax.broadcasted_iota(jnp.int32, (rows, HEAD_DIM), 1)

    def body(step, _):
        hs = [step * UNROLL + u for u in range(UNROLL)]
        for h in hs:
            cols = head_columns(h)
            keys = jnp.concatenate([ref[0, :, cols] for ref in slots], axis=0)
            values = jnp.concatenate([ref[1, :, cols] for ref in slots], axis=0)
            s = dot_last(query_ref[:, cols], keys) * (scale * LOG2E) + bias[...]
            top = jnp.maximum(jnp.max(s, axis=1, keepdims=True), FLOOR)
            e = jnp.exp2(s - top)
            total = jnp.sum(e, axis=1, keepdims=True)
            e = e.astype(jnp.bfloat16)
            exp_ref[h] = e
            acc = dot(e, values)
            top = jnp.broadcast_to(top, (rows, HEAD_DIM))
            total = jnp.broadcast_to(total, (rows, HEAD_DIM))
            if not last:
                sum_ref[:, cols], top_ref[:, cols], total_ref[:, cols] = acc, top, total
                continue
            near_top, own_top = tops[1][:, cols], tops[0][:, cols]
            row_max = jnp.maximum(jnp.maximum(own_top, near_top), top)
            row_total = total * jnp.exp2(top - row_max) + totals[0][:, cols] * jnp.exp2(own_top - row_max)
            row_total = row_total + totals[1][:, cols] * jnp.exp2(near_top - row_max)
            log_total = row_max + jnp.log2(row_total)
            factors = [jnp.exp2(x - log_total) for x in (own_top, near_top, top)]
            for ref, factor in zip((fac_own, fac_near, fac_far), factors):
                ref[:, cols] = factor
            attention = sums[0][:, cols] * factors[0] + sums[1][:, cols] * factors[1] + acc * factors[2]
            att_ref[:, cols] = attention
            delta = jnp.sum(grad_ref[:, cols].astype(jnp.float32) * attention, axis=1, keepdims=True)
            delta = jnp.broadcast_to(delta, (rows, HEAD_DIM))
            delta_ref[:, cols] = delta
            marked = jnp.where(which == h, log_total, stat[...])
            stat[...] = jnp.where(which == h + ROW_DELTA, delta, marked)
        return 0

    if last:
        stat[...] = jnp.zeros_like(stat)
    lax.fori_loop(0, heads // UNROLL, body, 0)
    if last:
        pad = jnp.zeros((-rows % HEAD_DIM, HEAD_DIM), jnp.float32)
        turned = jnp.concatenate([stat[...], pad], axis=0).T
        stat_ref[...] = turned[:STAT_ROWS, :rows]


def query_kernel(counts, width, grad_ref, weight_ref, *rest):
    slots, exps, factors = rest[:9], rest[9:12], rest[12:15]
    att_ref, delta_ref, _, _, out_ref, dq_ref, done_ref = rest[15:]
    done_ref[...] = jnp.zeros_like(done_ref)
    _, _, place_now = place(counts)
    rows, channels = grad_ref.shape
    heads = channels // HEAD_DIM
    scale = HEAD_DIM**-0.5
    wide = -(-3 * rows // HEAD_DIM)

    def body(step, _):
        for u in range(UNROLL):
            h = step * UNROLL + u
            cols = head_columns(h)
            grad = grad_ref[:, cols]
            delta = jnp.concatenate([delta_ref[:, cols]] * wide, axis=1)[:, : 3 * rows]
            dq = None
            for column in range(3):
                refs = slots[column::3]
                values = jnp.concatenate([ref[1, :, cols] for ref in refs], axis=0)
                keys = jnp.concatenate([ref[0, :, cols] for ref in refs], axis=0)
                ds = exps[column][h].astype(jnp.float32) * (dot_last(grad, values) - delta)
                part = dot(ds.astype(jnp.bfloat16), keys) * (factors[column][:, cols] * scale)
                dq = part if dq is None else dq + part
            dq_ref[:, cols] = dq.astype(jnp.bfloat16)
            slab = halo_slab(lambda slot: slots[slot][1, :, cols], place_now, width)
            conv = depthwise(slab, weight_ref[:, cols].astype(jnp.float32), False, width)
            out_ref[:, cols] = (att_ref[:, cols] + conv).astype(jnp.bfloat16)
        return 0

    lax.fori_loop(0, heads // UNROLL, body, 0)


def pack_kernel(rows, qg_ref, own_ref, near_ref, far_ref, *rest):
    out_ref = rest[-1]
    out_ref[:rows] = qg_ref[0]
    out_ref[rows : 2 * rows] = qg_ref[1]
    first = 2 * rows
    out_ref[first:] = jnp.zeros(out_ref[first:].shape, jnp.bfloat16)
    for i, ref in enumerate((own_ref, near_ref, far_ref)):
        left = ref[...]
        for part in range(3):
            high = left.astype(jnp.bfloat16)
            out_ref[first + part * STAT_ROWS : first + (part + 1) * STAT_ROWS, i * STAT_LANES : i * STAT_LANES + rows] = high
            left = left - high.astype(jnp.float32)


def key_kernel(counts, width, slot_t, mask_ref, clip_ref, own, own_ref, near_ref, far_ref, *rest):
    first, last = slot_t == 0, slot_t == 2
    index_t, index_h, place_now = place(counts)
    rows, channels = own.shape[1:]
    heads = channels // HEAD_DIM
    scale = HEAD_DIM**-0.5

    def packed(ref, what, cols):
        return ref[what * rows : (what + 1) * rows, cols] if len(ref.shape) == 2 else ref[what, :, cols]

    if first:
        *stat_refs, dk_ref, dv_ref, stats = rest
        pieces = [ref[...] for ref in stat_refs]
    else:
        dk_sum, dv_sum, *edges, dk_ref, dv_ref, stats = rest
        pieces = []
        for i in range(3):
            parts = []
            for part in range(3):
                start = 2 * rows + part * STAT_ROWS
                parts.append(far_ref[start : start + STAT_ROWS, i * STAT_LANES : i * STAT_LANES + rows].astype(jnp.float32))
            pieces.append(parts[0] + (parts[1] + parts[2]))
    line = lax.broadcasted_iota(jnp.int32, (STAT_ROWS, rows), 0)
    for column in range(3):
        a, b = offsets(index_t)[slot_t], offsets(index_h)[column]
        t, h = index_t + a, index_h + b
        safe_t, safe_h = jnp.clip(t, 0, counts[0] - 1), jnp.clip(h, 0, counts[1] - 1)
        kept = (mask_ref[safe_t, safe_h, 3 * (1 - a) + (1 - b)] == 1) & inside(t, counts[0]) & inside(h, counts[1])
        pieces[column] = jnp.where(kept | (line >= ROW_DELTA), pieces[column], jnp.inf)
    stats[...] = jnp.concatenate(pieces, axis=1)
    row = lax.broadcasted_iota(jnp.int32, (rows, HEAD_DIM), 0)
    lens = [clip_ref[2 * index_t + f] for f in range(2)]
    live = lax.rem(row, width) < jnp.where(row < 2 * width, lens[0], lens[1])

    def body(step, _):
        for u in range(UNROLL):
            head = step * UNROLL + u
            cols = head_columns(head)
            queries = jnp.concatenate([packed(ref, 0, cols) for ref in (own_ref, near_ref, far_ref)], axis=0)
            grads = jnp.concatenate([packed(ref, 1, cols) for ref in (own_ref, near_ref, far_ref)], axis=0)
            s = dot_last(own[0, :, cols], queries)
            p = jnp.exp2(s * (scale * LOG2E) - stats[pl.ds(head, 1), :])
            dp = dot_last(own[1, :, cols], grads)
            ds = (p * (dp - stats[pl.ds(head + ROW_DELTA, 1), :])).astype(jnp.bfloat16)
            dv = dot(p.astype(jnp.bfloat16), grads)
            dk = dot(ds, queries)
            if not first:
                dk, dv = dk + dk_sum[:, cols], dv + dv_sum[:, cols]
            if not last:
                dk_ref[:, cols], dv_ref[:, cols] = dk, dv
                continue
            dk_ref[:, cols] = jnp.where(live, dk * scale, 0.0).astype(jnp.bfloat16)
            around = (*edges[1:], own_ref, near_ref, far_ref)
            slab = halo_slab(lambda slot: packed(around[slot], 1, cols), place_now, width)
            conv = depthwise(slab, edges[0][:, cols].astype(jnp.float32), True, width)
            dv_ref[:, cols] = (jnp.where(live, dv, 0.0) + conv).astype(jnp.bfloat16)
        return 0

    lax.fori_loop(0, heads // UNROLL, body, 0)


def cost(heads, rows, matmuls, columns):
    work = heads * rows * 3 * columns * rows * HEAD_DIM * 2 * matmuls
    moved = heads * rows * HEAD_DIM * 2 * 8 * columns
    return pl.CostEstimate(flops=work, bytes_accessed=moved, transcendentals=heads * rows * rows * 3 * columns)


def shards(query_states, key_states, value_states, conv_weight, out_grad, tile_mask, clip_lengths):
    width, channels = query_states.shape[2:]
    rows = query_states.shape[0] * query_states.shape[1] * width
    counts = (lax.axis_size("ta"), lax.axis_size("ha"))
    heads = channels // HEAD_DIM
    query, key, value, grad = [x.reshape(rows, channels) for x in (query_states, key_states, value_states, out_grad)]

    smem = pl.BlockSpec(memory_space=pltpu.SMEM)
    vmem = pl.BlockSpec(memory_space=pltpu.VMEM)
    params = pltpu.CompilerParams(vmem_limit_bytes=LARGE)
    half = jax.ShapeDtypeStruct((rows, channels), jnp.bfloat16)
    full = jax.ShapeDtypeStruct((rows, channels), jnp.float32)
    exps = jax.ShapeDtypeStruct((heads, rows, 3 * rows), jnp.bfloat16)
    bias = pltpu.VMEM((1, 3 * rows), jnp.float32)

    def call(kernel, name, out_shape, scratch, work, *args):
        scalars = 2 if args[0] is tile_mask else 0
        return pl.pallas_call(
            kernel,
            in_specs=[smem] * scalars + [vmem] * (len(args) - scalars),
            out_specs=[vmem] * len(out_shape),
            out_shape=out_shape,
            scratch_shapes=scratch,
            compiler_params=params,
            cost_estimate=work,
            name=name,
        )(*args)

    def scores(column, tiles):
        kernel = functools.partial(column_kernel, counts, width, column, False)
        work = cost(heads, rows, 2, 1)
        return call(kernel, f"scores_{column}", [exps, full, full, full], [bias], work, tile_mask, clip_lengths, query, *tiles)

    def later(x, *earlier):
        def kernel(x_ref, *rest):
            rest[-1][...] = x_ref[...]

        return pl.pallas_call(
            kernel,
            in_specs=[vmem] + [pl.BlockSpec(memory_space=pl.ANY)] * len(earlier),
            out_specs=vmem,
            out_shape=jax.ShapeDtypeStruct(x.shape, x.dtype),
            compiler_params=pltpu.CompilerParams(vmem_limit_bytes=SMALL),
            name="later",
        )(x, *earlier)

    def pair_up(x, y, *earlier):
        def kernel(x_ref, y_ref, *rest):
            rest[-1][0] = x_ref[...]
            rest[-1][1] = y_ref[...]

        return pl.pallas_call(
            kernel,
            in_specs=[vmem] * 2 + [pl.BlockSpec(memory_space=pl.ANY)] * len(earlier),
            out_specs=vmem,
            out_shape=jax.ShapeDtypeStruct((2,) + x.shape, x.dtype),
            compiler_params=pltpu.CompilerParams(vmem_limit_bytes=SMALL),
            name="pair_up",
        )(x, y, *earlier)

    def gate(x, *earlier):
        return pl.pallas_call(
            lambda *refs: None,
            in_specs=[pl.BlockSpec(memory_space=pl.ANY)] * (1 + len(earlier)),
            out_specs=pl.BlockSpec(memory_space=pl.ANY),
            out_shape=jax.ShapeDtypeStruct(x.shape, x.dtype),
            input_output_aliases={0: 0},
            compiler_params=pltpu.CompilerParams(vmem_limit_bytes=SMALL),
            name="gate",
        )(x, *earlier)

    near_k = ha_near(key)
    kv = jnp.stack([key, value])
    kv_a, kv_b = ta_pair(kv), ta_other(kv)
    qg = pair_up(query, grad, kv_a)
    qg_a, qg_b = ta_pair(qg), ta_other(qg)
    near_v = ha_near(later(value, near_k))
    far_k = ha_relay(near_k)
    exp_own, *own_parts = scores(0, (kv, kv_a, kv_b))

    near_v = gate(near_v, own_parts[0])
    far_v = ha_relay(near_v)
    near_kv = pair_up(near_k, near_v, qg_a, qg_b, far_k)
    near_kv_a, near_kv_b = ta_pair(near_kv), ta_other(near_kv)
    near_qg = ha_near(pair_up(query, grad, near_v))
    far_kv = jnp.stack([far_k, far_v])
    far_kv_a, far_kv_b = ta_pair(far_kv), ta_other(far_kv)
    exp_near, *near_parts = scores(1, (near_kv, near_kv_a, near_kv_b))

    near_qg = gate(near_qg, near_parts[0])
    far_qg = ha_relay(near_qg)
    near_qg_a, near_qg_b = ta_pair(near_qg), ta_other(near_qg)
    exp_far, attention, fac_own, fac_near, fac_far, delta, stat = call(
        functools.partial(column_kernel, counts, width, 2, True),
        "scores_2",
        [exps] + [full] * 5 + [jax.ShapeDtypeStruct((STAT_ROWS, rows), jnp.float32)],
        [bias, pltpu.VMEM((rows, HEAD_DIM), jnp.float32)],
        cost(heads, rows, 2, 1),
        tile_mask, clip_lengths, query, far_kv, far_kv_a, far_kv_b, grad, *own_parts, *near_parts,
    )
    near_stat, far_stat = ha_near(stat), ha_far(stat)
    layer_out, query_grad, done = call(
        functools.partial(query_kernel, counts, width),
        "query_side",
        [half, half, jax.ShapeDtypeStruct((8, HEAD_DIM), jnp.float32)],
        [],
        cost(heads, rows, 2, 3),
        grad, conv_weight, kv, near_kv, far_kv, kv_a, near_kv_a, far_kv_a, kv_b, near_kv_b, far_kv_b,
        exp_own, exp_near, exp_far, fac_own, fac_near, fac_far, attention, delta, near_stat, far_stat,
    )
    message = pl.pallas_call(
        functools.partial(pack_kernel, rows),
        in_specs=[vmem] * 4 + [pl.BlockSpec(memory_space=pl.ANY)] * 3,
        out_specs=vmem,
        out_shape=jax.ShapeDtypeStruct((2 * rows + 3 * STAT_ROWS, channels), jnp.bfloat16),
        compiler_params=pltpu.CompilerParams(vmem_limit_bytes=SMALL),
        name="pack",
    )(far_qg, stat, near_stat, far_stat, done, near_qg_a, near_qg_b)
    message_a, message_b = ta_pair(message), ta_other(message)

    scratch = [pltpu.VMEM((STAT_ROWS, 3 * rows), jnp.float32)]
    work = cost(heads, rows, 4, 1)
    sums = call(
        functools.partial(key_kernel, counts, width, 0), "key_side_0", [full, full], scratch, work,
        tile_mask, clip_lengths, kv, qg, near_qg, far_qg, stat, near_stat, far_stat,
    )
    sums = call(
        functools.partial(key_kernel, counts, width, 1), "key_side_1", [full, full], scratch, work,
        tile_mask, clip_lengths, kv, qg_a, near_qg_a, message_a, *sums,
    )
    key_grad, value_grad = call(
        functools.partial(key_kernel, counts, width, 2), "key_side_2", [half, half], scratch, work,
        tile_mask, clip_lengths, kv, qg_b, near_qg_b, message_b, *sums,
        conv_weight, qg, near_qg, far_qg, qg_a, near_qg_a, message_a,
    )
    return tuple(x.reshape(query_states.shape) for x in (layer_out, query_grad, key_grad, value_grad))


def solution(mesh):
    placed = P("ta", "ha", None, None)
    return jax.shard_map(
        shards,
        mesh=mesh,
        in_specs=(placed, placed, placed, P(), placed, P(), P()),
        out_specs=(placed,) * 4,
        check_vma=False,
    )
```

```python
import functools

import jax
import jax.numpy as jnp
from jax import lax
from jax.experimental import pallas as pl
from jax.experimental.pallas import tpu as pltpu
from jax.sharding import PartitionSpec as P

HEAD_DIM = 128
LOG2E = 1.4426950408889634
ROW_DELTA = 8
STAT_ROWS = 16
STAT_LANES = 256
UNROLL = 2
FLOOR = -1e30
SMALL = 2 * 1024 * 1024
LARGE = 8 * 1024 * 1024


CONTRACT_LAST = (((1,), (1,)), ((), ()))


def flip_pairs(count):
    return [(i, i ^ 1) for i in range(count)]


def other_pairs(count):
    pairs = []
    for i in range(count):
        to = i + 1 if i % 2 else i - 1
        pairs.append((i, to if 0 <= to < count else i))
    return pairs


def relay_pairs(count):
    pairs = []
    for i in range(count):
        to = i - 2 if i % 2 else i + 2
        if 0 <= to < count:
            pairs.append((i, to))
    return pairs


def ha_near(x):
    return lax.ppermute(x, "ha", flip_pairs(lax.axis_size("ha")))


def ha_relay(near):
    return lax.ppermute(near, "ha", relay_pairs(lax.axis_size("ha")))


def ha_far(x):
    return lax.ppermute(x, "ha", other_pairs(lax.axis_size("ha")))


def ta_pair(x):
    return lax.ppermute(x, "ta", flip_pairs(lax.axis_size("ta")))


def ta_other(x):
    return lax.ppermute(x, "ta", other_pairs(lax.axis_size("ta")))


def offsets(index):
    sign = 1 - 2 * lax.rem(index, 2)
    return (0, sign, -sign)


def inside(index, count):
    return (index >= 0) & (index < count)


def row_of(tile, frame, row, width):
    start = (2 * frame + row) * width
    return tile[start : start + width]


def shifted_sum(parts, width):
    column = lax.broadcasted_iota(jnp.int32, (width, HEAD_DIM), 0)
    before = jnp.where(column == 0, 0.0, pltpu.roll(parts[0], 1, 0))
    behind = jnp.where(column == width - 1, 0.0, pltpu.roll(parts[2], width - 1, 0))
    return parts[1] + before + behind


def total_of(terms):
    return functools.reduce(lambda x, y: x + y, terms)


def along_t(own, pair, other, place_now):
    even_t, _, in_t, _ = place_now
    ahead = jnp.where(in_t[0], jnp.where(even_t, other(1), pair(1)), 0.0)
    behind = jnp.where(in_t[1], jnp.where(even_t, pair(0), other(0)), 0.0)
    return [ahead, own(0), own(1), behind]


def conv_inner(tiles, weight, flipped, place_now, width):
    _, even_h, _, in_h = place_now
    tiles = [[x.astype(jnp.float32) for x in pair] for pair in tiles]

    def cell(slot, R):
        if R in (1, 2):
            return lambda frame: row_of(tiles[slot][0], frame, R - 1, width)
        if R == 0:
            return lambda frame: jnp.where(even_h | ~in_h[0], 0.0, row_of(tiles[slot][1], frame, 1, width))
        return lambda frame: jnp.where(even_h & in_h[1], row_of(tiles[slot][1], frame, 0, width), 0.0)

    slab = [along_t(cell(0, R), cell(1, R), cell(2, R), place_now) for R in range(4)]
    rows = []
    for f in range(2):
        for r in range(2):
            parts = []
            for dw in range(3):
                taps = [(dt, dh, 9 * dt + 3 * dh + dw) for dt in range(3) for dh in range(3)]
                taps = [(dt, dh, 26 - tap if flipped else tap) for dt, dh, tap in taps]
                parts.append(total_of([weight[tap : tap + 1] * slab[r + dh][f + dt] for dt, dh, tap in taps]))
            rows.append(shifted_sum(parts, width))
    return jnp.concatenate(rows, axis=0)


def conv_far(tiles, weight, flipped, place_now, width):
    _, even_h, _, in_h = place_now
    tiles = [x.astype(jnp.float32) for x in tiles]
    there = (even_h & in_h[0]) | (~even_h & in_h[1])

    def cell(slot):
        def of(frame):
            row = jnp.where(even_h, row_of(tiles[slot], frame, 1, width), row_of(tiles[slot], frame, 0, width))
            return jnp.where(there, row, 0.0)

        return of

    line = along_t(cell(0), cell(1), cell(2), place_now)
    rows = []
    for f in range(2):
        parts = []
        for dw in range(3):
            terms = []
            for dt in range(3):
                up, down = 9 * dt + dw, 9 * dt + 6 + dw
                if flipped:
                    up, down = 26 - up, 26 - down
                tap = jnp.where(even_h, weight[up : up + 1], weight[down : down + 1])
                terms.append(tap * line[f + dt])
            parts.append(total_of(terms))
        beside = shifted_sum(parts, width)
        rows += [jnp.where(even_h, beside, 0.0), jnp.where(even_h, 0.0, beside)]
    return jnp.concatenate(rows, axis=0)


def place(counts):
    index_t, index_h = lax.axis_index("ta"), lax.axis_index("ha")
    even_t, even_h = lax.rem(index_t, 2) == 0, lax.rem(index_h, 2) == 0
    in_t = (index_t > 0, index_t < counts[0] - 1)
    in_h = (index_h > 0, index_h < counts[1] - 1)
    return index_t, index_h, (even_t, even_h, in_t, in_h)


def head_columns(head):
    return pl.ds(pl.multiple_of(head * HEAD_DIM, HEAD_DIM), HEAD_DIM)


def dot_last(x, y):
    return lax.dot_general(x, y, CONTRACT_LAST, preferred_element_type=jnp.float32)


def dot(x, y):
    return jnp.dot(x, y, preferred_element_type=jnp.float32)


def column_kernel(counts, width, column, last, mask_ref, clip_ref, query_ref, own, pair, other, *rest):
    slots = [own, pair, other]
    if last:
        grad_ref, sums, tops, totals = rest[0], (rest[1], rest[4]), (rest[2], rest[5]), (rest[3], rest[6])
        exp_ref, att_ref, fac_own, fac_near, fac_far, delta_ref, stat_ref, bias, stat = rest[8:]
    else:
        exp_ref, sum_ref, top_ref, total_ref, bias = rest
    index_t, index_h, _ = place(counts)
    rows, channels = query_ref.shape
    heads = channels // HEAD_DIM
    scale = HEAD_DIM**-0.5
    lane = lax.broadcasted_iota(jnp.int32, (1, 3 * rows), 1)
    limit = jnp.zeros((1, 3 * rows), jnp.int32)
    for slot in range(3):
        a, b = offsets(index_t)[slot], offsets(index_h)[column]
        t, h = index_t + a, index_h + b
        kept = (mask_ref[index_t, index_h, 3 * (a + 1) + (b + 1)] == 1) & inside(t, counts[0]) & inside(h, counts[1])
        safe = jnp.clip(t, 0, counts[0] - 1)
        for f in range(2):
            live = jnp.where(kept, clip_ref[2 * safe + f], 0)
            limit = jnp.where(lane >= slot * rows + f * (rows // 2), live, limit)
    bias[...] = jnp.where(lax.rem(lane, width) < limit, 0.0, -jnp.inf)
    which = lax.broadcasted_iota(jnp.int32, (rows, HEAD_DIM), 1)

    def body(step, _):
        hs = [step * UNROLL + u for u in range(UNROLL)]
        for h in hs:
            cols = head_columns(h)
            keys = jnp.concatenate([ref[0, :, cols] for ref in slots], axis=0)
            values = jnp.concatenate([ref[1, :, cols] for ref in slots], axis=0)
            s = dot_last(query_ref[:, cols], keys) * (scale * LOG2E) + bias[...]
            top = jnp.maximum(jnp.max(s, axis=1, keepdims=True), FLOOR)
            e = jnp.exp2(s - top)
            total = jnp.sum(e, axis=1, keepdims=True)
            e = e.astype(jnp.bfloat16)
            exp_ref[h] = e
            acc = dot(e, values)
            top = jnp.broadcast_to(top, (rows, HEAD_DIM))
            total = jnp.broadcast_to(total, (rows, HEAD_DIM))
            if not last:
                sum_ref[:, cols], top_ref[:, cols], total_ref[:, cols] = acc, top, total
                continue
            near_top, own_top = tops[1][:, cols], tops[0][:, cols]
            row_max = jnp.maximum(jnp.maximum(own_top, near_top), top)
            row_total = total * jnp.exp2(top - row_max) + totals[0][:, cols] * jnp.exp2(own_top - row_max)
            row_total = row_total + totals[1][:, cols] * jnp.exp2(near_top - row_max)
            log_total = row_max + jnp.log2(row_total)
            factors = [jnp.exp2(x - log_total) for x in (own_top, near_top, top)]
            for ref, factor in zip((fac_own, fac_near, fac_far), factors):
                ref[:, cols] = factor
            attention = sums[0][:, cols] * factors[0] + sums[1][:, cols] * factors[1] + acc * factors[2]
            att_ref[:, cols] = attention
            delta = jnp.sum(grad_ref[:, cols].astype(jnp.float32) * attention, axis=1, keepdims=True)
            delta = jnp.broadcast_to(delta, (rows, HEAD_DIM))
            delta_ref[:, cols] = delta
            marked = jnp.where(which == h, log_total, stat[...])
            stat[...] = jnp.where(which == h + ROW_DELTA, delta, marked)
        return 0

    if last:
        stat[...] = jnp.zeros_like(stat)
    lax.fori_loop(0, heads // UNROLL, body, 0)
    if last:
        pad = jnp.zeros((-rows % HEAD_DIM, HEAD_DIM), jnp.float32)
        turned = jnp.concatenate([stat[...], pad], axis=0).T
        stat_ref[...] = turned[:STAT_ROWS, :rows]


def conv_kernel(counts, width, flipped, own, near, pair, near_pair, other, near_other, weight_ref, out_ref):
    _, _, place_now = place(counts)
    rows, channels = out_ref.shape

    def body(head, _):
        cols = head_columns(head)
        tiles = [(x[1, :, cols], y[1, :, cols]) for x, y in ((own, near), (pair, near_pair), (other, near_other))]
        out_ref[:, cols] = conv_inner(tiles, weight_ref[:, cols].astype(jnp.float32), flipped, place_now, width)
        return 0

    lax.fori_loop(0, channels // HEAD_DIM, body, 0)


def query_kernel(counts, width, grad_ref, weight_ref, *rest):
    slots, exps, factors = rest[:9], rest[9:12], rest[12:15]
    att_ref, delta_ref, conv_ref, out_ref, dq_ref, done_ref = rest[15:]
    done_ref[...] = jnp.zeros_like(done_ref)
    _, _, place_now = place(counts)
    rows, channels = grad_ref.shape
    heads = channels // HEAD_DIM
    scale = HEAD_DIM**-0.5
    wide = -(-3 * rows // HEAD_DIM)

    def body(step, _):
        for u in range(UNROLL):
            h = step * UNROLL + u
            cols = head_columns(h)
            grad = grad_ref[:, cols]
            delta = jnp.concatenate([delta_ref[:, cols]] * wide, axis=1)[:, : 3 * rows]
            dq = None
            for column in range(3):
                refs = slots[column::3]
                values = jnp.concatenate([ref[1, :, cols] for ref in refs], axis=0)
                keys = jnp.concatenate([ref[0, :, cols] for ref in refs], axis=0)
                ds = exps[column][h].astype(jnp.float32) * (dot_last(grad, values) - delta)
                part = dot(ds.astype(jnp.bfloat16), keys) * (factors[column][:, cols] * scale)
                dq = part if dq is None else dq + part
            dq_ref[:, cols] = dq.astype(jnp.bfloat16)
            tiles = [slots[i][1, :, cols] for i in (2, 5, 8)]
            conv = conv_ref[:, cols] + conv_far(tiles, weight_ref[:, cols].astype(jnp.float32), False, place_now, width)
            out_ref[:, cols] = (att_ref[:, cols] + conv).astype(jnp.bfloat16)
        return 0

    lax.fori_loop(0, heads // UNROLL, body, 0)


def pack_kernel(rows, qg_ref, own_ref, near_ref, far_ref, *rest):
    out_ref = rest[-1]
    out_ref[:rows] = qg_ref[0]
    out_ref[rows : 2 * rows] = qg_ref[1]
    first = 2 * rows
    out_ref[first:] = jnp.zeros(out_ref[first:].shape, jnp.bfloat16)
    for i, ref in enumerate((own_ref, near_ref, far_ref)):
        left = ref[...]
        for part in range(3):
            high = left.astype(jnp.bfloat16)
            out_ref[first + part * STAT_ROWS : first + (part + 1) * STAT_ROWS, i * STAT_LANES : i * STAT_LANES + rows] = high
            left = left - high.astype(jnp.float32)


def key_kernel(counts, width, slot_t, mask_ref, clip_ref, own, own_ref, near_ref, far_ref, *rest):
    first, last = slot_t == 0, slot_t == 2
    index_t, index_h, place_now = place(counts)
    rows, channels = own.shape[1:]
    heads = channels // HEAD_DIM
    scale = HEAD_DIM**-0.5

    def packed(ref, what, cols):
        return ref[what * rows : (what + 1) * rows, cols] if len(ref.shape) == 2 else ref[what, :, cols]

    if first:
        *stat_refs, dk_ref, dv_ref, stats = rest
        pieces = [ref[...] for ref in stat_refs]
    else:
        dk_sum, dv_sum, *edges, dk_ref, dv_ref, stats = rest
        pieces = []
        for i in range(3):
            parts = []
            for part in range(3):
                start = 2 * rows + part * STAT_ROWS
                parts.append(far_ref[start : start + STAT_ROWS, i * STAT_LANES : i * STAT_LANES + rows].astype(jnp.float32))
            pieces.append(parts[0] + (parts[1] + parts[2]))
    line = lax.broadcasted_iota(jnp.int32, (STAT_ROWS, rows), 0)
    for column in range(3):
        a, b = offsets(index_t)[slot_t], offsets(index_h)[column]
        t, h = index_t + a, index_h + b
        safe_t, safe_h = jnp.clip(t, 0, counts[0] - 1), jnp.clip(h, 0, counts[1] - 1)
        kept = (mask_ref[safe_t, safe_h, 3 * (1 - a) + (1 - b)] == 1) & inside(t, counts[0]) & inside(h, counts[1])
        pieces[column] = jnp.where(kept | (line >= ROW_DELTA), pieces[column], jnp.inf)
    stats[...] = jnp.concatenate(pieces, axis=1)
    row = lax.broadcasted_iota(jnp.int32, (rows, HEAD_DIM), 0)
    lens = [clip_ref[2 * index_t + f] for f in range(2)]
    live = lax.rem(row, width) < jnp.where(row < 2 * width, lens[0], lens[1])

    def body(step, _):
        for u in range(UNROLL):
            head = step * UNROLL + u
            cols = head_columns(head)
            queries = jnp.concatenate([packed(ref, 0, cols) for ref in (own_ref, near_ref, far_ref)], axis=0)
            grads = jnp.concatenate([packed(ref, 1, cols) for ref in (own_ref, near_ref, far_ref)], axis=0)
            s = dot_last(own[0, :, cols], queries)
            p = jnp.exp2(s * (scale * LOG2E) - stats[pl.ds(head, 1), :])
            dp = dot_last(own[1, :, cols], grads)
            ds = (p * (dp - stats[pl.ds(head + ROW_DELTA, 1), :])).astype(jnp.bfloat16)
            dv = dot(p.astype(jnp.bfloat16), grads)
            dk = dot(ds, queries)
            if not first:
                dk, dv = dk + dk_sum[:, cols], dv + dv_sum[:, cols]
            if not last:
                dk_ref[:, cols], dv_ref[:, cols] = dk, dv
                continue
            dk_ref[:, cols] = jnp.where(live, dk * scale, 0.0).astype(jnp.bfloat16)
            weight_ref, conv_ref, *far_refs = edges
            tiles = [packed(ref, 1, cols) for ref in (*far_refs, far_ref)]
            conv = conv_ref[:, cols] + conv_far(tiles, weight_ref[:, cols].astype(jnp.float32), True, place_now, width)
            dv_ref[:, cols] = (jnp.where(live, dv, 0.0) + conv).astype(jnp.bfloat16)
        return 0

    lax.fori_loop(0, heads // UNROLL, body, 0)


def cost(heads, rows, matmuls, columns):
    work = heads * rows * 3 * columns * rows * HEAD_DIM * 2 * matmuls
    moved = heads * rows * HEAD_DIM * 2 * 8 * columns
    return pl.CostEstimate(flops=work, bytes_accessed=moved, transcendentals=heads * rows * rows * 3 * columns)


def shards(query_states, key_states, value_states, conv_weight, out_grad, tile_mask, clip_lengths):
    width, channels = query_states.shape[2:]
    rows = query_states.shape[0] * query_states.shape[1] * width
    counts = (lax.axis_size("ta"), lax.axis_size("ha"))
    heads = channels // HEAD_DIM
    query, key, value, grad = [x.reshape(rows, channels) for x in (query_states, key_states, value_states, out_grad)]

    smem = pl.BlockSpec(memory_space=pltpu.SMEM)
    vmem = pl.BlockSpec(memory_space=pltpu.VMEM)
    params = pltpu.CompilerParams(vmem_limit_bytes=LARGE)
    half = jax.ShapeDtypeStruct((rows, channels), jnp.bfloat16)
    full = jax.ShapeDtypeStruct((rows, channels), jnp.float32)
    exps = jax.ShapeDtypeStruct((heads, rows, 3 * rows), jnp.bfloat16)
    bias = pltpu.VMEM((1, 3 * rows), jnp.float32)

    def call(kernel, name, out_shape, scratch, work, *args):
        scalars = 2 if args[0] is tile_mask else 0
        return pl.pallas_call(
            kernel,
            in_specs=[smem] * scalars + [vmem] * (len(args) - scalars),
            out_specs=[vmem] * len(out_shape),
            out_shape=out_shape,
            scratch_shapes=scratch,
            compiler_params=params,
            cost_estimate=work,
            name=name,
        )(*args)

    def convolution(flipped, *tiles):
        kernel = functools.partial(conv_kernel, counts, width, flipped)
        return call(kernel, "convolution", [full], [], cost(heads, rows, 1, 1), *tiles, conv_weight)[0]

    def scores(column, tiles):
        kernel = functools.partial(column_kernel, counts, width, column, False)
        work = cost(heads, rows, 2, 1)
        return call(kernel, f"scores_{column}", [exps, full, full, full], [bias], work, tile_mask, clip_lengths, query, *tiles)

    def later(x, *earlier):
        def kernel(x_ref, *rest):
            rest[-1][...] = x_ref[...]

        return pl.pallas_call(
            kernel,
            in_specs=[vmem] + [pl.BlockSpec(memory_space=pl.ANY)] * len(earlier),
            out_specs=vmem,
            out_shape=jax.ShapeDtypeStruct(x.shape, x.dtype),
            compiler_params=pltpu.CompilerParams(vmem_limit_bytes=SMALL),
            name="later",
        )(x, *earlier)

    def pair_up(x, y, *earlier):
        def kernel(x_ref, y_ref, *rest):
            rest[-1][0] = x_ref[...]
            rest[-1][1] = y_ref[...]

        return pl.pallas_call(
            kernel,
            in_specs=[vmem] * 2 + [pl.BlockSpec(memory_space=pl.ANY)] * len(earlier),
            out_specs=vmem,
            out_shape=jax.ShapeDtypeStruct((2,) + x.shape, x.dtype),
            compiler_params=pltpu.CompilerParams(vmem_limit_bytes=SMALL),
            name="pair_up",
        )(x, y, *earlier)

    def gate(x, *earlier):
        return pl.pallas_call(
            lambda *refs: None,
            in_specs=[pl.BlockSpec(memory_space=pl.ANY)] * (1 + len(earlier)),
            out_specs=pl.BlockSpec(memory_space=pl.ANY),
            out_shape=jax.ShapeDtypeStruct(x.shape, x.dtype),
            input_output_aliases={0: 0},
            compiler_params=pltpu.CompilerParams(vmem_limit_bytes=SMALL),
            name="gate",
        )(x, *earlier)

    near_k = ha_near(key)
    kv = jnp.stack([key, value])
    kv_a, kv_b = ta_pair(kv), ta_other(kv)
    qg = pair_up(query, grad, kv_a)
    qg_a, qg_b = ta_pair(qg), ta_other(qg)
    near_v = ha_near(later(value, near_k))
    far_k = ha_relay(near_k)
    exp_own, *own_parts = scores(0, (kv, kv_a, kv_b))

    far_v = ha_relay(near_v)
    near_kv = pair_up(near_k, near_v, qg_a, qg_b)
    near_kv_a, near_kv_b = ta_pair(near_kv), ta_other(near_kv)
    near_qg = ha_near(pair_up(query, grad, near_v, far_k))
    far_kv = pair_up(far_k, far_v, own_parts[0])
    far_kv_a, far_kv_b = ta_pair(far_kv), ta_other(far_kv)
    exp_near, *near_parts = scores(1, (near_kv, near_kv_a, near_kv_b))

    conv_value = convolution(False, kv, near_kv, kv_a, near_kv_a, kv_b, near_kv_b)

    near_qg = gate(near_qg, near_parts[0])
    far_qg = ha_relay(near_qg)
    near_qg_a, near_qg_b = ta_pair(near_qg), ta_other(near_qg)
    exp_far, attention, fac_own, fac_near, fac_far, delta, stat = call(
        functools.partial(column_kernel, counts, width, 2, True),
        "scores_2",
        [exps] + [full] * 5 + [jax.ShapeDtypeStruct((STAT_ROWS, rows), jnp.float32)],
        [bias, pltpu.VMEM((rows, HEAD_DIM), jnp.float32)],
        cost(heads, rows, 2, 1),
        tile_mask, clip_lengths, query, far_kv, far_kv_a, far_kv_b, grad, *own_parts, *near_parts, conv_value,
    )
    near_stat, far_stat = ha_near(stat), ha_far(stat)
    layer_out, query_grad, done = call(
        functools.partial(query_kernel, counts, width),
        "query_side",
        [half, half, jax.ShapeDtypeStruct((8, HEAD_DIM), jnp.float32)],
        [],
        cost(heads, rows, 2, 3),
        grad, conv_weight, kv, near_kv, far_kv, kv_a, near_kv_a, far_kv_a, kv_b, near_kv_b, far_kv_b,
        exp_own, exp_near, exp_far, fac_own, fac_near, fac_far, attention, delta, conv_value,
    )
    message = pl.pallas_call(
        functools.partial(pack_kernel, rows),
        in_specs=[vmem] * 4 + [pl.BlockSpec(memory_space=pl.ANY)] * 3,
        out_specs=vmem,
        out_shape=jax.ShapeDtypeStruct((2 * rows + 3 * STAT_ROWS, channels), jnp.bfloat16),
        compiler_params=pltpu.CompilerParams(vmem_limit_bytes=SMALL),
        name="pack",
    )(far_qg, stat, near_stat, far_stat, done, near_qg_a, near_qg_b)
    message_a, message_b = ta_pair(message), ta_other(message)

    conv_grad = convolution(True, qg, near_qg, qg_a, near_qg_a, qg_b, near_qg_b)
    scratch = [pltpu.VMEM((STAT_ROWS, 3 * rows), jnp.float32)]
    work = cost(heads, rows, 4, 1)
    sums = call(
        functools.partial(key_kernel, counts, width, 0), "key_side_0", [full, full], scratch, work,
        tile_mask, clip_lengths, kv, qg, near_qg, far_qg, stat, near_stat, far_stat,
    )
    sums = call(
        functools.partial(key_kernel, counts, width, 1), "key_side_1", [full, full], scratch, work,
        tile_mask, clip_lengths, kv, qg_a, near_qg_a, message_a, *sums,
    )
    key_grad, value_grad = call(
        functools.partial(key_kernel, counts, width, 2), "key_side_2", [half, half], scratch, work,
        tile_mask, clip_lengths, kv, qg_b, near_qg_b, message_b, *sums,
        conv_weight, conv_grad, far_qg, message_a,
    )
    return tuple(x.reshape(query_states.shape) for x in (layer_out, query_grad, key_grad, value_grad))


def solution(mesh):
    placed = P("ta", "ha", None, None)
    return jax.shard_map(
        shards,
        mesh=mesh,
        in_specs=(placed, placed, placed, P(), placed, P(), P()),
        out_specs=(placed,) * 4,
        check_vma=False,
    )
```

```python
import functools

import jax
import jax.numpy as jnp
from jax import lax
from jax.experimental import pallas as pl
from jax.experimental.pallas import tpu as pltpu
from jax.sharding import PartitionSpec as P

HEAD_DIM = 128
LOG2E = 1.4426950408889634
ROW_DELTA = 8
STAT_ROWS = 16
STAT_LANES = 256
UNROLL = 2
FLOOR = -1e30
SMALL = 2 * 1024 * 1024
LARGE = 8 * 1024 * 1024


CONTRACT_LAST = (((1,), (1,)), ((), ()))


def flip_pairs(count):
    return [(i, i ^ 1) for i in range(count)]


def other_pairs(count):
    pairs = []
    for i in range(count):
        to = i + 1 if i % 2 else i - 1
        pairs.append((i, to if 0 <= to < count else i))
    return pairs


def relay_pairs(count):
    pairs = []
    for i in range(count):
        to = i - 2 if i % 2 else i + 2
        if 0 <= to < count:
            pairs.append((i, to))
    return pairs


def ha_near(x):
    return lax.ppermute(x, "ha", flip_pairs(lax.axis_size("ha")))


def ha_relay(near):
    return lax.ppermute(near, "ha", relay_pairs(lax.axis_size("ha")))


def ha_far(x):
    return lax.ppermute(x, "ha", other_pairs(lax.axis_size("ha")))


def ta_pair(x):
    return lax.ppermute(x, "ta", flip_pairs(lax.axis_size("ta")))


def ta_other(x):
    return lax.ppermute(x, "ta", other_pairs(lax.axis_size("ta")))


def offsets(index):
    sign = 1 - 2 * lax.rem(index, 2)
    return (0, sign, -sign)


def inside(index, count):
    return (index >= 0) & (index < count)


def row_of(tile, frame, row, width):
    start = (2 * frame + row) * width
    return tile[start : start + width]


def shifted_sum(parts, width):
    column = lax.broadcasted_iota(jnp.int32, (width, HEAD_DIM), 0)
    before = jnp.where(column == 0, 0.0, pltpu.roll(parts[0], 1, 0))
    behind = jnp.where(column == width - 1, 0.0, pltpu.roll(parts[2], width - 1, 0))
    return parts[1] + before + behind


def total_of(terms):
    return functools.reduce(lambda x, y: x + y, terms)


def along_t(own, pair, other, place_now):
    even_t, _, in_t, _ = place_now
    ahead = jnp.where(in_t[0], jnp.where(even_t, other(1), pair(1)), 0.0)
    behind = jnp.where(in_t[1], jnp.where(even_t, pair(0), other(0)), 0.0)
    return [ahead, own(0), own(1), behind]


def conv_inner(tiles, weight, flipped, place_now, width):
    _, even_h, _, in_h = place_now
    tiles = [[x.astype(jnp.float32) for x in pair] for pair in tiles]

    def cell(slot, R):
        if R in (1, 2):
            return lambda frame: row_of(tiles[slot][0], frame, R - 1, width)
        if R == 0:
            return lambda frame: jnp.where(even_h | ~in_h[0], 0.0, row_of(tiles[slot][1], frame, 1, width))
        return lambda frame: jnp.where(even_h & in_h[1], row_of(tiles[slot][1], frame, 0, width), 0.0)

    slab = [along_t(cell(0, R), cell(1, R), cell(2, R), place_now) for R in range(4)]
    rows = []
    for f in range(2):
        for r in range(2):
            parts = []
            for dw in range(3):
                taps = [(dt, dh, 9 * dt + 3 * dh + dw) for dt in range(3) for dh in range(3)]
                taps = [(dt, dh, 26 - tap if flipped else tap) for dt, dh, tap in taps]
                parts.append(total_of([weight[tap : tap + 1] * slab[r + dh][f + dt] for dt, dh, tap in taps]))
            rows.append(shifted_sum(parts, width))
    return jnp.concatenate(rows, axis=0)


def conv_far(tiles, weight, flipped, place_now, width):
    _, even_h, _, in_h = place_now
    tiles = [x.astype(jnp.float32) for x in tiles]
    there = (even_h & in_h[0]) | (~even_h & in_h[1])

    def cell(slot):
        def of(frame):
            row = jnp.where(even_h, row_of(tiles[slot], frame, 1, width), row_of(tiles[slot], frame, 0, width))
            return jnp.where(there, row, 0.0)

        return of

    line = along_t(cell(0), cell(1), cell(2), place_now)
    rows = []
    for f in range(2):
        parts = []
        for dw in range(3):
            terms = []
            for dt in range(3):
                up, down = 9 * dt + dw, 9 * dt + 6 + dw
                if flipped:
                    up, down = 26 - up, 26 - down
                tap = jnp.where(even_h, weight[up : up + 1], weight[down : down + 1])
                terms.append(tap * line[f + dt])
            parts.append(total_of(terms))
        beside = shifted_sum(parts, width)
        rows += [jnp.where(even_h, beside, 0.0), jnp.where(even_h, 0.0, beside)]
    return jnp.concatenate(rows, axis=0)


def place(counts):
    index_t, index_h = lax.axis_index("ta"), lax.axis_index("ha")
    even_t, even_h = lax.rem(index_t, 2) == 0, lax.rem(index_h, 2) == 0
    in_t = (index_t > 0, index_t < counts[0] - 1)
    in_h = (index_h > 0, index_h < counts[1] - 1)
    return index_t, index_h, (even_t, even_h, in_t, in_h)


def head_columns(head):
    return pl.ds(pl.multiple_of(head * HEAD_DIM, HEAD_DIM), HEAD_DIM)


def dot_last(x, y):
    return lax.dot_general(x, y, CONTRACT_LAST, preferred_element_type=jnp.float32)


def dot(x, y):
    return jnp.dot(x, y, preferred_element_type=jnp.float32)


def column_kernel(counts, width, column, last, mask_ref, clip_ref, query_ref, own, pair, other, *rest):
    slots = [own, pair, other]
    if last:
        grad_ref, sums, tops, totals = rest[0], (rest[1], rest[4]), (rest[2], rest[5]), (rest[3], rest[6])
        exp_ref, att_ref, fac_own, fac_near, fac_far, delta_ref, stat_ref, bias, stat = rest[8:]
    else:
        exp_ref, sum_ref, top_ref, total_ref, bias = rest
    index_t, index_h, _ = place(counts)
    rows, channels = query_ref.shape
    heads = channels // HEAD_DIM
    scale = HEAD_DIM**-0.5
    lane = lax.broadcasted_iota(jnp.int32, (1, 3 * rows), 1)
    limit = jnp.zeros((1, 3 * rows), jnp.int32)
    for slot in range(3):
        a, b = offsets(index_t)[slot], offsets(index_h)[column]
        t, h = index_t + a, index_h + b
        kept = (mask_ref[index_t, index_h, 3 * (a + 1) + (b + 1)] == 1) & inside(t, counts[0]) & inside(h, counts[1])
        safe = jnp.clip(t, 0, counts[0] - 1)
        for f in range(2):
            live = jnp.where(kept, clip_ref[2 * safe + f], 0)
            limit = jnp.where(lane >= slot * rows + f * (rows // 2), live, limit)
    bias[...] = jnp.where(lax.rem(lane, width) < limit, 0.0, -jnp.inf)
    which = lax.broadcasted_iota(jnp.int32, (rows, HEAD_DIM), 1)

    def body(step, _):
        hs = [step * UNROLL + u for u in range(UNROLL)]
        tops_, accs, sums_ = [], [], []
        scored = []
        for h in hs:
            keys = jnp.concatenate([ref[0, :, head_columns(h)] for ref in slots], axis=0)
            s = dot_last(query_ref[:, head_columns(h)], keys) * (scale * LOG2E) + bias[...]
            scored.append(s)
            tops_.append(jnp.maximum(jnp.max(s, axis=1, keepdims=True), FLOOR))
        for u, h in enumerate(hs):
            e = jnp.exp2(scored[u] - tops_[u]).astype(jnp.bfloat16)
            exp_ref[h] = e
            values = jnp.concatenate([ref[1, :, head_columns(h)] for ref in slots], axis=0)
            both = dot(e, jnp.concatenate([values, jnp.ones_like(values)], axis=1))
            accs.append(both[:, :HEAD_DIM])
            sums_.append(both[:, HEAD_DIM:])
        for u, h in enumerate(hs):
            cols = head_columns(h)
            acc, total = accs[u], sums_[u]
            top = jnp.broadcast_to(tops_[u], (rows, HEAD_DIM))
            if not last:
                sum_ref[:, cols], top_ref[:, cols], total_ref[:, cols] = acc, top, total
                continue
            near_top, own_top = tops[1][:, cols], tops[0][:, cols]
            row_max = jnp.maximum(jnp.maximum(own_top, near_top), top)
            row_total = total * jnp.exp2(top - row_max) + totals[0][:, cols] * jnp.exp2(own_top - row_max)
            row_total = row_total + totals[1][:, cols] * jnp.exp2(near_top - row_max)
            log_total = row_max + jnp.log2(row_total)
            factors = [jnp.exp2(x - log_total) for x in (own_top, near_top, top)]
            for ref, factor in zip((fac_own, fac_near, fac_far), factors):
                ref[:, cols] = factor
            attention = sums[0][:, cols] * factors[0] + sums[1][:, cols] * factors[1] + acc * factors[2]
            att_ref[:, cols] = attention
            delta = jnp.sum(grad_ref[:, cols].astype(jnp.float32) * attention, axis=1, keepdims=True)
            delta = jnp.broadcast_to(delta, (rows, HEAD_DIM))
            delta_ref[:, cols] = delta
            marked = jnp.where(which == h, log_total, stat[...])
            stat[...] = jnp.where(which == h + ROW_DELTA, delta, marked)
        return 0

    if last:
        stat[...] = jnp.zeros_like(stat)
    lax.fori_loop(0, heads // UNROLL, body, 0)
    if last:
        pad = jnp.zeros((-rows % HEAD_DIM, HEAD_DIM), jnp.float32)
        turned = jnp.concatenate([stat[...], pad], axis=0).T
        stat_ref[...] = turned[:STAT_ROWS, :rows]


def conv_kernel(counts, width, flipped, own, near, pair, near_pair, other, near_other, weight_ref, out_ref):
    _, _, place_now = place(counts)
    rows, channels = out_ref.shape

    def body(head, _):
        cols = head_columns(head)
        tiles = [(x[1, :, cols], y[1, :, cols]) for x, y in ((own, near), (pair, near_pair), (other, near_other))]
        out_ref[:, cols] = conv_inner(tiles, weight_ref[:, cols].astype(jnp.float32), flipped, place_now, width)
        return 0

    lax.fori_loop(0, channels // HEAD_DIM, body, 0)


def query_kernel(counts, width, grad_ref, weight_ref, *rest):
    slots, exps, factors = rest[:9], rest[9:12], rest[12:15]
    att_ref, delta_ref, conv_ref, out_ref, dq_ref, done_ref = rest[15:]
    done_ref[...] = jnp.zeros_like(done_ref)
    _, _, place_now = place(counts)
    rows, channels = grad_ref.shape
    heads = channels // HEAD_DIM
    scale = HEAD_DIM**-0.5
    wide = -(-3 * rows // HEAD_DIM)

    def body(step, _):
        for u in range(UNROLL):
            h = step * UNROLL + u
            cols = head_columns(h)
            grad = grad_ref[:, cols]
            delta = jnp.concatenate([delta_ref[:, cols]] * wide, axis=1)[:, : 3 * rows]
            dq = None
            for column in range(3):
                refs = slots[column::3]
                values = jnp.concatenate([ref[1, :, cols] for ref in refs], axis=0)
                keys = jnp.concatenate([ref[0, :, cols] for ref in refs], axis=0)
                ds = exps[column][h].astype(jnp.float32) * (dot_last(grad, values) - delta)
                part = dot(ds.astype(jnp.bfloat16), keys) * (factors[column][:, cols] * scale)
                dq = part if dq is None else dq + part
            dq_ref[:, cols] = dq.astype(jnp.bfloat16)
            tiles = [slots[i][1, :, cols] for i in (2, 5, 8)]
            conv = conv_ref[:, cols] + conv_far(tiles, weight_ref[:, cols].astype(jnp.float32), False, place_now, width)
            out_ref[:, cols] = (att_ref[:, cols] + conv).astype(jnp.bfloat16)
        return 0

    lax.fori_loop(0, heads // UNROLL, body, 0)


def pack_kernel(rows, qg_ref, own_ref, near_ref, far_ref, *rest):
    out_ref = rest[-1]
    out_ref[:rows] = qg_ref[0]
    out_ref[rows : 2 * rows] = qg_ref[1]
    first = 2 * rows
    out_ref[first:] = jnp.zeros(out_ref[first:].shape, jnp.bfloat16)
    for i, ref in enumerate((own_ref, near_ref, far_ref)):
        left = ref[...]
        for part in range(3):
            high = left.astype(jnp.bfloat16)
            out_ref[first + part * STAT_ROWS : first + (part + 1) * STAT_ROWS, i * STAT_LANES : i * STAT_LANES + rows] = high
            left = left - high.astype(jnp.float32)


def key_kernel(counts, width, slot_t, mask_ref, clip_ref, own, own_ref, near_ref, far_ref, *rest):
    first, last = slot_t == 0, slot_t == 2
    index_t, index_h, place_now = place(counts)
    rows, channels = own.shape[1:]
    heads = channels // HEAD_DIM
    scale = HEAD_DIM**-0.5

    def packed(ref, what, cols):
        return ref[what * rows : (what + 1) * rows, cols] if len(ref.shape) == 2 else ref[what, :, cols]

    if first:
        *stat_refs, dk_ref, dv_ref, stats = rest
        pieces = [ref[...] for ref in stat_refs]
    else:
        dk_sum, dv_sum, *edges, dk_ref, dv_ref, stats = rest
        pieces = []
        for i in range(3):
            parts = []
            for part in range(3):
                start = 2 * rows + part * STAT_ROWS
                parts.append(far_ref[start : start + STAT_ROWS, i * STAT_LANES : i * STAT_LANES + rows].astype(jnp.float32))
            pieces.append(parts[0] + (parts[1] + parts[2]))
    line = lax.broadcasted_iota(jnp.int32, (STAT_ROWS, rows), 0)
    for column in range(3):
        a, b = offsets(index_t)[slot_t], offsets(index_h)[column]
        t, h = index_t + a, index_h + b
        safe_t, safe_h = jnp.clip(t, 0, counts[0] - 1), jnp.clip(h, 0, counts[1] - 1)
        kept = (mask_ref[safe_t, safe_h, 3 * (1 - a) + (1 - b)] == 1) & inside(t, counts[0]) & inside(h, counts[1])
        pieces[column] = jnp.where(kept | (line >= ROW_DELTA), pieces[column], jnp.inf)
    stats[...] = jnp.concatenate(pieces, axis=1)
    row = lax.broadcasted_iota(jnp.int32, (rows, HEAD_DIM), 0)
    lens = [clip_ref[2 * index_t + f] for f in range(2)]
    live = lax.rem(row, width) < jnp.where(row < 2 * width, lens[0], lens[1])

    def body(step, _):
        for u in range(UNROLL):
            head = step * UNROLL + u
            cols = head_columns(head)
            queries = jnp.concatenate([packed(ref, 0, cols) for ref in (own_ref, near_ref, far_ref)], axis=0)
            grads = jnp.concatenate([packed(ref, 1, cols) for ref in (own_ref, near_ref, far_ref)], axis=0)
            s = dot_last(own[0, :, cols], queries)
            p = jnp.exp2(s * (scale * LOG2E) - stats[pl.ds(head, 1), :])
            dp = dot_last(own[1, :, cols], grads)
            ds = (p * (dp - stats[pl.ds(head + ROW_DELTA, 1), :])).astype(jnp.bfloat16)
            dv = dot(p.astype(jnp.bfloat16), grads)
            dk = dot(ds, queries)
            if not first:
                dk, dv = dk + dk_sum[:, cols], dv + dv_sum[:, cols]
            if not last:
                dk_ref[:, cols], dv_ref[:, cols] = dk, dv
                continue
            dk_ref[:, cols] = jnp.where(live, dk * scale, 0.0).astype(jnp.bfloat16)
            weight_ref, conv_ref, *far_refs = edges
            tiles = [packed(ref, 1, cols) for ref in (*far_refs, far_ref)]
            conv = conv_ref[:, cols] + conv_far(tiles, weight_ref[:, cols].astype(jnp.float32), True, place_now, width)
            dv_ref[:, cols] = (jnp.where(live, dv, 0.0) + conv).astype(jnp.bfloat16)
        return 0

    lax.fori_loop(0, heads // UNROLL, body, 0)


def cost(heads, rows, matmuls, columns):
    work = heads * rows * 3 * columns * rows * HEAD_DIM * 2 * matmuls
    moved = heads * rows * HEAD_DIM * 2 * 8 * columns
    return pl.CostEstimate(flops=work, bytes_accessed=moved, transcendentals=heads * rows * rows * 3 * columns)


def shards(query_states, key_states, value_states, conv_weight, out_grad, tile_mask, clip_lengths):
    width, channels = query_states.shape[2:]
    rows = query_states.shape[0] * query_states.shape[1] * width
    counts = (lax.axis_size("ta"), lax.axis_size("ha"))
    heads = channels // HEAD_DIM
    query, key, value, grad = [x.reshape(rows, channels) for x in (query_states, key_states, value_states, out_grad)]

    smem = pl.BlockSpec(memory_space=pltpu.SMEM)
    vmem = pl.BlockSpec(memory_space=pltpu.VMEM)
    params = pltpu.CompilerParams(vmem_limit_bytes=LARGE)
    half = jax.ShapeDtypeStruct((rows, channels), jnp.bfloat16)
    full = jax.ShapeDtypeStruct((rows, channels), jnp.float32)
    exps = jax.ShapeDtypeStruct((heads, rows, 3 * rows), jnp.bfloat16)
    bias = pltpu.VMEM((1, 3 * rows), jnp.float32)

    def call(kernel, name, out_shape, scratch, work, *args):
        scalars = 2 if args[0] is tile_mask else 0
        return pl.pallas_call(
            kernel,
            in_specs=[smem] * scalars + [vmem] * (len(args) - scalars),
            out_specs=[vmem] * len(out_shape),
            out_shape=out_shape,
            scratch_shapes=scratch,
            compiler_params=params,
            cost_estimate=work,
            name=name,
        )(*args)

    def convolution(flipped, *tiles):
        kernel = functools.partial(conv_kernel, counts, width, flipped)
        return call(kernel, "convolution", [full], [], cost(heads, rows, 1, 1), *tiles, conv_weight)[0]

    def scores(column, tiles):
        kernel = functools.partial(column_kernel, counts, width, column, False)
        work = cost(heads, rows, 2, 1)
        return call(kernel, f"scores_{column}", [exps, full, full, full], [bias], work, tile_mask, clip_lengths, query, *tiles)

    def later(x, *earlier):
        def kernel(x_ref, *rest):
            rest[-1][...] = x_ref[...]

        return pl.pallas_call(
            kernel,
            in_specs=[vmem] + [pl.BlockSpec(memory_space=pl.ANY)] * len(earlier),
            out_specs=vmem,
            out_shape=jax.ShapeDtypeStruct(x.shape, x.dtype),
            compiler_params=pltpu.CompilerParams(vmem_limit_bytes=SMALL),
            name="later",
        )(x, *earlier)

    def pair_up(x, y, *earlier):
        def kernel(x_ref, y_ref, *rest):
            rest[-1][0] = x_ref[...]
            rest[-1][1] = y_ref[...]

        return pl.pallas_call(
            kernel,
            in_specs=[vmem] * 2 + [pl.BlockSpec(memory_space=pl.ANY)] * len(earlier),
            out_specs=vmem,
            out_shape=jax.ShapeDtypeStruct((2,) + x.shape, x.dtype),
            compiler_params=pltpu.CompilerParams(vmem_limit_bytes=SMALL),
            name="pair_up",
        )(x, y, *earlier)

    def gate(x, *earlier):
        return pl.pallas_call(
            lambda *refs: None,
            in_specs=[pl.BlockSpec(memory_space=pl.ANY)] * (1 + len(earlier)),
            out_specs=pl.BlockSpec(memory_space=pl.ANY),
            out_shape=jax.ShapeDtypeStruct(x.shape, x.dtype),
            input_output_aliases={0: 0},
            compiler_params=pltpu.CompilerParams(vmem_limit_bytes=SMALL),
            name="gate",
        )(x, *earlier)

    near_k = ha_near(key)
    kv = jnp.stack([key, value])
    kv_a, kv_b = ta_pair(kv), ta_other(kv)
    qg = pair_up(query, grad, kv_a)
    qg_a, qg_b = ta_pair(qg), ta_other(qg)
    near_v = ha_near(later(value, near_k))
    far_k = ha_relay(near_k)
    exp_own, *own_parts = scores(0, (kv, kv_a, kv_b))

    far_v = ha_relay(near_v)
    near_kv = pair_up(near_k, near_v, qg_a, qg_b)
    near_kv_a, near_kv_b = ta_pair(near_kv), ta_other(near_kv)
    near_qg = ha_near(pair_up(query, grad, near_v, far_k))
    exp_near, *near_parts = scores(1, (near_kv, near_kv_a, near_kv_b))
    far_kv = pair_up(far_k, far_v, own_parts[0], near_parts[0])
    far_kv_a, far_kv_b = ta_pair(far_kv), ta_other(far_kv)

    conv_value = convolution(False, kv, near_kv, kv_a, near_kv_a, kv_b, near_kv_b)

    near_qg = gate(near_qg, near_parts[0])
    far_qg = ha_relay(near_qg)
    near_qg_a, near_qg_b = ta_pair(near_qg), ta_other(near_qg)
    exp_far, attention, fac_own, fac_near, fac_far, delta, stat = call(
        functools.partial(column_kernel, counts, width, 2, True),
        "scores_2",
        [exps] + [full] * 5 + [jax.ShapeDtypeStruct((STAT_ROWS, rows), jnp.float32)],
        [bias, pltpu.VMEM((rows, HEAD_DIM), jnp.float32)],
        cost(heads, rows, 2, 1),
        tile_mask, clip_lengths, query, far_kv, far_kv_a, far_kv_b, grad, *own_parts, *near_parts, conv_value,
    )
    near_stat, far_stat = ha_near(stat), ha_far(stat)
    layer_out, query_grad, done = call(
        functools.partial(query_kernel, counts, width),
        "query_side",
        [half, half, jax.ShapeDtypeStruct((8, HEAD_DIM), jnp.float32)],
        [],
        cost(heads, rows, 2, 3),
        grad, conv_weight, kv, near_kv, far_kv, kv_a, near_kv_a, far_kv_a, kv_b, near_kv_b, far_kv_b,
        exp_own, exp_near, exp_far, fac_own, fac_near, fac_far, attention, delta, conv_value,
    )
    message = pl.pallas_call(
        functools.partial(pack_kernel, rows),
        in_specs=[vmem] * 4 + [pl.BlockSpec(memory_space=pl.ANY)] * 3,
        out_specs=vmem,
        out_shape=jax.ShapeDtypeStruct((2 * rows + 3 * STAT_ROWS, channels), jnp.bfloat16),
        compiler_params=pltpu.CompilerParams(vmem_limit_bytes=SMALL),
        name="pack",
    )(far_qg, stat, near_stat, far_stat, done, near_qg_a, near_qg_b)
    message_a, message_b = ta_pair(message), ta_other(message)

    conv_grad = convolution(True, qg, near_qg, qg_a, near_qg_a, qg_b, near_qg_b)
    scratch = [pltpu.VMEM((STAT_ROWS, 3 * rows), jnp.float32)]
    work = cost(heads, rows, 4, 1)
    sums = call(
        functools.partial(key_kernel, counts, width, 0), "key_side_0", [full, full], scratch, work,
        tile_mask, clip_lengths, kv, qg, near_qg, far_qg, stat, near_stat, far_stat,
    )
    sums = call(
        functools.partial(key_kernel, counts, width, 1), "key_side_1", [full, full], scratch, work,
        tile_mask, clip_lengths, kv, qg_a, near_qg_a, message_a, *sums,
    )
    key_grad, value_grad = call(
        functools.partial(key_kernel, counts, width, 2), "key_side_2", [half, half], scratch, work,
        tile_mask, clip_lengths, kv, qg_b, near_qg_b, message_b, *sums,
        conv_weight, conv_grad, far_qg, message_a,
    )
    return tuple(x.reshape(query_states.shape) for x in (layer_out, query_grad, key_grad, value_grad))


def solution(mesh):
    placed = P("ta", "ha", None, None)
    return jax.shard_map(
        shards,
        mesh=mesh,
        in_specs=(placed, placed, placed, P(), placed, P(), P()),
        out_specs=(placed,) * 4,
        check_vma=False,
    )
```

```python
import functools

import jax
import jax.numpy as jnp
from jax import lax
from jax.experimental import pallas as pl
from jax.experimental.pallas import tpu as pltpu
from jax.sharding import PartitionSpec as P

HEAD_DIM = 128
LOG2E = 1.4426950408889634
ROW_DELTA = 8
STAT_ROWS = 16
STAT_LANES = 256
UNROLL = 3
SCORE_UNROLL = 6
FLOOR = -1e30
SMALL = 2 * 1024 * 1024
LARGE = 8 * 1024 * 1024


CONTRACT_LAST = (((1,), (1,)), ((), ()))


def flip_pairs(count):
    return [(i, i ^ 1) for i in range(count)]


def other_pairs(count):
    pairs = []
    for i in range(count):
        to = i + 1 if i % 2 else i - 1
        pairs.append((i, to if 0 <= to < count else i))
    return pairs


def relay_pairs(count):
    pairs = []
    for i in range(count):
        to = i - 2 if i % 2 else i + 2
        if 0 <= to < count:
            pairs.append((i, to))
    return pairs


def ha_near(x):
    return lax.ppermute(x, "ha", flip_pairs(lax.axis_size("ha")))


def ha_relay(near):
    return lax.ppermute(near, "ha", relay_pairs(lax.axis_size("ha")))


def ha_far(x):
    return lax.ppermute(x, "ha", other_pairs(lax.axis_size("ha")))


def ta_pair(x):
    return lax.ppermute(x, "ta", flip_pairs(lax.axis_size("ta")))


def ta_other(x):
    return lax.ppermute(x, "ta", other_pairs(lax.axis_size("ta")))


def offsets(index):
    sign = 1 - 2 * lax.rem(index, 2)
    return (0, sign, -sign)


def inside(index, count):
    return (index >= 0) & (index < count)


def row_of(tile, frame, row, width):
    start = (2 * frame + row) * width
    return tile[start : start + width]


def shifted_sum(parts, width):
    column = lax.broadcasted_iota(jnp.int32, (width, HEAD_DIM), 0)
    before = jnp.where(column == 0, 0.0, pltpu.roll(parts[0], 1, 0))
    behind = jnp.where(column == width - 1, 0.0, pltpu.roll(parts[2], width - 1, 0))
    return parts[1] + before + behind


def total_of(terms):
    return functools.reduce(lambda x, y: x + y, terms)


def along_t(own, pair, other, place_now):
    even_t, _, in_t, _ = place_now
    ahead = jnp.where(in_t[0], jnp.where(even_t, other(1), pair(1)), 0.0)
    behind = jnp.where(in_t[1], jnp.where(even_t, pair(0), other(0)), 0.0)
    return [ahead, own(0), own(1), behind]


def conv_inner(tiles, weight, flipped, place_now, width):
    _, even_h, _, in_h = place_now
    tiles = [[x.astype(jnp.float32) for x in pair] for pair in tiles]

    def cell(slot, R):
        if R in (1, 2):
            return lambda frame: row_of(tiles[slot][0], frame, R - 1, width)
        if R == 0:
            return lambda frame: jnp.where(even_h | ~in_h[0], 0.0, row_of(tiles[slot][1], frame, 1, width))
        return lambda frame: jnp.where(even_h & in_h[1], row_of(tiles[slot][1], frame, 0, width), 0.0)

    slab = [along_t(cell(0, R), cell(1, R), cell(2, R), place_now) for R in range(4)]
    rows = []
    for f in range(2):
        for r in range(2):
            parts = []
            for dw in range(3):
                taps = [(dt, dh, 9 * dt + 3 * dh + dw) for dt in range(3) for dh in range(3)]
                taps = [(dt, dh, 26 - tap if flipped else tap) for dt, dh, tap in taps]
                parts.append(total_of([weight[tap : tap + 1] * slab[r + dh][f + dt] for dt, dh, tap in taps]))
            rows.append(shifted_sum(parts, width))
    return jnp.concatenate(rows, axis=0)


def conv_far(tiles, weight, flipped, place_now, width):
    _, even_h, _, in_h = place_now
    tiles = [x.astype(jnp.float32) for x in tiles]
    there = (even_h & in_h[0]) | (~even_h & in_h[1])

    def cell(slot):
        def of(frame):
            row = jnp.where(even_h, row_of(tiles[slot], frame, 1, width), row_of(tiles[slot], frame, 0, width))
            return jnp.where(there, row, 0.0)

        return of

    line = along_t(cell(0), cell(1), cell(2), place_now)
    rows = []
    for f in range(2):
        parts = []
        for dw in range(3):
            terms = []
            for dt in range(3):
                up, down = 9 * dt + dw, 9 * dt + 6 + dw
                if flipped:
                    up, down = 26 - up, 26 - down
                tap = jnp.where(even_h, weight[up : up + 1], weight[down : down + 1])
                terms.append(tap * line[f + dt])
            parts.append(total_of(terms))
        beside = shifted_sum(parts, width)
        rows += [jnp.where(even_h, beside, 0.0), jnp.where(even_h, 0.0, beside)]
    return jnp.concatenate(rows, axis=0)


def place(counts):
    index_t, index_h = lax.axis_index("ta"), lax.axis_index("ha")
    even_t, even_h = lax.rem(index_t, 2) == 0, lax.rem(index_h, 2) == 0
    in_t = (index_t > 0, index_t < counts[0] - 1)
    in_h = (index_h > 0, index_h < counts[1] - 1)
    return index_t, index_h, (even_t, even_h, in_t, in_h)


def head_columns(head):
    return pl.ds(pl.multiple_of(head * HEAD_DIM, HEAD_DIM), HEAD_DIM)


def dot_last(x, y):
    return lax.dot_general(x, y, CONTRACT_LAST, preferred_element_type=jnp.float32)


def dot(x, y):
    return jnp.dot(x, y, preferred_element_type=jnp.float32)


def column_kernel(counts, width, column, last, mask_ref, clip_ref, query_ref, own, pair, other, *rest):
    slots = [own, pair, other]
    if last:
        grad_ref, sums, tops, totals = rest[0], (rest[1], rest[4]), (rest[2], rest[5]), (rest[3], rest[6])
        exp_ref, att_ref, fac_own, fac_near, fac_far, delta_ref, stat_ref, bias, stat = rest[8:]
    else:
        exp_ref, sum_ref, top_ref, total_ref, bias = rest
    index_t, index_h, _ = place(counts)
    rows, channels = query_ref.shape
    heads = channels // HEAD_DIM
    scale = HEAD_DIM**-0.5
    lane = lax.broadcasted_iota(jnp.int32, (1, 3 * rows), 1)
    limit = jnp.zeros((1, 3 * rows), jnp.int32)
    for slot in range(3):
        a, b = offsets(index_t)[slot], offsets(index_h)[column]
        t, h = index_t + a, index_h + b
        kept = (mask_ref[index_t, index_h, 3 * (a + 1) + (b + 1)] == 1) & inside(t, counts[0]) & inside(h, counts[1])
        safe = jnp.clip(t, 0, counts[0] - 1)
        for f in range(2):
            live = jnp.where(kept, clip_ref[2 * safe + f], 0)
            limit = jnp.where(lane >= slot * rows + f * (rows // 2), live, limit)
    bias[...] = jnp.where(lax.rem(lane, width) < limit, 0.0, -jnp.inf)
    which = lax.broadcasted_iota(jnp.int32, (rows, HEAD_DIM), 1)

    def body(step, _):
        hs = [step * SCORE_UNROLL + u for u in range(SCORE_UNROLL)]
        tops_, accs, sums_ = [], [], []
        scored = []
        for h in hs:
            keys = jnp.concatenate([ref[0, :, head_columns(h)] for ref in slots], axis=0)
            s = dot_last(query_ref[:, head_columns(h)], keys) * (scale * LOG2E) + bias[...]
            scored.append(s)
            tops_.append(jnp.maximum(jnp.max(s, axis=1, keepdims=True), FLOOR))
        for u, h in enumerate(hs):
            e = jnp.exp2(scored[u] - tops_[u]).astype(jnp.bfloat16)
            exp_ref[h] = e
            values = jnp.concatenate([ref[1, :, head_columns(h)] for ref in slots], axis=0)
            both = dot(e, jnp.concatenate([values, jnp.ones_like(values)], axis=1))
            accs.append(both[:, :HEAD_DIM])
            sums_.append(both[:, HEAD_DIM:])
        for u, h in enumerate(hs):
            cols = head_columns(h)
            acc, total = accs[u], sums_[u]
            top = jnp.broadcast_to(tops_[u], (rows, HEAD_DIM))
            if not last:
                sum_ref[:, cols], top_ref[:, cols], total_ref[:, cols] = acc, top, total
                continue
            near_top, own_top = tops[1][:, cols], tops[0][:, cols]
            row_max = jnp.maximum(jnp.maximum(own_top, near_top), top)
            row_total = total * jnp.exp2(top - row_max) + totals[0][:, cols] * jnp.exp2(own_top - row_max)
            row_total = row_total + totals[1][:, cols] * jnp.exp2(near_top - row_max)
            log_total = row_max + jnp.log2(row_total)
            factors = [jnp.exp2(x - log_total) for x in (own_top, near_top, top)]
            for ref, factor in zip((fac_own, fac_near, fac_far), factors):
                ref[:, cols] = factor
            attention = sums[0][:, cols] * factors[0] + sums[1][:, cols] * factors[1] + acc * factors[2]
            att_ref[:, cols] = attention
            delta = jnp.sum(grad_ref[:, cols].astype(jnp.float32) * attention, axis=1, keepdims=True)
            delta = jnp.broadcast_to(delta, (rows, HEAD_DIM))
            delta_ref[:, cols] = delta
            marked = jnp.where(which == h, log_total, stat[...])
            stat[...] = jnp.where(which == h + ROW_DELTA, delta, marked)
        return 0

    if last:
        stat[...] = jnp.zeros_like(stat)
    lax.fori_loop(0, heads // SCORE_UNROLL, body, 0)
    if last:
        pad = jnp.zeros((-rows % HEAD_DIM, HEAD_DIM), jnp.float32)
        turned = jnp.concatenate([stat[...], pad], axis=0).T
        stat_ref[...] = turned[:STAT_ROWS, :rows]


def conv_kernel(counts, width, flipped, own, near, pair, near_pair, other, near_other, weight_ref, out_ref):
    _, _, place_now = place(counts)
    rows, channels = out_ref.shape

    def body(head, _):
        cols = head_columns(head)
        tiles = [(x[1, :, cols], y[1, :, cols]) for x, y in ((own, near), (pair, near_pair), (other, near_other))]
        out_ref[:, cols] = conv_inner(tiles, weight_ref[:, cols].astype(jnp.float32), flipped, place_now, width)
        return 0

    lax.fori_loop(0, channels // HEAD_DIM, body, 0)


def query_kernel(counts, width, grad_ref, weight_ref, *rest):
    slots, exps, factors = rest[:9], rest[9:12], rest[12:15]
    att_ref, delta_ref, conv_ref, out_ref, dq_ref, done_ref = rest[15:]
    done_ref[...] = jnp.zeros_like(done_ref)
    _, _, place_now = place(counts)
    rows, channels = grad_ref.shape
    heads = channels // HEAD_DIM
    scale = HEAD_DIM**-0.5
    wide = -(-3 * rows // HEAD_DIM)

    def body(step, _):
        for u in range(UNROLL):
            h = step * UNROLL + u
            cols = head_columns(h)
            grad = grad_ref[:, cols]
            delta = jnp.concatenate([delta_ref[:, cols]] * wide, axis=1)[:, : 3 * rows]
            dq = None
            for column in range(3):
                refs = slots[column::3]
                values = jnp.concatenate([ref[1, :, cols] for ref in refs], axis=0)
                keys = jnp.concatenate([ref[0, :, cols] for ref in refs], axis=0)
                ds = exps[column][h].astype(jnp.float32) * (dot_last(grad, values) - delta)
                part = dot(ds.astype(jnp.bfloat16), keys) * (factors[column][:, cols] * scale)
                dq = part if dq is None else dq + part
            dq_ref[:, cols] = dq.astype(jnp.bfloat16)
            tiles = [slots[i][1, :, cols] for i in (2, 5, 8)]
            conv = conv_ref[:, cols] + conv_far(tiles, weight_ref[:, cols].astype(jnp.float32), False, place_now, width)
            out_ref[:, cols] = (att_ref[:, cols] + conv).astype(jnp.bfloat16)
        return 0

    lax.fori_loop(0, heads // UNROLL, body, 0)


def pack_kernel(rows, qg_ref, own_ref, near_ref, far_ref, *rest):
    out_ref = rest[-1]
    out_ref[:rows] = qg_ref[0]
    out_ref[rows : 2 * rows] = qg_ref[1]
    first = 2 * rows
    out_ref[first:] = jnp.zeros(out_ref[first:].shape, jnp.bfloat16)
    for i, ref in enumerate((own_ref, near_ref, far_ref)):
        left = ref[...]
        for part in range(3):
            high = left.astype(jnp.bfloat16)
            out_ref[first + part * STAT_ROWS : first + (part + 1) * STAT_ROWS, i * STAT_LANES : i * STAT_LANES + rows] = high
            left = left - high.astype(jnp.float32)


def key_kernel(counts, width, slot_t, mask_ref, clip_ref, own, own_ref, near_ref, far_ref, *rest):
    first, last = slot_t == 0, slot_t == 2
    index_t, index_h, place_now = place(counts)
    rows, channels = own.shape[1:]
    heads = channels // HEAD_DIM
    scale = HEAD_DIM**-0.5

    def packed(ref, what, cols):
        return ref[what * rows : (what + 1) * rows, cols] if len(ref.shape) == 2 else ref[what, :, cols]

    if first:
        *stat_refs, dk_ref, dv_ref, stats = rest
        pieces = [ref[...] for ref in stat_refs]
    else:
        dk_sum, dv_sum, *edges, dk_ref, dv_ref, stats = rest
        pieces = []
        for i in range(3):
            parts = []
            for part in range(3):
                start = 2 * rows + part * STAT_ROWS
                parts.append(far_ref[start : start + STAT_ROWS, i * STAT_LANES : i * STAT_LANES + rows].astype(jnp.float32))
            pieces.append(parts[0] + (parts[1] + parts[2]))
    line = lax.broadcasted_iota(jnp.int32, (STAT_ROWS, rows), 0)
    for column in range(3):
        a, b = offsets(index_t)[slot_t], offsets(index_h)[column]
        t, h = index_t + a, index_h + b
        safe_t, safe_h = jnp.clip(t, 0, counts[0] - 1), jnp.clip(h, 0, counts[1] - 1)
        kept = (mask_ref[safe_t, safe_h, 3 * (1 - a) + (1 - b)] == 1) & inside(t, counts[0]) & inside(h, counts[1])
        pieces[column] = jnp.where(kept | (line >= ROW_DELTA), pieces[column], jnp.inf)
    stats[...] = jnp.concatenate(pieces, axis=1)
    row = lax.broadcasted_iota(jnp.int32, (rows, HEAD_DIM), 0)
    lens = [clip_ref[2 * index_t + f] for f in range(2)]
    live = lax.rem(row, width) < jnp.where(row < 2 * width, lens[0], lens[1])

    def body(step, _):
        for u in range(UNROLL):
            head = step * UNROLL + u
            cols = head_columns(head)
            queries = jnp.concatenate([packed(ref, 0, cols) for ref in (own_ref, near_ref, far_ref)], axis=0)
            grads = jnp.concatenate([packed(ref, 1, cols) for ref in (own_ref, near_ref, far_ref)], axis=0)
            s = dot_last(own[0, :, cols], queries)
            p = jnp.exp2(s * (scale * LOG2E) - stats[pl.ds(head, 1), :])
            dp = dot_last(own[1, :, cols], grads)
            ds = (p * (dp - stats[pl.ds(head + ROW_DELTA, 1), :])).astype(jnp.bfloat16)
            dv = dot(p.astype(jnp.bfloat16), grads)
            dk = dot(ds, queries)
            if not first:
                dk, dv = dk + dk_sum[:, cols], dv + dv_sum[:, cols]
            if not last:
                dk_ref[:, cols], dv_ref[:, cols] = dk, dv
                continue
            dk_ref[:, cols] = jnp.where(live, dk * scale, 0.0).astype(jnp.bfloat16)
            weight_ref, conv_ref, *far_refs = edges
            tiles = [packed(ref, 1, cols) for ref in (*far_refs, far_ref)]
            conv = conv_ref[:, cols] + conv_far(tiles, weight_ref[:, cols].astype(jnp.float32), True, place_now, width)
            dv_ref[:, cols] = (jnp.where(live, dv, 0.0) + conv).astype(jnp.bfloat16)
        return 0

    lax.fori_loop(0, heads // UNROLL, body, 0)


def cost(heads, rows, matmuls, columns):
    work = heads * rows * 3 * columns * rows * HEAD_DIM * 2 * matmuls
    moved = heads * rows * HEAD_DIM * 2 * 8 * columns
    return pl.CostEstimate(flops=work, bytes_accessed=moved, transcendentals=heads * rows * rows * 3 * columns)


def shards(query_states, key_states, value_states, conv_weight, out_grad, tile_mask, clip_lengths):
    width, channels = query_states.shape[2:]
    rows = query_states.shape[0] * query_states.shape[1] * width
    counts = (lax.axis_size("ta"), lax.axis_size("ha"))
    heads = channels // HEAD_DIM
    query, key, value, grad = [x.reshape(rows, channels) for x in (query_states, key_states, value_states, out_grad)]

    smem = pl.BlockSpec(memory_space=pltpu.SMEM)
    vmem = pl.BlockSpec(memory_space=pltpu.VMEM)
    params = pltpu.CompilerParams(vmem_limit_bytes=LARGE)
    half = jax.ShapeDtypeStruct((rows, channels), jnp.bfloat16)
    full = jax.ShapeDtypeStruct((rows, channels), jnp.float32)
    exps = jax.ShapeDtypeStruct((heads, rows, 3 * rows), jnp.bfloat16)
    bias = pltpu.VMEM((1, 3 * rows), jnp.float32)

    def call(kernel, name, out_shape, scratch, work, *args):
        scalars = 2 if args[0] is tile_mask else 0
        return pl.pallas_call(
            kernel,
            in_specs=[smem] * scalars + [vmem] * (len(args) - scalars),
            out_specs=[vmem] * len(out_shape),
            out_shape=out_shape,
            scratch_shapes=scratch,
            compiler_params=params,
            cost_estimate=work,
            name=name,
        )(*args)

    def convolution(flipped, *tiles):
        kernel = functools.partial(conv_kernel, counts, width, flipped)
        return call(kernel, "convolution", [full], [], cost(heads, rows, 1, 1), *tiles, conv_weight)[0]

    def scores(column, tiles):
        kernel = functools.partial(column_kernel, counts, width, column, False)
        work = cost(heads, rows, 2, 1)
        return call(kernel, f"scores_{column}", [exps, full, full, full], [bias], work, tile_mask, clip_lengths, query, *tiles)

    def later(x, *earlier):
        def kernel(x_ref, *rest):
            rest[-1][...] = x_ref[...]

        return pl.pallas_call(
            kernel,
            in_specs=[vmem] + [pl.BlockSpec(memory_space=pl.ANY)] * len(earlier),
            out_specs=vmem,
            out_shape=jax.ShapeDtypeStruct(x.shape, x.dtype),
            compiler_params=pltpu.CompilerParams(vmem_limit_bytes=SMALL),
            name="later",
        )(x, *earlier)

    def pair_up(x, y, *earlier):
        def kernel(x_ref, y_ref, *rest):
            rest[-1][0] = x_ref[...]
            rest[-1][1] = y_ref[...]

        return pl.pallas_call(
            kernel,
            in_specs=[vmem] * 2 + [pl.BlockSpec(memory_space=pl.ANY)] * len(earlier),
            out_specs=vmem,
            out_shape=jax.ShapeDtypeStruct((2,) + x.shape, x.dtype),
            compiler_params=pltpu.CompilerParams(vmem_limit_bytes=SMALL),
            name="pair_up",
        )(x, y, *earlier)

    def gate(x, *earlier):
        return pl.pallas_call(
            lambda *refs: None,
            in_specs=[pl.BlockSpec(memory_space=pl.ANY)] * (1 + len(earlier)),
            out_specs=pl.BlockSpec(memory_space=pl.ANY),
            out_shape=jax.ShapeDtypeStruct(x.shape, x.dtype),
            input_output_aliases={0: 0},
            compiler_params=pltpu.CompilerParams(vmem_limit_bytes=SMALL),
            name="gate",
        )(x, *earlier)

    kv = jnp.stack([key, value])
    near_kv = ha_near(kv)
    kv_a, kv_b = ta_pair(kv), ta_other(kv)
    qg = pair_up(query, grad, kv_a)
    qg_a, qg_b = ta_pair(qg), ta_other(qg)
    exp_own, *own_parts = scores(0, (kv, kv_a, kv_b))

    far_kv = ha_relay(near_kv)
    near_kv_again = later(near_kv, qg_a, qg_b, kv_b)
    near_kv_a, near_kv_b = ta_pair(near_kv_again), ta_other(near_kv_again)
    near_qg = ha_near(pair_up(query, grad, near_kv))
    exp_near, *near_parts = scores(1, (near_kv, near_kv_a, near_kv_b))
    conv_value = convolution(False, kv, near_kv, kv_a, near_kv_a, kv_b, near_kv_b)
    far_kv = later(far_kv, near_parts[0], own_parts[0], conv_value)
    far_kv_a, far_kv_b = ta_pair(far_kv), ta_other(far_kv)

    near_qg = gate(near_qg, near_parts[0])
    far_qg = ha_relay(near_qg)
    near_qg_a, near_qg_b = ta_pair(near_qg), ta_other(near_qg)
    exp_far, attention, fac_own, fac_near, fac_far, delta, stat = call(
        functools.partial(column_kernel, counts, width, 2, True),
        "scores_2",
        [exps] + [full] * 5 + [jax.ShapeDtypeStruct((STAT_ROWS, rows), jnp.float32)],
        [bias, pltpu.VMEM((rows, HEAD_DIM), jnp.float32)],
        cost(heads, rows, 2, 1),
        tile_mask, clip_lengths, query, far_kv, far_kv_a, far_kv_b, grad, *own_parts, *near_parts, conv_value,
    )
    near_stat, far_stat = ha_near(stat), ha_far(stat)
    layer_out, query_grad, done = call(
        functools.partial(query_kernel, counts, width),
        "query_side",
        [half, half, jax.ShapeDtypeStruct((8, HEAD_DIM), jnp.float32)],
        [],
        cost(heads, rows, 2, 3),
        grad, conv_weight, kv, near_kv, far_kv, kv_a, near_kv_a, far_kv_a, kv_b, near_kv_b, far_kv_b,
        exp_own, exp_near, exp_far, fac_own, fac_near, fac_far, attention, delta, conv_value,
    )
    message = pl.pallas_call(
        functools.partial(pack_kernel, rows),
        in_specs=[vmem] * 4 + [pl.BlockSpec(memory_space=pl.ANY)] * 3,
        out_specs=vmem,
        out_shape=jax.ShapeDtypeStruct((2 * rows + 3 * STAT_ROWS, channels), jnp.bfloat16),
        compiler_params=pltpu.CompilerParams(vmem_limit_bytes=SMALL),
        name="pack",
    )(far_qg, stat, near_stat, far_stat, done, near_qg_a, near_qg_b)
    message_a, message_b = ta_pair(message), ta_other(message)

    conv_grad = convolution(True, qg, near_qg, qg_a, near_qg_a, qg_b, near_qg_b)
    scratch = [pltpu.VMEM((STAT_ROWS, 3 * rows), jnp.float32)]
    work = cost(heads, rows, 4, 1)
    sums = call(
        functools.partial(key_kernel, counts, width, 0), "key_side_0", [full, full], scratch, work,
        tile_mask, clip_lengths, kv, qg, near_qg, far_qg, stat, near_stat, far_stat,
    )
    sums = call(
        functools.partial(key_kernel, counts, width, 1), "key_side_1", [full, full], scratch, work,
        tile_mask, clip_lengths, kv, qg_a, near_qg_a, message_a, *sums,
    )
    key_grad, value_grad = call(
        functools.partial(key_kernel, counts, width, 2), "key_side_2", [half, half], scratch, work,
        tile_mask, clip_lengths, kv, qg_b, near_qg_b, message_b, *sums,
        conv_weight, conv_grad, far_qg, message_a,
    )
    return tuple(x.reshape(query_states.shape) for x in (layer_out, query_grad, key_grad, value_grad))


def solution(mesh):
    placed = P("ta", "ha", None, None)
    return jax.shard_map(
        shards,
        mesh=mesh,
        in_specs=(placed, placed, placed, P(), placed, P(), P()),
        out_specs=(placed,) * 4,
        check_vma=False,
    )
```

```python
import functools

import jax
import jax.numpy as jnp
from jax import lax
from jax.experimental import pallas as pl
from jax.experimental.pallas import tpu as pltpu
from jax.sharding import PartitionSpec as P

HEAD_DIM = 128
LOG2E = 1.4426950408889634
ROW_DELTA = 8
STAT_ROWS = 16
STAT_LANES = 256
UNROLL = 6
FLOOR = -1e30
SMALL = 2 * 1024 * 1024
LARGE = 8 * 1024 * 1024


CONTRACT_LAST = (((1,), (1,)), ((), ()))


def flip_pairs(count):
    return [(i, i ^ 1) for i in range(count)]


def other_pairs(count):
    pairs = []
    for i in range(count):
        to = i + 1 if i % 2 else i - 1
        pairs.append((i, to if 0 <= to < count else i))
    return pairs


def relay_pairs(count):
    pairs = []
    for i in range(count):
        to = i - 2 if i % 2 else i + 2
        if 0 <= to < count:
            pairs.append((i, to))
    return pairs


def ha_near(x):
    return lax.ppermute(x, "ha", flip_pairs(lax.axis_size("ha")))


def ha_relay(near):
    return lax.ppermute(near, "ha", relay_pairs(lax.axis_size("ha")))


def ha_far(x):
    return lax.ppermute(x, "ha", other_pairs(lax.axis_size("ha")))


def ta_pair(x):
    return lax.ppermute(x, "ta", flip_pairs(lax.axis_size("ta")))


def ta_other(x):
    return lax.ppermute(x, "ta", other_pairs(lax.axis_size("ta")))


def offsets(index):
    sign = 1 - 2 * lax.rem(index, 2)
    return (0, sign, -sign)


def inside(index, count):
    return (index >= 0) & (index < count)


def row_of(tile, frame, row, width):
    start = (2 * frame + row) * width
    return tile[start : start + width]


def shifted_sum(parts, width):
    column = lax.broadcasted_iota(jnp.int32, (width, HEAD_DIM), 0)
    before = jnp.where(column == 0, 0.0, pltpu.roll(parts[0], 1, 0))
    behind = jnp.where(column == width - 1, 0.0, pltpu.roll(parts[2], width - 1, 0))
    return parts[1] + before + behind


def total_of(terms):
    return functools.reduce(lambda x, y: x + y, terms)


def along_t(own, pair, other, place_now):
    even_t, _, in_t, _ = place_now
    ahead = jnp.where(in_t[0], jnp.where(even_t, other(1), pair(1)), 0.0)
    behind = jnp.where(in_t[1], jnp.where(even_t, pair(0), other(0)), 0.0)
    return [ahead, own(0), own(1), behind]


def conv_inner(tiles, weight, flipped, place_now, width):
    _, even_h, _, in_h = place_now
    tiles = [[x.astype(jnp.float32) for x in pair] for pair in tiles]

    def cell(slot, R):
        if R in (1, 2):
            return lambda frame: row_of(tiles[slot][0], frame, R - 1, width)
        if R == 0:
            return lambda frame: jnp.where(even_h | ~in_h[0], 0.0, row_of(tiles[slot][1], frame, 1, width))
        return lambda frame: jnp.where(even_h & in_h[1], row_of(tiles[slot][1], frame, 0, width), 0.0)

    slab = [along_t(cell(0, R), cell(1, R), cell(2, R), place_now) for R in range(4)]
    rows = []
    for f in range(2):
        for r in range(2):
            parts = []
            for dw in range(3):
                taps = [(dt, dh, 9 * dt + 3 * dh + dw) for dt in range(3) for dh in range(3)]
                taps = [(dt, dh, 26 - tap if flipped else tap) for dt, dh, tap in taps]
                parts.append(total_of([weight[tap : tap + 1] * slab[r + dh][f + dt] for dt, dh, tap in taps]))
            rows.append(shifted_sum(parts, width))
    return jnp.concatenate(rows, axis=0)


def conv_far(tiles, weight, flipped, place_now, width):
    _, even_h, _, in_h = place_now
    tiles = [x.astype(jnp.float32) for x in tiles]
    there = (even_h & in_h[0]) | (~even_h & in_h[1])

    def cell(slot):
        def of(frame):
            row = jnp.where(even_h, row_of(tiles[slot], frame, 1, width), row_of(tiles[slot], frame, 0, width))
            return jnp.where(there, row, 0.0)

        return of

    line = along_t(cell(0), cell(1), cell(2), place_now)
    rows = []
    for f in range(2):
        parts = []
        for dw in range(3):
            terms = []
            for dt in range(3):
                up, down = 9 * dt + dw, 9 * dt + 6 + dw
                if flipped:
                    up, down = 26 - up, 26 - down
                tap = jnp.where(even_h, weight[up : up + 1], weight[down : down + 1])
                terms.append(tap * line[f + dt])
            parts.append(total_of(terms))
        beside = shifted_sum(parts, width)
        rows += [jnp.where(even_h, beside, 0.0), jnp.where(even_h, 0.0, beside)]
    return jnp.concatenate(rows, axis=0)


def place(counts):
    index_t, index_h = lax.axis_index("ta"), lax.axis_index("ha")
    even_t, even_h = lax.rem(index_t, 2) == 0, lax.rem(index_h, 2) == 0
    in_t = (index_t > 0, index_t < counts[0] - 1)
    in_h = (index_h > 0, index_h < counts[1] - 1)
    return index_t, index_h, (even_t, even_h, in_t, in_h)


def head_columns(head):
    return pl.ds(pl.multiple_of(head * HEAD_DIM, HEAD_DIM), HEAD_DIM)


def dot_last(x, y):
    return lax.dot_general(x, y, CONTRACT_LAST, preferred_element_type=jnp.float32)


def dot(x, y):
    return jnp.dot(x, y, preferred_element_type=jnp.float32)


def column_kernel(counts, width, column, last, mask_ref, clip_ref, query_ref, own, pair, other, *rest):
    slots = [own, pair, other]
    if last:
        grad_ref, sums, tops, totals = rest[0], (rest[1], rest[4]), (rest[2], rest[5]), (rest[3], rest[6])
        exp_ref, att_ref, fac_own, fac_near, fac_far, delta_ref, stat_ref, bias, stat = rest[8:]
    else:
        exp_ref, sum_ref, top_ref, total_ref, bias = rest
    index_t, index_h, _ = place(counts)
    rows, channels = query_ref.shape
    heads = channels // HEAD_DIM
    scale = HEAD_DIM**-0.5
    lane = lax.broadcasted_iota(jnp.int32, (1, 3 * rows), 1)
    limit = jnp.zeros((1, 3 * rows), jnp.int32)
    for slot in range(3):
        a, b = offsets(index_t)[slot], offsets(index_h)[column]
        t, h = index_t + a, index_h + b
        kept = (mask_ref[index_t, index_h, 3 * (a + 1) + (b + 1)] == 1) & inside(t, counts[0]) & inside(h, counts[1])
        safe = jnp.clip(t, 0, counts[0] - 1)
        for f in range(2):
            live = jnp.where(kept, clip_ref[2 * safe + f], 0)
            limit = jnp.where(lane >= slot * rows + f * (rows // 2), live, limit)
    bias[...] = jnp.where(lax.rem(lane, width) < limit, 0.0, -jnp.inf)
    which = lax.broadcasted_iota(jnp.int32, (rows, HEAD_DIM), 1)

    def body(step, _):
        hs = [step * UNROLL + u for u in range(UNROLL)]
        tops_, accs, sums_ = [], [], []
        scored = []
        for h in hs:
            keys = jnp.concatenate([ref[0, :, head_columns(h)] for ref in slots], axis=0)
            s = dot_last(query_ref[:, head_columns(h)], keys) * (scale * LOG2E) + bias[...]
            scored.append(s)
            tops_.append(jnp.maximum(jnp.max(s, axis=1, keepdims=True), FLOOR))
        for u, h in enumerate(hs):
            e = jnp.exp2(scored[u] - tops_[u]).astype(jnp.bfloat16)
            exp_ref[h] = e
            values = jnp.concatenate([ref[1, :, head_columns(h)] for ref in slots], axis=0)
            both = dot(e, jnp.concatenate([values, jnp.ones_like(values)], axis=1))
            accs.append(both[:, :HEAD_DIM])
            sums_.append(both[:, HEAD_DIM:])
        for u, h in enumerate(hs):
            cols = head_columns(h)
            acc, total = accs[u], sums_[u]
            top = jnp.broadcast_to(tops_[u], (rows, HEAD_DIM))
            if not last:
                sum_ref[:, cols], top_ref[:, cols], total_ref[:, cols] = acc, top, total
                continue
            near_top, own_top = tops[1][:, cols], tops[0][:, cols]
            row_max = jnp.maximum(jnp.maximum(own_top, near_top), top)
            row_total = total * jnp.exp2(top - row_max) + totals[0][:, cols] * jnp.exp2(own_top - row_max)
            row_total = row_total + totals[1][:, cols] * jnp.exp2(near_top - row_max)
            log_total = row_max + jnp.log2(row_total)
            factors = [jnp.exp2(x - log_total) for x in (own_top, near_top, top)]
            for ref, factor in zip((fac_own, fac_near, fac_far), factors):
                ref[:, cols] = factor
            attention = sums[0][:, cols] * factors[0] + sums[1][:, cols] * factors[1] + acc * factors[2]
            att_ref[:, cols] = attention
            delta = jnp.sum(grad_ref[:, cols].astype(jnp.float32) * attention, axis=1, keepdims=True)
            delta = jnp.broadcast_to(delta, (rows, HEAD_DIM))
            delta_ref[:, cols] = delta
            marked = jnp.where(which == h, log_total, stat[...])
            stat[...] = jnp.where(which == h + ROW_DELTA, delta, marked)
        return 0

    if last:
        stat[...] = jnp.zeros_like(stat)
    lax.fori_loop(0, heads // UNROLL, body, 0)
    if last:
        pad = jnp.zeros((-rows % HEAD_DIM, HEAD_DIM), jnp.float32)
        turned = jnp.concatenate([stat[...], pad], axis=0).T
        stat_ref[...] = turned[:STAT_ROWS, :rows]


def conv_kernel(counts, width, flipped, own, near, pair, near_pair, other, near_other, weight_ref, out_ref):
    _, _, place_now = place(counts)
    rows, channels = out_ref.shape

    def body(head, _):
        cols = head_columns(head)
        tiles = [(x[1, :, cols], y[1, :, cols]) for x, y in ((own, near), (pair, near_pair), (other, near_other))]
        out_ref[:, cols] = conv_inner(tiles, weight_ref[:, cols].astype(jnp.float32), flipped, place_now, width)
        return 0

    lax.fori_loop(0, channels // HEAD_DIM, body, 0)


def query_kernel(counts, width, grad_ref, weight_ref, *rest):
    slots, exps, factors = rest[:9], rest[9:12], rest[12:15]
    att_ref, delta_ref, conv_ref, out_ref, dq_ref, done_ref = rest[15:]
    done_ref[...] = jnp.zeros_like(done_ref)
    _, _, place_now = place(counts)
    rows, channels = grad_ref.shape
    heads = channels // HEAD_DIM
    scale = HEAD_DIM**-0.5
    wide = -(-3 * rows // HEAD_DIM)

    def body(step, _):
        for u in range(UNROLL):
            h = step * UNROLL + u
            cols = head_columns(h)
            grad = grad_ref[:, cols]
            delta = jnp.concatenate([delta_ref[:, cols]] * wide, axis=1)[:, : 3 * rows]
            dq = None
            for column in range(3):
                refs = slots[column::3]
                values = jnp.concatenate([ref[1, :, cols] for ref in refs], axis=0)
                keys = jnp.concatenate([ref[0, :, cols] for ref in refs], axis=0)
                ds = exps[column][h].astype(jnp.float32) * (dot_last(grad, values) - delta)
                part = dot(ds.astype(jnp.bfloat16), keys) * (factors[column][:, cols] * scale)
                dq = part if dq is None else dq + part
            dq_ref[:, cols] = dq.astype(jnp.bfloat16)
            tiles = [slots[i][1, :, cols] for i in (2, 5, 8)]
            conv = conv_ref[:, cols] + conv_far(tiles, weight_ref[:, cols].astype(jnp.float32), False, place_now, width)
            out_ref[:, cols] = (att_ref[:, cols] + conv).astype(jnp.bfloat16)
        return 0

    lax.fori_loop(0, heads // UNROLL, body, 0)


def pack_kernel(rows, qg_ref, own_ref, near_ref, far_ref, *rest):
    out_ref = rest[-1]
    out_ref[:rows] = qg_ref[0]
    out_ref[rows : 2 * rows] = qg_ref[1]
    first = 2 * rows
    out_ref[first:] = jnp.zeros(out_ref[first:].shape, jnp.bfloat16)
    for i, ref in enumerate((own_ref, near_ref, far_ref)):
        left = ref[...]
        for part in range(3):
            high = left.astype(jnp.bfloat16)
            out_ref[first + part * STAT_ROWS : first + (part + 1) * STAT_ROWS, i * STAT_LANES : i * STAT_LANES + rows] = high
            left = left - high.astype(jnp.float32)


def key_kernel(counts, width, slot_t, mask_ref, clip_ref, own, own_ref, near_ref, far_ref, *rest):
    first, last = slot_t == 0, slot_t == 2
    index_t, index_h, place_now = place(counts)
    rows, channels = own.shape[1:]
    heads = channels // HEAD_DIM
    scale = HEAD_DIM**-0.5

    def packed(ref, what, cols):
        return ref[what * rows : (what + 1) * rows, cols] if len(ref.shape) == 2 else ref[what, :, cols]

    if first:
        *stat_refs, dk_ref, dv_ref, stats = rest
        pieces = [ref[...] for ref in stat_refs]
    else:
        dk_sum, dv_sum, *edges, dk_ref, dv_ref, stats = rest
        pieces = []
        for i in range(3):
            parts = []
            for part in range(3):
                start = 2 * rows + part * STAT_ROWS
                parts.append(far_ref[start : start + STAT_ROWS, i * STAT_LANES : i * STAT_LANES + rows].astype(jnp.float32))
            pieces.append(parts[0] + (parts[1] + parts[2]))
    line = lax.broadcasted_iota(jnp.int32, (STAT_ROWS, rows), 0)
    for column in range(3):
        a, b = offsets(index_t)[slot_t], offsets(index_h)[column]
        t, h = index_t + a, index_h + b
        safe_t, safe_h = jnp.clip(t, 0, counts[0] - 1), jnp.clip(h, 0, counts[1] - 1)
        kept = (mask_ref[safe_t, safe_h, 3 * (1 - a) + (1 - b)] == 1) & inside(t, counts[0]) & inside(h, counts[1])
        pieces[column] = jnp.where(kept | (line >= ROW_DELTA), pieces[column], jnp.inf)
    stats[...] = jnp.concatenate(pieces, axis=1)
    row = lax.broadcasted_iota(jnp.int32, (rows, HEAD_DIM), 0)
    lens = [clip_ref[2 * index_t + f] for f in range(2)]
    live = lax.rem(row, width) < jnp.where(row < 2 * width, lens[0], lens[1])

    def body(step, _):
        for u in range(UNROLL):
            head = step * UNROLL + u
            cols = head_columns(head)
            queries = jnp.concatenate([packed(ref, 0, cols) for ref in (own_ref, near_ref, far_ref)], axis=0)
            grads = jnp.concatenate([packed(ref, 1, cols) for ref in (own_ref, near_ref, far_ref)], axis=0)
            s = dot_last(own[0, :, cols], queries)
            p = jnp.exp2(s * (scale * LOG2E) - stats[pl.ds(head, 1), :])
            dp = dot_last(own[1, :, cols], grads)
            ds = (p * (dp - stats[pl.ds(head + ROW_DELTA, 1), :])).astype(jnp.bfloat16)
            dv = dot(p.astype(jnp.bfloat16), grads)
            dk = dot(ds, queries)
            if not first:
                dk, dv = dk + dk_sum[:, cols], dv + dv_sum[:, cols]
            if not last:
                dk_ref[:, cols], dv_ref[:, cols] = dk, dv
                continue
            dk_ref[:, cols] = jnp.where(live, dk * scale, 0.0).astype(jnp.bfloat16)
            weight_ref, conv_ref, *far_refs = edges
            tiles = [packed(ref, 1, cols) for ref in (*far_refs, far_ref)]
            conv = conv_ref[:, cols] + conv_far(tiles, weight_ref[:, cols].astype(jnp.float32), True, place_now, width)
            dv_ref[:, cols] = (jnp.where(live, dv, 0.0) + conv).astype(jnp.bfloat16)
        return 0

    lax.fori_loop(0, heads // UNROLL, body, 0)


def cost(heads, rows, matmuls, columns):
    work = heads * rows * 3 * columns * rows * HEAD_DIM * 2 * matmuls
    moved = heads * rows * HEAD_DIM * 2 * 8 * columns
    return pl.CostEstimate(flops=work, bytes_accessed=moved, transcendentals=heads * rows * rows * 3 * columns)


def shards(query_states, key_states, value_states, conv_weight, out_grad, tile_mask, clip_lengths):
    width, channels = query_states.shape[2:]
    rows = query_states.shape[0] * query_states.shape[1] * width
    counts = (lax.axis_size("ta"), lax.axis_size("ha"))
    heads = channels // HEAD_DIM
    query, key, value, grad = [x.reshape(rows, channels) for x in (query_states, key_states, value_states, out_grad)]

    smem = pl.BlockSpec(memory_space=pltpu.SMEM)
    vmem = pl.BlockSpec(memory_space=pltpu.VMEM)
    params = pltpu.CompilerParams(vmem_limit_bytes=LARGE)
    half = jax.ShapeDtypeStruct((rows, channels), jnp.bfloat16)
    full = jax.ShapeDtypeStruct((rows, channels), jnp.float32)
    exps = jax.ShapeDtypeStruct((heads, rows, 3 * rows), jnp.bfloat16)
    bias = pltpu.VMEM((1, 3 * rows), jnp.float32)

    def call(kernel, name, out_shape, scratch, work, *args):
        scalars = 2 if args[0] is tile_mask else 0
        return pl.pallas_call(
            kernel,
            in_specs=[smem] * scalars + [vmem] * (len(args) - scalars),
            out_specs=[vmem] * len(out_shape),
            out_shape=out_shape,
            scratch_shapes=scratch,
            compiler_params=params,
            cost_estimate=work,
            name=name,
        )(*args)

    def convolution(flipped, *tiles):
        kernel = functools.partial(conv_kernel, counts, width, flipped)
        return call(kernel, "convolution", [full], [], cost(heads, rows, 1, 1), *tiles, conv_weight)[0]

    def scores(column, tiles):
        kernel = functools.partial(column_kernel, counts, width, column, False)
        work = cost(heads, rows, 2, 1)
        return call(kernel, f"scores_{column}", [exps, full, full, full], [bias], work, tile_mask, clip_lengths, query, *tiles)

    def later(x, *earlier):
        def kernel(x_ref, *rest):
            rest[-1][...] = x_ref[...]

        return pl.pallas_call(
            kernel,
            in_specs=[vmem] + [pl.BlockSpec(memory_space=pl.ANY)] * len(earlier),
            out_specs=vmem,
            out_shape=jax.ShapeDtypeStruct(x.shape, x.dtype),
            compiler_params=pltpu.CompilerParams(vmem_limit_bytes=SMALL),
            name="later",
        )(x, *earlier)

    def pair_up(x, y, *earlier):
        def kernel(x_ref, y_ref, *rest):
            rest[-1][0] = x_ref[...]
            rest[-1][1] = y_ref[...]

        return pl.pallas_call(
            kernel,
            in_specs=[vmem] * 2 + [pl.BlockSpec(memory_space=pl.ANY)] * len(earlier),
            out_specs=vmem,
            out_shape=jax.ShapeDtypeStruct((2,) + x.shape, x.dtype),
            compiler_params=pltpu.CompilerParams(vmem_limit_bytes=SMALL),
            name="pair_up",
        )(x, y, *earlier)

    def gate(x, *earlier):
        return pl.pallas_call(
            lambda *refs: None,
            in_specs=[pl.BlockSpec(memory_space=pl.ANY)] * (1 + len(earlier)),
            out_specs=pl.BlockSpec(memory_space=pl.ANY),
            out_shape=jax.ShapeDtypeStruct(x.shape, x.dtype),
            input_output_aliases={0: 0},
            compiler_params=pltpu.CompilerParams(vmem_limit_bytes=SMALL),
            name="gate",
        )(x, *earlier)

    near_k = ha_near(key)
    kv = jnp.stack([key, value])
    kv_a, kv_b = ta_pair(kv), ta_other(kv)
    qg = pair_up(query, grad, kv_a)
    qg_a, qg_b = ta_pair(qg), ta_other(qg)
    near_v = ha_near(later(value, near_k))
    far_k = ha_relay(near_k)
    exp_own, *own_parts = scores(0, (kv, kv_a, kv_b))

    far_v = ha_relay(near_v)
    near_kv = pair_up(near_k, near_v, qg_a, qg_b)
    near_kv_a, near_kv_b = ta_pair(near_kv), ta_other(near_kv)
    near_qg = ha_near(pair_up(query, grad, near_v, far_k))
    exp_near, *near_parts = scores(1, (near_kv, near_kv_a, near_kv_b))
    far_kv = pair_up(far_k, far_v, own_parts[0], near_parts[0])
    far_kv_a, far_kv_b = ta_pair(far_kv), ta_other(far_kv)

    conv_value = convolution(False, kv, near_kv, kv_a, near_kv_a, kv_b, near_kv_b)

    near_qg = gate(near_qg, near_parts[0])
    far_qg = ha_relay(near_qg)
    near_qg_a, near_qg_b = ta_pair(near_qg), ta_other(near_qg)
    exp_far, attention, fac_own, fac_near, fac_far, delta, stat = call(
        functools.partial(column_kernel, counts, width, 2, True),
        "scores_2",
        [exps] + [full] * 5 + [jax.ShapeDtypeStruct((STAT_ROWS, rows), jnp.float32)],
        [bias, pltpu.VMEM((rows, HEAD_DIM), jnp.float32)],
        cost(heads, rows, 2, 1),
        tile_mask, clip_lengths, query, far_kv, far_kv_a, far_kv_b, grad, *own_parts, *near_parts, conv_value,
    )
    near_stat, far_stat = ha_near(stat), ha_far(stat)
    layer_out, query_grad, done = call(
        functools.partial(query_kernel, counts, width),
        "query_side",
        [half, half, jax.ShapeDtypeStruct((8, HEAD_DIM), jnp.float32)],
        [],
        cost(heads, rows, 2, 3),
        grad, conv_weight, kv, near_kv, far_kv, kv_a, near_kv_a, far_kv_a, kv_b, near_kv_b, far_kv_b,
        exp_own, exp_near, exp_far, fac_own, fac_near, fac_far, attention, delta, conv_value,
    )
    message = pl.pallas_call(
        functools.partial(pack_kernel, rows),
        in_specs=[vmem] * 4 + [pl.BlockSpec(memory_space=pl.ANY)] * 3,
        out_specs=vmem,
        out_shape=jax.ShapeDtypeStruct((2 * rows + 3 * STAT_ROWS, channels), jnp.bfloat16),
        compiler_params=pltpu.CompilerParams(vmem_limit_bytes=SMALL),
        name="pack",
    )(far_qg, stat, near_stat, far_stat, done, near_qg_a, near_qg_b)
    message_a, message_b = ta_pair(message), ta_other(message)

    conv_grad = convolution(True, qg, near_qg, qg_a, near_qg_a, qg_b, near_qg_b)
    scratch = [pltpu.VMEM((STAT_ROWS, 3 * rows), jnp.float32)]
    work = cost(heads, rows, 4, 1)
    sums = call(
        functools.partial(key_kernel, counts, width, 0), "key_side_0", [full, full], scratch, work,
        tile_mask, clip_lengths, kv, qg, near_qg, far_qg, stat, near_stat, far_stat,
    )
    sums = call(
        functools.partial(key_kernel, counts, width, 1), "key_side_1", [full, full], scratch, work,
        tile_mask, clip_lengths, kv, qg_a, near_qg_a, message_a, *sums,
    )
    key_grad, value_grad = call(
        functools.partial(key_kernel, counts, width, 2), "key_side_2", [half, half], scratch, work,
        tile_mask, clip_lengths, kv, qg_b, near_qg_b, message_b, *sums,
        conv_weight, conv_grad, far_qg, message_a,
    )
    return tuple(x.reshape(query_states.shape) for x in (layer_out, query_grad, key_grad, value_grad))


def solution(mesh):
    placed = P("ta", "ha", None, None)
    return jax.shard_map(
        shards,
        mesh=mesh,
        in_specs=(placed, placed, placed, P(), placed, P(), P()),
        out_specs=(placed,) * 4,
        check_vma=False,
    )
```

```python
import functools

import jax
import jax.numpy as jnp
from jax import lax
from jax.experimental import pallas as pl
from jax.experimental.pallas import tpu as pltpu
from jax.sharding import PartitionSpec as P

HEAD_DIM = 128
LOG2E = 1.4426950408889634
ROW_DELTA = 8
STAT_ROWS = 16
STAT_LANES = 256
UNROLL = 6
FLOOR = -1e30
SMALL = 2 * 1024 * 1024
LARGE = 8 * 1024 * 1024


CONTRACT_LAST = (((1,), (1,)), ((), ()))


def flip_pairs(count):
    return [(i, i ^ 1) for i in range(count)]


def other_pairs(count):
    pairs = []
    for i in range(count):
        to = i + 1 if i % 2 else i - 1
        pairs.append((i, to if 0 <= to < count else i))
    return pairs


def relay_pairs(count):
    pairs = []
    for i in range(count):
        to = i - 2 if i % 2 else i + 2
        if 0 <= to < count:
            pairs.append((i, to))
    return pairs


def ha_near(x):
    return lax.ppermute(x, "ha", flip_pairs(lax.axis_size("ha")))


def ha_relay(near):
    return lax.ppermute(near, "ha", relay_pairs(lax.axis_size("ha")))


def ha_far(x):
    return lax.ppermute(x, "ha", other_pairs(lax.axis_size("ha")))


def ta_pair(x):
    return lax.ppermute(x, "ta", flip_pairs(lax.axis_size("ta")))


def ta_other(x):
    return lax.ppermute(x, "ta", other_pairs(lax.axis_size("ta")))


def offsets(index):
    sign = 1 - 2 * lax.rem(index, 2)
    return (0, sign, -sign)


def inside(index, count):
    return (index >= 0) & (index < count)


def row_of(tile, frame, row, width):
    start = (2 * frame + row) * width
    return tile[start : start + width]


def shifted_sum(parts, width):
    column = lax.broadcasted_iota(jnp.int32, (width, HEAD_DIM), 0)
    before = jnp.where(column == 0, 0.0, pltpu.roll(parts[0], 1, 0))
    behind = jnp.where(column == width - 1, 0.0, pltpu.roll(parts[2], width - 1, 0))
    return parts[1] + before + behind


def total_of(terms):
    return functools.reduce(lambda x, y: x + y, terms)


def along_t(own, pair, other, place_now):
    even_t, _, in_t, _ = place_now
    ahead = jnp.where(in_t[0], jnp.where(even_t, other(1), pair(1)), 0.0)
    behind = jnp.where(in_t[1], jnp.where(even_t, pair(0), other(0)), 0.0)
    return [ahead, own(0), own(1), behind]


def conv_inner(tiles, weight, flipped, place_now, width):
    _, even_h, _, in_h = place_now
    tiles = [[x.astype(jnp.float32) for x in pair] for pair in tiles]

    def cell(slot, R):
        if R in (1, 2):
            return lambda frame: row_of(tiles[slot][0], frame, R - 1, width)
        if R == 0:
            return lambda frame: jnp.where(even_h | ~in_h[0], 0.0, row_of(tiles[slot][1], frame, 1, width))
        return lambda frame: jnp.where(even_h & in_h[1], row_of(tiles[slot][1], frame, 0, width), 0.0)

    slab = [along_t(cell(0, R), cell(1, R), cell(2, R), place_now) for R in range(4)]
    rows = []
    for f in range(2):
        for r in range(2):
            parts = []
            for dw in range(3):
                taps = [(dt, dh, 9 * dt + 3 * dh + dw) for dt in range(3) for dh in range(3)]
                taps = [(dt, dh, 26 - tap if flipped else tap) for dt, dh, tap in taps]
                parts.append(total_of([weight[tap : tap + 1] * slab[r + dh][f + dt] for dt, dh, tap in taps]))
            rows.append(shifted_sum(parts, width))
    return jnp.concatenate(rows, axis=0)


def conv_far(tiles, weight, flipped, place_now, width):
    _, even_h, _, in_h = place_now
    tiles = [x.astype(jnp.float32) for x in tiles]
    there = (even_h & in_h[0]) | (~even_h & in_h[1])

    def cell(slot):
        def of(frame):
            row = jnp.where(even_h, row_of(tiles[slot], frame, 1, width), row_of(tiles[slot], frame, 0, width))
            return jnp.where(there, row, 0.0)

        return of

    line = along_t(cell(0), cell(1), cell(2), place_now)
    rows = []
    for f in range(2):
        parts = []
        for dw in range(3):
            terms = []
            for dt in range(3):
                up, down = 9 * dt + dw, 9 * dt + 6 + dw
                if flipped:
                    up, down = 26 - up, 26 - down
                tap = jnp.where(even_h, weight[up : up + 1], weight[down : down + 1])
                terms.append(tap * line[f + dt])
            parts.append(total_of(terms))
        beside = shifted_sum(parts, width)
        rows += [jnp.where(even_h, beside, 0.0), jnp.where(even_h, 0.0, beside)]
    return jnp.concatenate(rows, axis=0)


def place(counts):
    index_t, index_h = lax.axis_index("ta"), lax.axis_index("ha")
    even_t, even_h = lax.rem(index_t, 2) == 0, lax.rem(index_h, 2) == 0
    in_t = (index_t > 0, index_t < counts[0] - 1)
    in_h = (index_h > 0, index_h < counts[1] - 1)
    return index_t, index_h, (even_t, even_h, in_t, in_h)


def head_columns(head):
    return pl.ds(pl.multiple_of(head * HEAD_DIM, HEAD_DIM), HEAD_DIM)


def dot_last(x, y):
    return lax.dot_general(x, y, CONTRACT_LAST, preferred_element_type=jnp.float32)


def dot(x, y):
    return jnp.dot(x, y, preferred_element_type=jnp.float32)


def column_kernel(counts, width, column, last, mask_ref, clip_ref, query_ref, own, pair, other, *rest):
    slots = [own, pair, other]
    if last:
        grad_ref, sums, tops, totals = rest[0], (rest[1], rest[4]), (rest[2], rest[5]), (rest[3], rest[6])
        exp_ref, att_ref, fac_own, fac_near, fac_far, delta_ref, stat_ref, bias, stat = rest[8:]
    else:
        exp_ref, sum_ref, top_ref, total_ref, bias = rest
    index_t, index_h, _ = place(counts)
    rows, channels = query_ref.shape
    heads = channels // HEAD_DIM
    scale = HEAD_DIM**-0.5
    lane = lax.broadcasted_iota(jnp.int32, (1, 3 * rows), 1)
    limit = jnp.zeros((1, 3 * rows), jnp.int32)
    for slot in range(3):
        a, b = offsets(index_t)[slot], offsets(index_h)[column]
        t, h = index_t + a, index_h + b
        kept = (mask_ref[index_t, index_h, 3 * (a + 1) + (b + 1)] == 1) & inside(t, counts[0]) & inside(h, counts[1])
        safe = jnp.clip(t, 0, counts[0] - 1)
        for f in range(2):
            live = jnp.where(kept, clip_ref[2 * safe + f], 0)
            limit = jnp.where(lane >= slot * rows + f * (rows // 2), live, limit)
    bias[...] = jnp.where(lax.rem(lane, width) < limit, 0.0, -jnp.inf)
    which = lax.broadcasted_iota(jnp.int32, (rows, HEAD_DIM), 1)

    def body(step, _):
        hs = [step * UNROLL + u for u in range(UNROLL)]
        tops_, accs, sums_ = [], [], []
        scored = []
        for h in hs:
            keys = jnp.concatenate([ref[0, :, head_columns(h)] for ref in slots], axis=0)
            s = dot_last(query_ref[:, head_columns(h)], keys) * (scale * LOG2E) + bias[...]
            scored.append(s)
            tops_.append(jnp.maximum(jnp.max(s, axis=1, keepdims=True), FLOOR))
        for u, h in enumerate(hs):
            e = jnp.exp2(scored[u] - tops_[u]).astype(jnp.bfloat16)
            exp_ref[h] = e
            values = jnp.concatenate([ref[1, :, head_columns(h)] for ref in slots], axis=0)
            both = dot(e, jnp.concatenate([values, jnp.ones_like(values)], axis=1))
            accs.append(both[:, :HEAD_DIM])
            sums_.append(both[:, HEAD_DIM:])
        for u, h in enumerate(hs):
            cols = head_columns(h)
            acc, total = accs[u], sums_[u]
            top = jnp.broadcast_to(tops_[u], (rows, HEAD_DIM))
            if not last:
                sum_ref[:, cols], top_ref[:, cols], total_ref[:, cols] = acc, top, total
                continue
            near_top, own_top = tops[1][:, cols], tops[0][:, cols]
            row_max = jnp.maximum(jnp.maximum(own_top, near_top), top)
            row_total = total * jnp.exp2(top - row_max) + totals[0][:, cols] * jnp.exp2(own_top - row_max)
            row_total = row_total + totals[1][:, cols] * jnp.exp2(near_top - row_max)
            log_total = row_max + jnp.log2(row_total)
            factors = [jnp.exp2(x - log_total) for x in (own_top, near_top, top)]
            for ref, factor in zip((fac_own, fac_near, fac_far), factors):
                ref[:, cols] = factor
            attention = sums[0][:, cols] * factors[0] + sums[1][:, cols] * factors[1] + acc * factors[2]
            att_ref[:, cols] = attention
            delta = jnp.sum(grad_ref[:, cols].astype(jnp.float32) * attention, axis=1, keepdims=True)
            delta = jnp.broadcast_to(delta, (rows, HEAD_DIM))
            delta_ref[:, cols] = delta
            marked = jnp.where(which == h, log_total, stat[...])
            stat[...] = jnp.where(which == h + ROW_DELTA, delta, marked)
        return 0

    if last:
        stat[...] = jnp.zeros_like(stat)
    lax.fori_loop(0, heads // UNROLL, body, 0)
    if last:
        pad = jnp.zeros((-rows % HEAD_DIM, HEAD_DIM), jnp.float32)
        turned = jnp.concatenate([stat[...], pad], axis=0).T
        stat_ref[...] = turned[:STAT_ROWS, :rows]


def conv_kernel(counts, width, flipped, own, near, pair, near_pair, other, near_other, weight_ref, out_ref):
    _, _, place_now = place(counts)
    rows, channels = out_ref.shape

    def body(head, _):
        cols = head_columns(head)
        tiles = [(x[1, :, cols], y[1, :, cols]) for x, y in ((own, near), (pair, near_pair), (other, near_other))]
        out_ref[:, cols] = conv_inner(tiles, weight_ref[:, cols].astype(jnp.float32), flipped, place_now, width)
        return 0

    lax.fori_loop(0, channels // HEAD_DIM, body, 0, unroll=3)


def query_kernel(grad_ref, *rest):
    slots, exps, factors = rest[:9], rest[9:12], rest[12:15]
    delta_ref, dq_ref, done_ref = rest[15:]
    done_ref[...] = jnp.zeros_like(done_ref)
    rows, channels = grad_ref.shape
    heads = channels // HEAD_DIM
    scale = HEAD_DIM**-0.5
    wide = -(-3 * rows // HEAD_DIM)

    def body(step, _):
        for u in range(UNROLL):
            h = step * UNROLL + u
            cols = head_columns(h)
            grad = grad_ref[:, cols]
            delta = jnp.concatenate([delta_ref[:, cols]] * wide, axis=1)[:, : 3 * rows]
            dq = None
            for column in range(3):
                refs = slots[column::3]
                values = jnp.concatenate([ref[1, :, cols] for ref in refs], axis=0)
                keys = jnp.concatenate([ref[0, :, cols] for ref in refs], axis=0)
                ds = exps[column][h].astype(jnp.float32) * (dot_last(grad, values) - delta)
                part = dot(ds.astype(jnp.bfloat16), keys) * (factors[column][:, cols] * scale)
                dq = part if dq is None else dq + part
            dq_ref[:, cols] = dq.astype(jnp.bfloat16)
        return 0

    lax.fori_loop(0, heads // UNROLL, body, 0)


def out_kernel(counts, width, att_ref, conv_ref, own, pair, other, weight_ref, _, out_ref):
    _, _, place_now = place(counts)

    def body(head, _):
        cols = head_columns(head)
        tiles = [ref[1, :, cols] for ref in (own, pair, other)]
        conv = conv_ref[:, cols] + conv_far(tiles, weight_ref[:, cols].astype(jnp.float32), False, place_now, width)
        out_ref[:, cols] = (att_ref[:, cols] + conv).astype(jnp.bfloat16)
        return 0

    lax.fori_loop(0, out_ref.shape[1] // HEAD_DIM, body, 0, unroll=3)


def pack_kernel(rows, qg_ref, own_ref, near_ref, far_ref, *rest):
    out_ref = rest[-1]
    out_ref[:rows] = qg_ref[0]
    out_ref[rows : 2 * rows] = qg_ref[1]
    first = 2 * rows
    out_ref[first:] = jnp.zeros(out_ref[first:].shape, jnp.bfloat16)
    for i, ref in enumerate((own_ref, near_ref, far_ref)):
        left = ref[...]
        for part in range(3):
            high = left.astype(jnp.bfloat16)
            out_ref[first + part * STAT_ROWS : first + (part + 1) * STAT_ROWS, i * STAT_LANES : i * STAT_LANES + rows] = high
            left = left - high.astype(jnp.float32)


def key_kernel(counts, width, slot_t, mask_ref, clip_ref, own, own_ref, near_ref, far_ref, *rest):
    first, last = slot_t == 0, slot_t == 2
    index_t, index_h, place_now = place(counts)
    rows, channels = own.shape[1:]
    heads = channels // HEAD_DIM
    scale = HEAD_DIM**-0.5

    def packed(ref, what, cols):
        return ref[what * rows : (what + 1) * rows, cols] if len(ref.shape) == 2 else ref[what, :, cols]

    if first:
        *stat_refs, dk_ref, dv_ref, stats = rest
        pieces = [ref[...] for ref in stat_refs]
    else:
        dk_sum, dv_sum, *edges, dk_ref, dv_ref, stats = rest
        pieces = []
        for i in range(3):
            parts = []
            for part in range(3):
                start = 2 * rows + part * STAT_ROWS
                parts.append(far_ref[start : start + STAT_ROWS, i * STAT_LANES : i * STAT_LANES + rows].astype(jnp.float32))
            pieces.append(parts[0] + (parts[1] + parts[2]))
    line = lax.broadcasted_iota(jnp.int32, (STAT_ROWS, rows), 0)
    for column in range(3):
        a, b = offsets(index_t)[slot_t], offsets(index_h)[column]
        t, h = index_t + a, index_h + b
        safe_t, safe_h = jnp.clip(t, 0, counts[0] - 1), jnp.clip(h, 0, counts[1] - 1)
        kept = (mask_ref[safe_t, safe_h, 3 * (1 - a) + (1 - b)] == 1) & inside(t, counts[0]) & inside(h, counts[1])
        pieces[column] = jnp.where(kept | (line >= ROW_DELTA), pieces[column], jnp.inf)
    stats[...] = jnp.concatenate(pieces, axis=1)
    row = lax.broadcasted_iota(jnp.int32, (rows, HEAD_DIM), 0)
    lens = [clip_ref[2 * index_t + f] for f in range(2)]
    live = lax.rem(row, width) < jnp.where(row < 2 * width, lens[0], lens[1])

    def body(step, _):
        for u in range(UNROLL):
            head = step * UNROLL + u
            cols = head_columns(head)
            queries = jnp.concatenate([packed(ref, 0, cols) for ref in (own_ref, near_ref, far_ref)], axis=0)
            grads = jnp.concatenate([packed(ref, 1, cols) for ref in (own_ref, near_ref, far_ref)], axis=0)
            s = dot_last(own[0, :, cols], queries)
            p = jnp.exp2(s * (scale * LOG2E) - stats[pl.ds(head, 1), :])
            dp = dot_last(own[1, :, cols], grads)
            ds = (p * (dp - stats[pl.ds(head + ROW_DELTA, 1), :])).astype(jnp.bfloat16)
            dv = dot(p.astype(jnp.bfloat16), grads)
            dk = dot(ds, queries)
            if not first:
                dk, dv = dk + dk_sum[:, cols], dv + dv_sum[:, cols]
            if not last:
                dk_ref[:, cols], dv_ref[:, cols] = dk, dv
                continue
            dk_ref[:, cols] = jnp.where(live, dk * scale, 0.0).astype(jnp.bfloat16)
            weight_ref, conv_ref, *far_refs = edges
            tiles = [packed(ref, 1, cols) for ref in (*far_refs, far_ref)]
            conv = conv_ref[:, cols] + conv_far(tiles, weight_ref[:, cols].astype(jnp.float32), True, place_now, width)
            dv_ref[:, cols] = (jnp.where(live, dv, 0.0) + conv).astype(jnp.bfloat16)
        return 0

    lax.fori_loop(0, heads // UNROLL, body, 0)


def cost(heads, rows, matmuls, columns):
    work = heads * rows * 3 * columns * rows * HEAD_DIM * 2 * matmuls
    moved = heads * rows * HEAD_DIM * 2 * 8 * columns
    return pl.CostEstimate(flops=work, bytes_accessed=moved, transcendentals=heads * rows * rows * 3 * columns)


def shards(query_states, key_states, value_states, conv_weight, out_grad, tile_mask, clip_lengths):
    width, channels = query_states.shape[2:]
    rows = query_states.shape[0] * query_states.shape[1] * width
    counts = (lax.axis_size("ta"), lax.axis_size("ha"))
    heads = channels // HEAD_DIM
    query, key, value, grad = [x.reshape(rows, channels) for x in (query_states, key_states, value_states, out_grad)]

    smem = pl.BlockSpec(memory_space=pltpu.SMEM)
    vmem = pl.BlockSpec(memory_space=pltpu.VMEM)
    params = pltpu.CompilerParams(vmem_limit_bytes=LARGE)
    half = jax.ShapeDtypeStruct((rows, channels), jnp.bfloat16)
    full = jax.ShapeDtypeStruct((rows, channels), jnp.float32)
    exps = jax.ShapeDtypeStruct((heads, rows, 3 * rows), jnp.bfloat16)
    bias = pltpu.VMEM((1, 3 * rows), jnp.float32)

    def call(kernel, name, out_shape, scratch, work, *args):
        scalars = 2 if args[0] is tile_mask else 0
        return pl.pallas_call(
            kernel,
            in_specs=[smem] * scalars + [vmem] * (len(args) - scalars),
            out_specs=[vmem] * len(out_shape),
            out_shape=out_shape,
            scratch_shapes=scratch,
            compiler_params=params,
            cost_estimate=work,
            name=name,
        )(*args)

    def convolution(flipped, *tiles):
        kernel = functools.partial(conv_kernel, counts, width, flipped)
        return call(kernel, "convolution", [full], [], cost(heads, rows, 1, 1), *tiles, conv_weight)[0]

    def scores(column, tiles):
        kernel = functools.partial(column_kernel, counts, width, column, False)
        work = cost(heads, rows, 2, 1)
        return call(kernel, f"scores_{column}", [exps, full, full, full], [bias], work, tile_mask, clip_lengths, query, *tiles)

    def later(x, *earlier):
        def kernel(x_ref, *rest):
            rest[-1][...] = x_ref[...]

        return pl.pallas_call(
            kernel,
            in_specs=[vmem] + [pl.BlockSpec(memory_space=pl.ANY)] * len(earlier),
            out_specs=vmem,
            out_shape=jax.ShapeDtypeStruct(x.shape, x.dtype),
            compiler_params=pltpu.CompilerParams(vmem_limit_bytes=SMALL),
            name="later",
        )(x, *earlier)

    def pair_up(x, y, *earlier):
        def kernel(x_ref, y_ref, *rest):
            rest[-1][0] = x_ref[...]
            rest[-1][1] = y_ref[...]

        return pl.pallas_call(
            kernel,
            in_specs=[vmem] * 2 + [pl.BlockSpec(memory_space=pl.ANY)] * len(earlier),
            out_specs=vmem,
            out_shape=jax.ShapeDtypeStruct((2,) + x.shape, x.dtype),
            compiler_params=pltpu.CompilerParams(vmem_limit_bytes=SMALL),
            name="pair_up",
        )(x, y, *earlier)

    def gate(x, *earlier):
        return pl.pallas_call(
            lambda *refs: None,
            in_specs=[pl.BlockSpec(memory_space=pl.ANY)] * (1 + len(earlier)),
            out_specs=pl.BlockSpec(memory_space=pl.ANY),
            out_shape=jax.ShapeDtypeStruct(x.shape, x.dtype),
            input_output_aliases={0: 0},
            compiler_params=pltpu.CompilerParams(vmem_limit_bytes=SMALL),
            name="gate",
        )(x, *earlier)

    near_k = ha_near(key)
    kv = jnp.stack([key, value])
    kv_a, kv_b = ta_pair(kv), ta_other(kv)
    qg = pair_up(query, grad, kv_a)
    qg_a, qg_b = ta_pair(qg), ta_other(qg)
    near_v = ha_near(later(value, near_k))
    far_k = ha_relay(near_k)
    exp_own, *own_parts = scores(0, (kv, kv_a, kv_b))

    far_v = ha_relay(near_v)
    near_kv = pair_up(near_k, near_v, qg_a, qg_b)
    near_kv_a, near_kv_b = ta_pair(near_kv), ta_other(near_kv)
    near_qg = ha_near(pair_up(query, grad, near_v, far_k))
    exp_near, *near_parts = scores(1, (near_kv, near_kv_a, near_kv_b))
    far_kv = pair_up(far_k, far_v, own_parts[0], near_parts[0])
    far_kv_a, far_kv_b = ta_pair(far_kv), ta_other(far_kv)

    conv_value = convolution(False, kv, near_kv, kv_a, near_kv_a, kv_b, near_kv_b)

    near_qg = gate(near_qg, near_parts[0])
    far_qg = ha_relay(near_qg)
    near_qg_a, near_qg_b = ta_pair(near_qg), ta_other(near_qg)
    exp_far, attention, fac_own, fac_near, fac_far, delta, stat = call(
        functools.partial(column_kernel, counts, width, 2, True),
        "scores_2",
        [exps] + [full] * 5 + [jax.ShapeDtypeStruct((STAT_ROWS, rows), jnp.float32)],
        [bias, pltpu.VMEM((rows, HEAD_DIM), jnp.float32)],
        cost(heads, rows, 2, 1),
        tile_mask, clip_lengths, query, far_kv, far_kv_a, far_kv_b, grad, *own_parts, *near_parts, conv_value,
    )
    near_stat, far_stat = ha_near(stat), ha_far(stat)
    query_grad, done = call(
        query_kernel,
        "query_side",
        [half, jax.ShapeDtypeStruct((8, HEAD_DIM), jnp.float32)],
        [],
        cost(heads, rows, 2, 3),
        grad, kv, near_kv, far_kv, kv_a, near_kv_a, far_kv_a, kv_b, near_kv_b, far_kv_b,
        exp_own, exp_near, exp_far, fac_own, fac_near, fac_far, delta,
    )
    message = pl.pallas_call(
        functools.partial(pack_kernel, rows),
        in_specs=[vmem] * 4 + [pl.BlockSpec(memory_space=pl.ANY)] * 3,
        out_specs=vmem,
        out_shape=jax.ShapeDtypeStruct((2 * rows + 3 * STAT_ROWS, channels), jnp.bfloat16),
        compiler_params=pltpu.CompilerParams(vmem_limit_bytes=SMALL),
        name="pack",
    )(far_qg, stat, near_stat, far_stat, done, near_qg_a, near_qg_b)
    message_a, message_b = ta_pair(message), ta_other(message)
    layer_out = call(
        functools.partial(out_kernel, counts, width), "layer_out", [half], [], cost(heads, rows, 1, 1),
        attention, conv_value, far_kv, far_kv_a, far_kv_b, conv_weight, message_a,
    )[0]

    conv_grad = convolution(True, qg, near_qg, qg_a, near_qg_a, qg_b, near_qg_b)
    scratch = [pltpu.VMEM((STAT_ROWS, 3 * rows), jnp.float32)]
    work = cost(heads, rows, 4, 1)
    sums = call(
        functools.partial(key_kernel, counts, width, 0), "key_side_0", [full, full], scratch, work,
        tile_mask, clip_lengths, kv, qg, near_qg, far_qg, stat, near_stat, far_stat,
    )
    sums = call(
        functools.partial(key_kernel, counts, width, 1), "key_side_1", [full, full], scratch, work,
        tile_mask, clip_lengths, kv, qg_a, near_qg_a, message_a, *sums,
    )
    key_grad, value_grad = call(
        functools.partial(key_kernel, counts, width, 2), "key_side_2", [half, half], scratch, work,
        tile_mask, clip_lengths, kv, qg_b, near_qg_b, message_b, *sums,
        conv_weight, conv_grad, far_qg, message_a,
    )
    return tuple(x.reshape(query_states.shape) for x in (layer_out, query_grad, key_grad, value_grad))


def solution(mesh):
    placed = P("ta", "ha", None, None)
    return jax.shard_map(
        shards,
        mesh=mesh,
        in_specs=(placed, placed, placed, P(), placed, P(), P()),
        out_specs=(placed,) * 4,
        check_vma=False,
    )
```

```python
import functools

import jax
import jax.numpy as jnp
from jax import lax
from jax.experimental import pallas as pl
from jax.experimental.pallas import tpu as pltpu
from jax.sharding import PartitionSpec as P

HEAD_DIM = 128
LOG2E = 1.4426950408889634
ROW_DELTA = 8
STAT_ROWS = 16
STAT_LANES = 256
UNROLL = 6
FLOOR = -1e30
SMALL = 2 * 1024 * 1024
LARGE = 8 * 1024 * 1024


CONTRACT_LAST = (((1,), (1,)), ((), ()))


def flip_pairs(count):
    return [(i, i ^ 1) for i in range(count)]


def other_pairs(count):
    pairs = []
    for i in range(count):
        to = i + 1 if i % 2 else i - 1
        pairs.append((i, to if 0 <= to < count else i))
    return pairs


def relay_pairs(count):
    pairs = []
    for i in range(count):
        to = i - 2 if i % 2 else i + 2
        if 0 <= to < count:
            pairs.append((i, to))
    return pairs


def ha_near(x):
    return lax.ppermute(x, "ha", flip_pairs(lax.axis_size("ha")))


def ha_relay(near):
    return lax.ppermute(near, "ha", relay_pairs(lax.axis_size("ha")))


def ha_far(x):
    return lax.ppermute(x, "ha", other_pairs(lax.axis_size("ha")))


def ta_pair(x):
    return lax.ppermute(x, "ta", flip_pairs(lax.axis_size("ta")))


def ta_other(x):
    return lax.ppermute(x, "ta", other_pairs(lax.axis_size("ta")))


def offsets(index):
    sign = 1 - 2 * lax.rem(index, 2)
    return (0, sign, -sign)


def inside(index, count):
    return (index >= 0) & (index < count)


def row_of(tile, frame, row, width):
    start = (2 * frame + row) * width
    return tile[start : start + width]


def shifted_sum(parts, width):
    column = lax.broadcasted_iota(jnp.int32, (width, HEAD_DIM), 0)
    before = jnp.where(column == 0, 0.0, pltpu.roll(parts[0], 1, 0))
    behind = jnp.where(column == width - 1, 0.0, pltpu.roll(parts[2], width - 1, 0))
    return parts[1] + before + behind


def total_of(terms):
    return functools.reduce(lambda x, y: x + y, terms)


def along_t(own, pair, other, place_now):
    even_t, _, in_t, _ = place_now
    ahead = jnp.where(in_t[0], jnp.where(even_t, other(1), pair(1)), 0.0)
    behind = jnp.where(in_t[1], jnp.where(even_t, pair(0), other(0)), 0.0)
    return [ahead, own(0), own(1), behind]


def conv_inner(tiles, weight, flipped, place_now, width):
    _, even_h, _, in_h = place_now
    tiles = [[x.astype(jnp.float32) for x in pair] for pair in tiles]

    def cell(slot, R):
        if R in (1, 2):
            return lambda frame: row_of(tiles[slot][0], frame, R - 1, width)
        if R == 0:
            return lambda frame: jnp.where(even_h | ~in_h[0], 0.0, row_of(tiles[slot][1], frame, 1, width))
        return lambda frame: jnp.where(even_h & in_h[1], row_of(tiles[slot][1], frame, 0, width), 0.0)

    lines = range(4) if len(tiles[0]) == 2 else (1, 2)
    slab = {R: along_t(cell(0, R), cell(1, R), cell(2, R), place_now) for R in lines}
    rows = []
    for f in range(2):
        for r in range(2):
            parts = []
            for dw in range(3):
                taps = [(dt, dh, 9 * dt + 3 * dh + dw) for dt in range(3) for dh in range(3) if r + dh in slab]
                taps = [(dt, dh, 26 - tap if flipped else tap) for dt, dh, tap in taps]
                parts.append(total_of([weight[tap : tap + 1] * slab[r + dh][f + dt] for dt, dh, tap in taps]))
            rows.append(shifted_sum(parts, width))
    return jnp.concatenate(rows, axis=0)


def conv_beside(tiles, weight, flipped, place_now, width, far):
    _, even_h, _, in_h = place_now
    above = even_h if far else ~even_h
    tiles = [x.astype(jnp.float32) for x in tiles]
    there = (above & in_h[0]) | (~above & in_h[1])

    def cell(slot):
        def of(frame):
            row = jnp.where(above, row_of(tiles[slot], frame, 1, width), row_of(tiles[slot], frame, 0, width))
            return jnp.where(there, row, 0.0)

        return of

    line = along_t(cell(0), cell(1), cell(2), place_now)
    rows = []
    for f in range(2):
        parts = []
        for dw in range(3):
            terms = []
            for dt in range(3):
                up, down = 9 * dt + dw, 9 * dt + 6 + dw
                if flipped:
                    up, down = 26 - up, 26 - down
                tap = jnp.where(above, weight[up : up + 1], weight[down : down + 1])
                terms.append(tap * line[f + dt])
            parts.append(total_of(terms))
        beside = shifted_sum(parts, width)
        rows += [jnp.where(above, beside, 0.0), jnp.where(above, 0.0, beside)]
    return jnp.concatenate(rows, axis=0)


def place(counts):
    index_t, index_h = lax.axis_index("ta"), lax.axis_index("ha")
    even_t, even_h = lax.rem(index_t, 2) == 0, lax.rem(index_h, 2) == 0
    in_t = (index_t > 0, index_t < counts[0] - 1)
    in_h = (index_h > 0, index_h < counts[1] - 1)
    return index_t, index_h, (even_t, even_h, in_t, in_h)


def head_columns(head):
    return pl.ds(pl.multiple_of(head * HEAD_DIM, HEAD_DIM), HEAD_DIM)


def dot_last(x, y):
    return lax.dot_general(x, y, CONTRACT_LAST, preferred_element_type=jnp.float32)


def dot(x, y):
    return jnp.dot(x, y, preferred_element_type=jnp.float32)


def column_kernel(counts, width, column, last, mask_ref, clip_ref, query_ref, own, pair, other, *rest):
    slots = [own, pair, other]
    if last:
        grad_ref, sums, tops, totals = rest[0], (rest[1], rest[4]), (rest[2], rest[5]), (rest[3], rest[6])
        exp_ref, att_ref, fac_own, fac_near, fac_far, delta_ref, stat_ref, bias, stat = rest[8:]
    else:
        exp_ref, sum_ref, top_ref, total_ref, bias = rest
    index_t, index_h, _ = place(counts)
    rows, channels = query_ref.shape
    heads = channels // HEAD_DIM
    scale = HEAD_DIM**-0.5
    lane = lax.broadcasted_iota(jnp.int32, (1, 3 * rows), 1)
    limit = jnp.zeros((1, 3 * rows), jnp.int32)
    for slot in range(3):
        a, b = offsets(index_t)[slot], offsets(index_h)[column]
        t, h = index_t + a, index_h + b
        kept = (mask_ref[index_t, index_h, 3 * (a + 1) + (b + 1)] == 1) & inside(t, counts[0]) & inside(h, counts[1])
        safe = jnp.clip(t, 0, counts[0] - 1)
        for f in range(2):
            live = jnp.where(kept, clip_ref[2 * safe + f], 0)
            limit = jnp.where(lane >= slot * rows + f * (rows // 2), live, limit)
    bias[...] = jnp.where(lax.rem(lane, width) < limit, 0.0, -jnp.inf)
    which = lax.broadcasted_iota(jnp.int32, (rows, HEAD_DIM), 1)

    def body(step, _):
        hs = [step * UNROLL + u for u in range(UNROLL)]
        tops_, accs, sums_ = [], [], []
        scored = []
        for h in hs:
            keys = jnp.concatenate([ref[0, :, head_columns(h)] for ref in slots], axis=0)
            s = dot_last(query_ref[:, head_columns(h)], keys) * (scale * LOG2E) + bias[...]
            scored.append(s)
            tops_.append(jnp.maximum(jnp.max(s, axis=1, keepdims=True), FLOOR))
        for u, h in enumerate(hs):
            e = jnp.exp2(scored[u] - tops_[u]).astype(jnp.bfloat16)
            exp_ref[h] = e
            values = jnp.concatenate([ref[1, :, head_columns(h)] for ref in slots], axis=0)
            both = dot(e, jnp.concatenate([values, jnp.ones_like(values)], axis=1))
            accs.append(both[:, :HEAD_DIM])
            sums_.append(both[:, HEAD_DIM:])
        for u, h in enumerate(hs):
            cols = head_columns(h)
            acc, total = accs[u], sums_[u]
            top = jnp.broadcast_to(tops_[u], (rows, HEAD_DIM))
            if not last:
                sum_ref[:, cols], top_ref[:, cols], total_ref[:, cols] = acc, top, total
                continue
            near_top, own_top = tops[1][:, cols], tops[0][:, cols]
            row_max = jnp.maximum(jnp.maximum(own_top, near_top), top)
            row_total = total * jnp.exp2(top - row_max) + totals[0][:, cols] * jnp.exp2(own_top - row_max)
            row_total = row_total + totals[1][:, cols] * jnp.exp2(near_top - row_max)
            log_total = row_max + jnp.log2(row_total)
            factors = [jnp.exp2(x - log_total) for x in (own_top, near_top, top)]
            for ref, factor in zip((fac_own, fac_near, fac_far), factors):
                ref[:, cols] = factor
            attention = sums[0][:, cols] * factors[0] + sums[1][:, cols] * factors[1] + acc * factors[2]
            att_ref[:, cols] = attention
            delta = jnp.sum(grad_ref[:, cols].astype(jnp.float32) * attention, axis=1, keepdims=True)
            delta = jnp.broadcast_to(delta, (rows, HEAD_DIM))
            delta_ref[:, cols] = delta
            marked = jnp.where(which == h, log_total, stat[...])
            stat[...] = jnp.where(which == h + ROW_DELTA, delta, marked)
        return 0

    if last:
        stat[...] = jnp.zeros_like(stat)
    lax.fori_loop(0, heads // UNROLL, body, 0)
    if last:
        pad = jnp.zeros((-rows % HEAD_DIM, HEAD_DIM), jnp.float32)
        turned = jnp.concatenate([stat[...], pad], axis=0).T
        stat_ref[...] = turned[:STAT_ROWS, :rows]


def conv_kernel(counts, width, flipped, columns, *refs):
    *tile_refs, weight_ref, out_ref = refs
    _, _, place_now = place(counts)
    rows, channels = out_ref.shape

    def body(head, _):
        cols = head_columns(head)
        tiles = [[ref[1, :, cols] for ref in tile_refs[columns * i : columns * (i + 1)]] for i in range(3)]
        out_ref[:, cols] = conv_inner(tiles, weight_ref[:, cols].astype(jnp.float32), flipped, place_now, width)
        return 0

    lax.fori_loop(0, channels // HEAD_DIM, body, 0, unroll=3)


def query_kernel(grad_ref, *rest):
    slots, exps, factors = rest[:9], rest[9:12], rest[12:15]
    delta_ref, dq_ref, done_ref = rest[15:]
    done_ref[...] = jnp.zeros_like(done_ref)
    rows, channels = grad_ref.shape
    heads = channels // HEAD_DIM
    scale = HEAD_DIM**-0.5
    wide = -(-3 * rows // HEAD_DIM)

    def body(step, _):
        for u in range(UNROLL):
            h = step * UNROLL + u
            cols = head_columns(h)
            grad = grad_ref[:, cols]
            delta = jnp.concatenate([delta_ref[:, cols]] * wide, axis=1)[:, : 3 * rows]
            dq = None
            for column in range(3):
                refs = slots[column::3]
                values = jnp.concatenate([ref[1, :, cols] for ref in refs], axis=0)
                keys = jnp.concatenate([ref[0, :, cols] for ref in refs], axis=0)
                ds = exps[column][h].astype(jnp.float32) * (dot_last(grad, values) - delta)
                part = dot(ds.astype(jnp.bfloat16), keys) * (factors[column][:, cols] * scale)
                dq = part if dq is None else dq + part
            dq_ref[:, cols] = dq.astype(jnp.bfloat16)
        return 0

    lax.fori_loop(0, heads // UNROLL, body, 0)


def out_kernel(counts, width, att_ref, conv_ref, own, pair, other, weight_ref, _, out_ref):
    _, _, place_now = place(counts)

    def body(head, _):
        cols = head_columns(head)
        tiles = [ref[1, :, cols] for ref in (own, pair, other)]
        conv = conv_ref[:, cols] + conv_beside(tiles, weight_ref[:, cols].astype(jnp.float32), False, place_now, width, True)
        out_ref[:, cols] = (att_ref[:, cols] + conv).astype(jnp.bfloat16)
        return 0

    lax.fori_loop(0, out_ref.shape[1] // HEAD_DIM, body, 0, unroll=3)


def pack_kernel(rows, qg_ref, own_ref, near_ref, far_ref, *rest):
    out_ref = rest[-1]
    out_ref[:rows] = qg_ref[0]
    out_ref[rows : 2 * rows] = qg_ref[1]
    first = 2 * rows
    out_ref[first:] = jnp.zeros(out_ref[first:].shape, jnp.bfloat16)
    for i, ref in enumerate((own_ref, near_ref, far_ref)):
        left = ref[...]
        for part in range(3):
            high = left.astype(jnp.bfloat16)
            out_ref[first + part * STAT_ROWS : first + (part + 1) * STAT_ROWS, i * STAT_LANES : i * STAT_LANES + rows] = high
            left = left - high.astype(jnp.float32)


def key_kernel(counts, width, slot_t, mask_ref, clip_ref, own, own_ref, near_ref, far_ref, *rest):
    first, last = slot_t == 0, slot_t == 2
    index_t, index_h, place_now = place(counts)
    rows, channels = own.shape[1:]
    heads = channels // HEAD_DIM
    scale = HEAD_DIM**-0.5

    def packed(ref, what, cols):
        return ref[what * rows : (what + 1) * rows, cols] if len(ref.shape) == 2 else ref[what, :, cols]

    if first:
        *stat_refs, dk_ref, dv_ref, stats = rest
        pieces = [ref[...] for ref in stat_refs]
    else:
        dk_sum, dv_sum, *edges, dk_ref, dv_ref, stats = rest
        pieces = []
        for i in range(3):
            parts = []
            for part in range(3):
                start = 2 * rows + part * STAT_ROWS
                parts.append(far_ref[start : start + STAT_ROWS, i * STAT_LANES : i * STAT_LANES + rows].astype(jnp.float32))
            pieces.append(parts[0] + (parts[1] + parts[2]))
    line = lax.broadcasted_iota(jnp.int32, (STAT_ROWS, rows), 0)
    for column in range(3):
        a, b = offsets(index_t)[slot_t], offsets(index_h)[column]
        t, h = index_t + a, index_h + b
        safe_t, safe_h = jnp.clip(t, 0, counts[0] - 1), jnp.clip(h, 0, counts[1] - 1)
        kept = (mask_ref[safe_t, safe_h, 3 * (1 - a) + (1 - b)] == 1) & inside(t, counts[0]) & inside(h, counts[1])
        pieces[column] = jnp.where(kept | (line >= ROW_DELTA), pieces[column], jnp.inf)
    stats[...] = jnp.concatenate(pieces, axis=1)
    row = lax.broadcasted_iota(jnp.int32, (rows, HEAD_DIM), 0)
    lens = [clip_ref[2 * index_t + f] for f in range(2)]
    live = lax.rem(row, width) < jnp.where(row < 2 * width, lens[0], lens[1])

    def body(step, _):
        for u in range(UNROLL):
            head = step * UNROLL + u
            cols = head_columns(head)
            queries = jnp.concatenate([packed(ref, 0, cols) for ref in (own_ref, near_ref, far_ref)], axis=0)
            grads = jnp.concatenate([packed(ref, 1, cols) for ref in (own_ref, near_ref, far_ref)], axis=0)
            s = dot_last(own[0, :, cols], queries)
            p = jnp.exp2(s * (scale * LOG2E) - stats[pl.ds(head, 1), :])
            dp = dot_last(own[1, :, cols], grads)
            ds = (p * (dp - stats[pl.ds(head + ROW_DELTA, 1), :])).astype(jnp.bfloat16)
            dv = dot(p.astype(jnp.bfloat16), grads)
            dk = dot(ds, queries)
            if not first:
                dk, dv = dk + dk_sum[:, cols], dv + dv_sum[:, cols]
            if not last:
                dk_ref[:, cols], dv_ref[:, cols] = dk, dv
                continue
            dk_ref[:, cols] = jnp.where(live, dk * scale, 0.0).astype(jnp.bfloat16)
            weight_ref, conv_ref, *sides = edges
            weight = weight_ref[:, cols].astype(jnp.float32)
            conv = conv_ref[:, cols]
            for far, refs in ((True, (*sides[:2], far_ref)), (False, (*sides[2:], near_ref))):
                conv = conv + conv_beside([packed(ref, 1, cols) for ref in refs], weight, True, place_now, width, far)
            dv_ref[:, cols] = (jnp.where(live, dv, 0.0) + conv).astype(jnp.bfloat16)
        return 0

    lax.fori_loop(0, heads // UNROLL, body, 0)


def cost(heads, rows, matmuls, columns):
    work = heads * rows * 3 * columns * rows * HEAD_DIM * 2 * matmuls
    moved = heads * rows * HEAD_DIM * 2 * 8 * columns
    return pl.CostEstimate(flops=work, bytes_accessed=moved, transcendentals=heads * rows * rows * 3 * columns)


def shards(query_states, key_states, value_states, conv_weight, out_grad, tile_mask, clip_lengths):
    width, channels = query_states.shape[2:]
    rows = query_states.shape[0] * query_states.shape[1] * width
    counts = (lax.axis_size("ta"), lax.axis_size("ha"))
    heads = channels // HEAD_DIM
    query, key, value, grad = [x.reshape(rows, channels) for x in (query_states, key_states, value_states, out_grad)]

    smem = pl.BlockSpec(memory_space=pltpu.SMEM)
    vmem = pl.BlockSpec(memory_space=pltpu.VMEM)
    params = pltpu.CompilerParams(vmem_limit_bytes=LARGE)
    half = jax.ShapeDtypeStruct((rows, channels), jnp.bfloat16)
    full = jax.ShapeDtypeStruct((rows, channels), jnp.float32)
    exps = jax.ShapeDtypeStruct((heads, rows, 3 * rows), jnp.bfloat16)
    bias = pltpu.VMEM((1, 3 * rows), jnp.float32)

    def call(kernel, name, out_shape, scratch, work, *args):
        scalars = 2 if args[0] is tile_mask else 0
        return pl.pallas_call(
            kernel,
            in_specs=[smem] * scalars + [vmem] * (len(args) - scalars),
            out_specs=[vmem] * len(out_shape),
            out_shape=out_shape,
            scratch_shapes=scratch,
            compiler_params=params,
            cost_estimate=work,
            name=name,
        )(*args)

    def convolution(flipped, *tiles):
        kernel = functools.partial(conv_kernel, counts, width, flipped, len(tiles) // 3)
        return call(kernel, "convolution", [full], [], cost(heads, rows, 1, 1), *tiles, conv_weight)[0]

    def scores(column, tiles):
        kernel = functools.partial(column_kernel, counts, width, column, False)
        work = cost(heads, rows, 2, 1)
        return call(kernel, f"scores_{column}", [exps, full, full, full], [bias], work, tile_mask, clip_lengths, query, *tiles)

    def later(x, *earlier):
        def kernel(x_ref, *rest):
            rest[-1][...] = x_ref[...]

        return pl.pallas_call(
            kernel,
            in_specs=[vmem] + [pl.BlockSpec(memory_space=pl.ANY)] * len(earlier),
            out_specs=vmem,
            out_shape=jax.ShapeDtypeStruct(x.shape, x.dtype),
            compiler_params=pltpu.CompilerParams(vmem_limit_bytes=SMALL),
            name="later",
        )(x, *earlier)

    def pair_up(x, y, *earlier):
        def kernel(x_ref, y_ref, *rest):
            rest[-1][0] = x_ref[...]
            rest[-1][1] = y_ref[...]

        return pl.pallas_call(
            kernel,
            in_specs=[vmem] * 2 + [pl.BlockSpec(memory_space=pl.ANY)] * len(earlier),
            out_specs=vmem,
            out_shape=jax.ShapeDtypeStruct((2,) + x.shape, x.dtype),
            compiler_params=pltpu.CompilerParams(vmem_limit_bytes=SMALL),
            name="pair_up",
        )(x, y, *earlier)

    def gate(x, *earlier):
        return pl.pallas_call(
            lambda *refs: None,
            in_specs=[pl.BlockSpec(memory_space=pl.ANY)] * (1 + len(earlier)),
            out_specs=pl.BlockSpec(memory_space=pl.ANY),
            out_shape=jax.ShapeDtypeStruct(x.shape, x.dtype),
            input_output_aliases={0: 0},
            compiler_params=pltpu.CompilerParams(vmem_limit_bytes=SMALL),
            name="gate",
        )(x, *earlier)

    near_k = ha_near(key)
    kv = jnp.stack([key, value])
    kv_a, kv_b = ta_pair(kv), ta_other(kv)
    qg = pair_up(query, grad, kv_a)
    qg_a, qg_b = ta_pair(qg), ta_other(qg)
    near_v = ha_near(later(value, near_k))
    far_k = ha_relay(near_k)
    exp_own, *own_parts = scores(0, (kv, kv_a, kv_b))

    far_v = ha_relay(near_v)
    near_kv = pair_up(near_k, near_v, qg_a, qg_b)
    near_kv_a, near_kv_b = ta_pair(near_kv), ta_other(near_kv)
    near_qg = ha_near(pair_up(query, grad, near_v, far_k))
    conv_grad = convolution(True, qg, qg_a, qg_b)
    exp_near, *near_parts = scores(1, (near_kv, near_kv_a, near_kv_b))
    far_kv = pair_up(far_k, far_v, own_parts[0], near_parts[0], conv_grad)
    far_kv_a, far_kv_b = ta_pair(far_kv), ta_other(far_kv)

    conv_value = convolution(False, kv, near_kv, kv_a, near_kv_a, kv_b, near_kv_b)

    near_qg = gate(near_qg, near_parts[0])
    far_qg = ha_relay(near_qg)
    near_qg_a, near_qg_b = ta_pair(near_qg), ta_other(near_qg)
    exp_far, attention, fac_own, fac_near, fac_far, delta, stat = call(
        functools.partial(column_kernel, counts, width, 2, True),
        "scores_2",
        [exps] + [full] * 5 + [jax.ShapeDtypeStruct((STAT_ROWS, rows), jnp.float32)],
        [bias, pltpu.VMEM((rows, HEAD_DIM), jnp.float32)],
        cost(heads, rows, 2, 1),
        tile_mask, clip_lengths, query, far_kv, far_kv_a, far_kv_b, grad, *own_parts, *near_parts, conv_value,
    )
    near_stat, far_stat = ha_near(stat), ha_far(stat)
    query_grad, done = call(
        query_kernel,
        "query_side",
        [half, jax.ShapeDtypeStruct((8, HEAD_DIM), jnp.float32)],
        [],
        cost(heads, rows, 2, 3),
        grad, kv, near_kv, far_kv, kv_a, near_kv_a, far_kv_a, kv_b, near_kv_b, far_kv_b,
        exp_own, exp_near, exp_far, fac_own, fac_near, fac_far, delta,
    )
    message = pl.pallas_call(
        functools.partial(pack_kernel, rows),
        in_specs=[vmem] * 4 + [pl.BlockSpec(memory_space=pl.ANY)] * 3,
        out_specs=vmem,
        out_shape=jax.ShapeDtypeStruct((2 * rows + 3 * STAT_ROWS, channels), jnp.bfloat16),
        compiler_params=pltpu.CompilerParams(vmem_limit_bytes=SMALL),
        name="pack",
    )(far_qg, stat, near_stat, far_stat, done, near_qg_a, near_qg_b)
    message_a, message_b = ta_pair(message), ta_other(message)
    layer_out = call(
        functools.partial(out_kernel, counts, width), "layer_out", [half], [], cost(heads, rows, 1, 1),
        attention, conv_value, far_kv, far_kv_a, far_kv_b, conv_weight, message_a,
    )[0]

    scratch = [pltpu.VMEM((STAT_ROWS, 3 * rows), jnp.float32)]
    work = cost(heads, rows, 4, 1)
    sums = call(
        functools.partial(key_kernel, counts, width, 0), "key_side_0", [full, full], scratch, work,
        tile_mask, clip_lengths, kv, qg, near_qg, far_qg, stat, near_stat, far_stat,
    )
    sums = call(
        functools.partial(key_kernel, counts, width, 1), "key_side_1", [full, full], scratch, work,
        tile_mask, clip_lengths, kv, qg_a, near_qg_a, message_a, *sums,
    )
    key_grad, value_grad = call(
        functools.partial(key_kernel, counts, width, 2), "key_side_2", [half, half], scratch, work,
        tile_mask, clip_lengths, kv, qg_b, near_qg_b, message_b, *sums,
        conv_weight, conv_grad, far_qg, message_a, near_qg, near_qg_a,
    )
    return tuple(x.reshape(query_states.shape) for x in (layer_out, query_grad, key_grad, value_grad))


def solution(mesh):
    placed = P("ta", "ha", None, None)
    return jax.shard_map(
        shards,
        mesh=mesh,
        in_specs=(placed, placed, placed, P(), placed, P(), P()),
        out_specs=(placed,) * 4,
        check_vma=False,
    )
```
